32 devices in a mesh: groups: 2 (over y), coord: 8 (over z, x), ckpt: 2 (over core).
Axes of the slice: x: 2, y: 2, z: 4, core: 2. Of those that a mesh axis runs over, the one named last changes fastest.
Arguments:
- projection_input: bfloat16 [2, 2, 384, 4096], P('ckpt', 'groups', None, 'coord'), parts along dimension 1, may hold values from -6 to 6
- gate_output_gradient: bfloat16 [2, 2, 14336, 384], P('ckpt', 'groups', 'coord'), parts along dimension 1, may hold values from -0.59765625 to 0.59765625
- up_output_gradient: bfloat16 [2, 2, 14336, 384], P('ckpt', 'groups', 'coord'), parts along dimension 1, may hold values from -0.59765625 to 0.59765625
- hidden: bfloat16 [2, 2, 14336, 384], P('ckpt', 'groups', 'coord'), parts along dimension 1, may hold values from -6 to 6
- down_output_gradient: bfloat16 [2, 2, 384, 4096], P('ckpt', 'groups', None, 'coord'), parts along dimension 1, may hold values from -0.59765625 to 0.59765625
- gate_adapter_first: bfloat16 [2, 4096, 128], P('ckpt', 'coord'), may hold values from -0.09375 to 0.09375
- gate_adapter_second: bfloat16 [2, 14336, 128], P('ckpt', 'coord'), may hold values from -0.5 to 0.5
- up_adapter_first: bfloat16 [2, 4096, 128], P('ckpt', 'coord'), may hold values from -0.09375 to 0.09375
- up_adapter_second: bfloat16 [2, 14336, 128], P('ckpt', 'coord'), may hold values from -0.5 to 0.5
- down_adapter_first: bfloat16 [2, 14336, 128], P('ckpt', 'coord'), may hold values from -0.046875 to 0.046875
- down_adapter_second: bfloat16 [2, 4096, 128], P('ckpt', 'coord'), may hold values from -0.5 to 0.5
- random_sign_flags: int32 [16777216], P(('coord', 'ckpt')), may hold values 0 or 1
- sampled_coordinate_index: int32 [8192], replicated, may hold values from 0 to 16777215
Outputs:
- features: float32 [2, 8192], P('groups'), parts along dimension 0
The draws below stay inside these ranges and needn't reach their ends.
There are 2 independent parts, one for each index of `groups`. The reference program is written for one: setup_inputs(seed, part) draws one part's arguments, and reference() takes and returns one part's arrays. A program takes and returns all parts, laid end to end along the dimension named above; an argument that names none is the same for every part. Nothing has to cross between parts.
All inputs are finite; a program needn't handle non-finite values. No bound on the sum of `random_sign_flags` on one device may be relied on, other than what follows from the above.
Results may differ from the reference program's by a relative error of at most 0.0031.
Values may be sent and summed in bfloat16 or wider, within the bound.
No kernel may reach another device: no remote copies, remote signals or barrier semaphores. Data moves between devices by JAX's collectives and lax.ppermute only.
A program may use at most 64 MiB of HBM per device.

```python
import jax
import jax.numpy as jnp

MODEL_WIDTH = 4096
HIDDEN_UNITS = 14336
ADAPTER_RANK = 128
HAD = 16777216
K = 8192
SEQ = 384
EX = 1
LOC = 1048576
N_COORD = 8


def place_ends(entries, rng, least, largest):
    place = [jax.random.randint(jax.random.fold_in(rng, axis), (), 0, length) for axis, length in enumerate(entries.shape)]
    widest = entries.shape.index(max(entries.shape))
    next_to = place[:widest] + [(place[widest] + 1) % entries.shape[widest]] + place[widest + 1:]
    return entries.at[tuple(place)].set(least).at[tuple(next_to)].set(largest)


def levels(key, shape, cuts, smallest, top_value):
    level, own = 1.0, jax.random.fold_in(key, 6)
    for position, shards_of in cuts:
        heights = jnp.exp(jax.random.uniform(jax.random.fold_in(own, position), (shards_of,), jnp.float32, smallest / len(cuts), top_value / len(cuts)))
        level = level * jnp.repeat(heights, shape[position] // shards_of).reshape([-1 if axis == position else 1 for axis in range(len(shape))])
    return level


def scatter_about(own_key, shape, spread, reach, cuts=(), dtype=jnp.bfloat16):
    gain = levels(own_key, shape, cuts, -0.22, 0.18) if cuts else 1.0
    entries = jax.random.normal(own_key, shape, jnp.float32) * spread * gain
    return jnp.minimum(jnp.maximum(entries, -reach), reach).astype(dtype)


def setup_inputs(seed: int = 0, part: int = 0) -> dict:
    splits = jax.random.split(jax.random.key(seed), 14)
    own_keys = jax.random.split(jax.random.fold_in(splits[13], part), 14)
    projection_input = scatter_about(own_keys[0], (2, EX, SEQ, MODEL_WIDTH), 1.0, 6.0, ((0, 2), (3, 8)))
    gate_output_gradient = scatter_about(own_keys[1], (2, EX, HIDDEN_UNITS, SEQ), 0.1, 0.59765625, ((0, 2), (2, 8)))
    up_output_gradient = scatter_about(own_keys[2], (2, EX, HIDDEN_UNITS, SEQ), 0.1, 0.59765625, ((0, 2), (2, 8)))
    hidden = scatter_about(own_keys[3], (2, EX, HIDDEN_UNITS, SEQ), 1.0, 6.0, ((0, 2), (2, 8)))
    down_output_gradient = scatter_about(own_keys[4], (2, EX, SEQ, MODEL_WIDTH), 0.1, 0.59765625, ((0, 2), (3, 8)))
    gate_adapter_first = scatter_about(splits[5], (2, MODEL_WIDTH, ADAPTER_RANK), MODEL_WIDTH ** -0.5, 0.09375, ((0, 2), (1, 8)))
    gate_adapter_second = scatter_about(splits[6], (2, HIDDEN_UNITS, ADAPTER_RANK), ADAPTER_RANK ** -0.5, 0.5, ((0, 2), (1, 8)))
    up_adapter_first = scatter_about(splits[7], (2, MODEL_WIDTH, ADAPTER_RANK), MODEL_WIDTH ** -0.5, 0.09375, ((0, 2), (1, 8)))
    up_adapter_second = scatter_about(splits[8], (2, HIDDEN_UNITS, ADAPTER_RANK), ADAPTER_RANK ** -0.5, 0.5, ((0, 2), (1, 8)))
    down_adapter_first = scatter_about(splits[9], (2, HIDDEN_UNITS, ADAPTER_RANK), HIDDEN_UNITS ** -0.5, 0.046875, ((0, 2), (1, 8)))
    down_adapter_second = scatter_about(splits[10], (2, MODEL_WIDTH, ADAPTER_RANK), ADAPTER_RANK ** -0.5, 0.5, ((0, 2), (1, 8)))
    random_sign_flags = place_ends((jax.random.randint(splits[11], (HAD,), 0, 2) < 1).astype(jnp.int32), jax.random.fold_in(splits[11], 1), 0, 1)
    sampled_coordinate_index = place_ends(jax.random.randint(splits[12], (K,), 0, HAD), jax.random.fold_in(splits[12], 1), 0, HAD - 1).astype(jnp.int32)
    return dict(projection_input=projection_input, gate_output_gradient=gate_output_gradient, up_output_gradient=up_output_gradient, hidden=hidden, down_output_gradient=down_output_gradient, gate_adapter_first=gate_adapter_first, gate_adapter_second=gate_adapter_second, up_adapter_first=up_adapter_first, up_adapter_second=up_adapter_second, down_adapter_first=down_adapter_first, down_adapter_second=down_adapter_second, random_sign_flags=random_sign_flags, sampled_coordinate_index=sampled_coordinate_index)


adapter_scale = 2.0


def cast_to_single_float(array):
    return array.astype(jnp.float32)


def cast_to_brain_float(array):
    return array.astype(jnp.bfloat16)


def walsh_full(vector):
    length = vector.shape[0]
    stride = 1
    while stride < length:
        pieces = vector.reshape(length // (2 * stride), 2, stride)
        vector = jnp.stack([pieces[:, 0] + pieces[:, 1], pieces[:, 0] - pieces[:, 1]], axis=1).reshape(length)
        stride = stride * 2
    return vector


def blocks(matrix):
    return matrix.reshape(matrix.shape[0], N_COORD, matrix.shape[1] // N_COORD, matrix.shape[2])


def reference(projection_input, gate_output_gradient, up_output_gradient, hidden, down_output_gradient, gate_adapter_first, gate_adapter_second, up_adapter_first, up_adapter_second, down_adapter_first, down_adapter_second, random_sign_flags, sampled_coordinate_index):
    columns = []
    for ensemble_member in range(2):
        input_tensors = cast_to_single_float(projection_input[ensemble_member])
        gate_cotangent_value = cast_to_single_float(gate_output_gradient[ensemble_member])
        up_cotangent_value = cast_to_single_float(up_output_gradient[ensemble_member])
        hidden_input_rows = cast_to_single_float(hidden[ensemble_member])
        output_cotangent_value = cast_to_single_float(down_output_gradient[ensemble_member])
        gate_forward_pass = cast_to_brain_float(jnp.einsum('nuj,jx->nux', input_tensors, cast_to_single_float(gate_adapter_first[ensemble_member])))
        up_forward_pass = cast_to_brain_float(jnp.einsum('nuj,jx->nux', input_tensors, cast_to_single_float(up_adapter_first[ensemble_member])))
        down_forward_pass = cast_to_brain_float(jnp.einsum('udo,da->uoa', hidden_input_rows, cast_to_single_float(down_adapter_first[ensemble_member])))
        gate_backward_pass = cast_to_brain_float(jnp.einsum('udo,da->uoa', gate_cotangent_value, cast_to_single_float(gate_adapter_second[ensemble_member])))
        up_backward_pass = cast_to_brain_float(jnp.einsum('udo,da->uoa', up_cotangent_value, cast_to_single_float(up_adapter_second[ensemble_member])))
        down_backward_pass = cast_to_brain_float(jnp.einsum('nuj,jx->nux', output_cotangent_value, cast_to_single_float(down_adapter_second[ensemble_member])))
        gate_adapter_a_gradient = adapter_scale * jnp.einsum('ktv,ktj->kvj', input_tensors, cast_to_single_float(gate_backward_pass))
        up_adapter_a_gradient = adapter_scale * jnp.einsum('ktv,ktj->kvj', input_tensors, cast_to_single_float(up_backward_pass))
        down_adapter_b_gradient = adapter_scale * jnp.einsum('ktv,ktj->kvj', output_cotangent_value, cast_to_single_float(down_forward_pass))
        gate_adapter_b_gradient = adapter_scale * jnp.einsum('jpx,jxg->jpg', gate_cotangent_value, cast_to_single_float(gate_forward_pass))
        up_adapter_b_gradient = adapter_scale * jnp.einsum('jpx,jxg->jpg', up_cotangent_value, cast_to_single_float(up_forward_pass))
        down_adapter_a_gradient = adapter_scale * jnp.einsum('jpx,jxg->jpg', hidden_input_rows, cast_to_single_float(down_backward_pass))
        padding = jnp.zeros((EX, N_COORD, LOC // ADAPTER_RANK - 3 * (MODEL_WIDTH + HIDDEN_UNITS) // N_COORD, ADAPTER_RANK), jnp.float32)
        columns.append(jnp.concatenate([blocks(gate_adapter_a_gradient), blocks(up_adapter_a_gradient), blocks(down_adapter_b_gradient), blocks(gate_adapter_b_gradient), blocks(up_adapter_b_gradient), blocks(down_adapter_a_gradient), padding], axis=2))
    joined = jnp.stack(columns, axis=2).reshape(EX, HAD)
    signed = joined * (1.0 - 2.0 * cast_to_single_float(random_sign_flags))[None, :]
    row_list = []
    for prompt in range(EX):
        row_list.append(walsh_full(signed[prompt])[sampled_coordinate_index])
    return jnp.stack(row_list) * (float(HAD) ** -0.5)
```

```python
import functools

import jax
import jax.numpy as jnp
import numpy as np
from jax import lax
from jax.experimental import pallas as pl
from jax.experimental.pallas import tpu as pltpu
from jax.sharding import PartitionSpec as P

F32 = jnp.float32
BF16 = jnp.bfloat16
adapter_scale = 2.0

ANY = pl.BlockSpec(memory_space=pl.ANY)
VMEM = pl.BlockSpec(memory_space=pltpu.VMEM)
SMEM = pl.BlockSpec(memory_space=pltpu.SMEM)


def walsh(degree):
    table = np.ones((1, 1), np.float32)
    while table.shape[0] < degree:
        table = np.block([[table, table], [table, -table]])
    return table


def exchange(value, axis, apart):
    pairs = [(source, source ^ apart) for source in range(lax.axis_size(axis))]
    return lax.ppermute(value, axis, pairs)


def dot(left, right, contract):
    return lax.dot_general(left, right, (contract, ((), ())), preferred_element_type=F32)


def products_kernel(chunk, *refs):
    ins, refs = refs[:11], refs[11:]
    count = len(refs) - 13
    outs, refs = refs[:count], refs[count:]
    bufs, table, sems = refs[:11], refs[11], refs[12]
    copies = [pltpu.make_async_copy(ins[i], bufs[i], sems.at[i]) for i in range(11)]
    for copy in copies:
        copy.start()
    x, go, gg, gu, h, a_gate, b_gate, a_up, b_up, a_down, b_down = bufs
    tokens, rank = x.shape[0], a_gate.shape[1]

    def ready(*which):
        for i in which:
            copies[i].wait()

    def put(slot, value):
        if value.shape[0] == tokens:
            table[slot * tokens : (slot + 1) * tokens, :] = value.astype(BF16)
        else:
            for part in range(tokens // rank):
                row = slot * tokens + part * rank
                table[row : row + rank, :] = value[:, part * rank : (part + 1) * rank].astype(BF16)

    if table.shape[0] > 6 * tokens:
        table[6 * tokens :, :] = jnp.zeros((table.shape[0] - 6 * tokens, rank), BF16)
    ready(0, 5)
    put(3, dot(x[...], a_gate[...], ((1,), (0,))))
    ready(7)
    put(4, dot(x[...], a_up[...], ((1,), (0,))))
    ready(1, 10)
    put(5, dot(go[...], b_down[...], ((1,), (0,))))
    ready(2, 6)
    put(0, dot(b_gate[...].T, gg[...], ((1,), (0,))))
    ready(3, 8)
    put(1, dot(b_up[...].T, gu[...], ((1,), (0,))))
    ready(4, 9)
    put(2, dot(a_down[...].T, h[...], ((1,), (0,))))
    me = lax.axis_index("coord")
    for step in range(count):
        start = pl.multiple_of((me ^ step) * chunk, 16)
        outs[step][...] = table[pl.ds(start, chunk), :]


def products(chunk, count, *ins):
    rank = ins[5].shape[1]
    return pl.pallas_call(
        functools.partial(products_kernel, chunk),
        out_shape=[jax.ShapeDtypeStruct((chunk, rank), BF16)] * count,
        in_specs=[ANY] * 11,
        out_specs=[VMEM] * count,
        scratch_shapes=[pltpu.VMEM(a.shape, a.dtype) for a in ins]
        + [pltpu.VMEM((chunk * count, rank), BF16), pltpu.SemaphoreType.DMA((11,))],
        compiler_params=pltpu.CompilerParams(vmem_limit_bytes=32 * 2**20),
        name="products",
    )(*ins)


def turn_kernel(x, go, x_t, go_t):
    x_t[...] = x[...].T
    go_t[...] = go[...].T


def turn(x, go):
    shape = jax.ShapeDtypeStruct(x.shape[::-1], BF16)
    return pl.pallas_call(
        turn_kernel,
        out_shape=[shape, shape],
        in_specs=[VMEM, VMEM],
        out_specs=[VMEM, VMEM],
        name="turn",
    )(x, go)


def sum_kernel(*refs):
    total = refs[0][...].astype(F32)
    for ref in refs[1:-1]:
        total = total + ref[...].astype(F32)
    refs[-1][...] = total.astype(BF16)


def add_up(parts):
    return pl.pallas_call(
        sum_kernel,
        out_shape=jax.ShapeDtypeStruct(parts[0].shape, BF16),
        in_specs=[VMEM] * len(parts),
        out_specs=VMEM,
        name="add_up",
    )(*parts)


def butterflies(blocks):
    half = 1
    while half < len(blocks):
        done = list(blocks)
        for low in range(len(blocks)):
            if not low & half:
                a, b = blocks[low], blocks[low | half]
                if b is None:
                    done[low], done[low | half] = a, a
                else:
                    done[low], done[low | half] = a + b, a - b
        blocks, half = done, half * 2
    return blocks


def features_kernel(chunk, final_scale, count, *refs):
    parts, refs = refs[:count], refs[count:]
    x_t, go_t, gg, gu, h, flags, where, lanes, inner, columns, out = refs[:11]
    b_gg, b_gu, b_h, b_flags, table, mix, rows, sems = refs[11:]
    sources, targets = (flags, gg, gu, h), (b_flags, b_gg, b_gu, b_h)
    copies = [pltpu.make_async_copy(sources[i], targets[i], sems.at[i]) for i in range(4)]
    for copy in copies:
        copy.start()
    rank = mix.shape[1]
    tokens = gg.shape[1]
    length, block = mix.shape[0], inner.shape[0]
    me = lax.axis_index("coord")
    for step in range(count):
        start = pl.multiple_of((me ^ step) * chunk, 16)
        table[pl.ds(start, chunk), :] = parts[step][...]
    walsh_block = inner[...]

    def along_block(value):
        high = value.astype(BF16)
        low = (value - high.astype(F32)).astype(BF16)
        both = dot(walsh_block, jnp.concatenate([high, low], axis=1), ((1,), (0,)))
        return both[:, :rank] + both[:, rank:]

    copies[0].wait()
    row = 0
    pieces = ((x_t, 0), (x_t, 1), (go_t, 2), (b_gg, 3), (b_gu, 4), (b_h, 5))
    filled = sum(piece.shape[0] for piece, _ in pieces)
    aligned = all(piece.shape[0] % block == 0 for piece, _ in pieces)
    for piece, slot in pieces:
        if slot >= 3:
            copies[slot - 2].wait()
            product = table[slot * tokens : (slot + 1) * tokens, :]
        else:
            product = jnp.concatenate(
                [
                    table[slot * tokens + part * rank : slot * tokens + (part + 1) * rank, :]
                    for part in range(tokens // rank)
                ],
                axis=1,
            )
        size = block if aligned else piece.shape[0]
        for begin in range(0, piece.shape[0], size):
            left = piece[begin : begin + size, :]
            if slot >= 3:
                value = dot(left, product, ((1,), (0,)))
            else:
                value = dot(left, product, ((1,), (1,)))
            value = adapter_scale * value
            value = jnp.where(b_flags[row : row + size, :] == 0, value, -value)
            mix[row : row + size, :] = along_block(value) if aligned else value
            row += size
    if not aligned:
        mix[filled:, :] = jnp.zeros((length - filled, rank), F32)
        for begin in range(0, length, block):
            mix[begin : begin + block, :] = along_block(mix[begin : begin + block, :])
        filled = length
    number = length // block
    full = -(-filled // block)

    def across(step, _):
        begin = pl.multiple_of(step * 8, 8)
        values = [mix[pl.ds(i * block + begin, 8), :] if i < full else None for i in range(number)]
        for i, value in enumerate(butterflies(values)):
            mix[pl.ds(i * block + begin, 8), :] = value
        return _

    if number > 1:
        lax.fori_loop(0, block // 8, across, 0)

    samples = rows.shape[0]
    unroll = 32
    shift = rank.bit_length() - 1

    def pick(step, _):
        begin = pl.multiple_of(step * unroll, unroll)
        for i in range(unroll):
            source = (where[begin + i] >> shift) & (length - 1)
            rows[pl.ds(begin + i, 1), :] = mix[pl.ds(source, 1), :]
        return _

    lax.fori_loop(0, samples // unroll, pick, 0)

    device = me * lax.axis_size("ckpt") + lax.axis_index("ckpt")
    bits = (length * rank).bit_length() - 1
    group = min(512, samples)
    for begin in range(0, samples, group):
        value = rows[begin : begin + group, :]
        high = value.astype(BF16)
        low = (value - high.astype(F32)).astype(BF16)
        mixed = dot(columns[...], jnp.concatenate([high, low], axis=1), ((1,), (1,)))
        index = lanes[:, begin : begin + group]
        column = index & (rank - 1)
        here = lax.broadcasted_iota(jnp.int32, mixed.shape, 0) == column
        chosen = jnp.sum(jnp.where(here, mixed, 0.0), axis=0, keepdims=True)
        parity = (index >> bits) & device
        for fold in (16, 8, 4, 2, 1):
            parity = parity ^ (parity >> fold)
        out[:, begin : begin + group] = jnp.where((parity & 1) == 0, chosen, -chosen) * final_scale


def features(chunk, final_scale, parts, x_t, go_t, gg, gu, h, flags, index):
    rank = flags.shape[1]
    length = flags.shape[0]
    samples = index.shape[0]
    block = min(256, length)
    inner = jnp.asarray(walsh(block), BF16)
    columns = jnp.asarray(np.concatenate([walsh(rank)] * 2, axis=1), BF16)
    return pl.pallas_call(
        functools.partial(features_kernel, chunk, final_scale, len(parts)),
        out_shape=jax.ShapeDtypeStruct((1, samples), F32),
        in_specs=[VMEM] * (len(parts) + 2) + [ANY] * 4 + [SMEM, VMEM, VMEM, VMEM],
        out_specs=VMEM,
        scratch_shapes=[
            pltpu.VMEM(gg.shape, BF16),
            pltpu.VMEM(gu.shape, BF16),
            pltpu.VMEM(h.shape, BF16),
            pltpu.VMEM(flags.shape, jnp.int32),
            pltpu.VMEM((chunk * len(parts), rank), BF16),
            pltpu.VMEM((length, rank), F32),
            pltpu.VMEM((samples, rank), F32),
            pltpu.SemaphoreType.DMA((4,)),
        ],
        compiler_params=pltpu.CompilerParams(vmem_limit_bytes=48 * 2**20),
        name="features",
    )(*parts, x_t, go_t, gg, gu, h, flags, index, index.reshape(1, samples), inner, columns)


def shards(x, gg, gu, h, go, a_gate, b_gate, a_up, b_up, a_down, b_down, flags, index):
    x, go, gg, gu, h = x[0, 0], go[0, 0], gg[0, 0], gu[0, 0], h[0, 0]
    adapters = [a[0] for a in (a_gate, b_gate, a_up, b_up, a_down, b_down)]
    count = lax.axis_size("coord")
    tokens, rank = x.shape[0], adapters[0].shape[1]
    total = flags.shape[0] * count * lax.axis_size("ckpt")
    chunk = 16 * -(-6 * tokens // (16 * count))
    mine = products(chunk, count, x, go, gg, gu, h, *adapters)
    got = [mine[0]] + [exchange(mine[step], "coord", step) for step in range(1, count)]
    x_t, go_t = turn(x, go)
    summed = add_up(got)
    parts = [summed] + [exchange(summed, "coord", step) for step in range(1, count)]
    contrib = features(
        chunk, float(total) ** -0.5, parts, x_t, go_t, gg, gu, h, flags.reshape(-1, rank), index
    )
    contrib = contrib + exchange(contrib, "ckpt", 1)
    apart = 1
    while apart < count:
        contrib = contrib + exchange(contrib, "coord", apart)
        apart *= 2
    return contrib


def solution(mesh):
    in_specs = (
        P("ckpt", "groups", None, "coord"),
        P("ckpt", "groups", "coord", None),
        P("ckpt", "groups", "coord", None),
        P("ckpt", "groups", "coord", None),
        P("ckpt", "groups", None, "coord"),
        P("ckpt", "coord", None),
        P("ckpt", "coord", None),
        P("ckpt", "coord", None),
        P("ckpt", "coord", None),
        P("ckpt", "coord", None),
        P("ckpt", "coord", None),
        P(("coord", "ckpt")),
        P(),
    )
    out_specs = P("groups", None)
    return jax.shard_map(shards, mesh=mesh, in_specs=in_specs, out_specs=out_specs, check_vma=False)
```

```python
import functools

import jax
import jax.numpy as jnp
import numpy as np
from jax import lax
from jax.experimental import pallas as pl
from jax.experimental.pallas import tpu as pltpu
from jax.sharding import PartitionSpec as P

F32 = jnp.float32
BF16 = jnp.bfloat16
MIB = 2**20
adapter_scale = 2.0

ANY = pl.BlockSpec(memory_space=pl.ANY)
VMEM = pl.BlockSpec(memory_space=pltpu.VMEM)
SMEM = pl.BlockSpec(memory_space=pltpu.SMEM)


def limit(size):
    return pltpu.CompilerParams(vmem_limit_bytes=int(size * MIB))


def in_hbm(value):
    return pltpu.with_memory_space_constraint(value, pltpu.HBM)


def walsh(degree):
    table = np.ones((1, 1), np.float32)
    while table.shape[0] < degree:
        table = np.block([[table, table], [table, -table]])
    return table


def exchange(value, axis, apart):
    pairs = [(source, source ^ apart) for source in range(lax.axis_size(axis))]
    return lax.ppermute(value, axis, pairs)


def dot(left, right, contract):
    return lax.dot_general(left, right, (contract, ((), ())), preferred_element_type=F32)


def fetch(sources, targets, sems, cuts):
    groups = []
    slot = 0
    for source, target, cut in zip(sources, targets, cuts, strict=True):
        rows = source.shape[0]
        size = -(-rows // (cut * 16)) * 16
        group = []
        for begin in range(0, rows, size):
            end = min(begin + size, rows)
            copy = pltpu.make_async_copy(
                source.at[begin:end], target.at[begin:end], sems.at[slot]
            )
            copy.start()
            group.append(copy)
            slot += 1
        groups.append(group)

    def wait(which):
        for copy in groups[which]:
            copy.wait()

    return wait


def products_kernel(chunk, transposed, cuts, *refs):
    count = len(transposed)
    places = sorted(set(place for place, _ in transposed))
    number = len(places) + count
    ins, refs = refs[:number], refs[number:]
    out, own, refs = refs[0], refs[1], refs[2:]
    bufs, table, sems = refs[:number], refs[number], refs[number + 1]
    wait = fetch(ins, bufs, sems, cuts)
    rank = out.shape[1]
    arrived = set()
    row = 0
    for slot, (place, turned) in enumerate(transposed):
        for which in (place, len(places) + slot):
            if which not in arrived:
                wait(which)
                arrived.add(which)
        wide, adapter = bufs[place], bufs[len(places) + slot]
        if turned:
            value = dot(adapter[...].T, wide[...], ((1,), (0,)))
            for part in range(value.shape[1] // rank):
                table[row : row + rank, :] = value[:, part * rank : (part + 1) * rank]
                row += rank
        else:
            value = dot(wide[...], adapter[...], ((1,), (0,)))
            table[row : row + value.shape[0], :] = value
            row += value.shape[0]
    if table.shape[0] > row:
        table[row:, :] = jnp.zeros((table.shape[0] - row, rank), F32)
    out[...] = table[...].astype(BF16)
    me = lax.axis_index("coord")
    own[...] = table[pl.ds(pl.multiple_of(me * chunk, 16), chunk), :]


def products(name, chunk, count, transposed, cuts, *ins):
    rank = ins[-1].shape[1]
    return pl.pallas_call(
        functools.partial(products_kernel, chunk, transposed, cuts),
        out_shape=[
            jax.ShapeDtypeStruct((chunk * count, rank), BF16),
            jax.ShapeDtypeStruct((chunk, rank), F32),
        ],
        in_specs=[ANY] * len(ins),
        out_specs=[VMEM, VMEM],
        scratch_shapes=[pltpu.VMEM(a.shape, a.dtype) for a in ins]
        + [pltpu.VMEM((chunk * count, rank), F32), pltpu.SemaphoreType.DMA((sum(cuts),))],
        compiler_params=limit(16),
        name=name,
    )(*ins)


def turn_kernel(x, go, x_t, go_t):
    x_t[...] = x[...].T
    go_t[...] = go[...].T


def turn(x, go):
    shape = jax.ShapeDtypeStruct(x.shape[::-1], BF16)
    return pl.pallas_call(
        turn_kernel,
        out_shape=[shape, shape],
        in_specs=[VMEM, VMEM],
        out_specs=[VMEM, VMEM],
        compiler_params=limit(8),
        name="turn",
    )(x, go)


def sum_kernel(own, got, out):
    me = lax.axis_index("coord")
    total = own[...]
    for source in range(got.shape[0]):
        value = got[source].astype(F32)
        total = total + jnp.where(me == source, 0.0, value)
    total = total.astype(BF16)
    for target in range(got.shape[0]):
        out[target] = total


def add_up(own, got):
    return pl.pallas_call(
        sum_kernel,
        out_shape=jax.ShapeDtypeStruct(got.shape, BF16),
        in_specs=[VMEM, VMEM],
        out_specs=VMEM,
        compiler_params=limit(4),
        name="add_up",
    )(own, got)


def all_sums(out, own, count):
    got = lax.all_to_all(out.reshape(count, -1, out.shape[1]), "coord", 0, 0, tiled=True)
    summed = add_up(own, got)
    got = lax.all_to_all(summed, "coord", 0, 0, tiled=True)
    return got.reshape(out.shape)


def split_dot(table, value, along):
    high = value.astype(BF16)
    low = (value - high.astype(F32)).astype(BF16)
    width = value.shape[1]
    if along == 0:
        both = dot(table, jnp.concatenate([high, low], axis=1), ((1,), (0,)))
        return both[:, :width] + both[:, width:]
    return dot(table, jnp.concatenate([high, low], axis=1), ((1,), (1,)))


def make_pieces(aligned, pieces, products_ref, turned, flags, inner, out):
    block = inner.shape[0]
    rank = products_ref.shape[1]
    row = 0
    for slot, (piece, wait) in enumerate(pieces):
        wait()
        tokens = piece.shape[1]
        start = slot * tokens
        if turned:
            parts = [
                products_ref[start + part : start + part + rank, :]
                for part in range(0, tokens, rank)
            ]
            product, contract = jnp.concatenate(parts, axis=1), ((1,), (1,))
        else:
            product, contract = products_ref[start : start + tokens, :], ((1,), (0,))
        size = block if aligned else piece.shape[0]
        for begin in range(0, piece.shape[0], size):
            value = adapter_scale * dot(piece[begin : begin + size, :], product, contract)
            value = jnp.where(flags[row : row + size, :] == 0, value, -value)
            out[row : row + size, :] = split_dot(inner[...], value, 0) if aligned else value
            row += size


def wide_kernel(aligned, first, cuts, summed, gg, gu, h, flags, inner, out, b_gg, b_gu, b_h, b_flags, sems):
    rows = out.shape[0]
    flags = flags.at[first : first + rows]
    wait = fetch((flags, gg, gu, h), (b_flags, b_gg, b_gu, b_h), sems, cuts)
    wait(0)
    pieces = [
        (piece, functools.partial(wait, which))
        for which, piece in ((1, b_gg), (2, b_gu), (3, b_h))
    ]
    make_pieces(aligned, pieces, summed, False, b_flags, inner, out)


def wide(aligned, first, summed, gg, gu, h, flags, inner):
    rank = flags.shape[1]
    rows = 3 * gg.shape[0]
    cuts = (4, 2, 2, 2)
    return pl.pallas_call(
        functools.partial(wide_kernel, aligned, first, cuts),
        out_shape=jax.ShapeDtypeStruct((rows, rank), F32),
        in_specs=[VMEM] + [ANY] * 4 + [VMEM],
        out_specs=VMEM,
        scratch_shapes=[
            pltpu.VMEM(gg.shape, BF16),
            pltpu.VMEM(gu.shape, BF16),
            pltpu.VMEM(h.shape, BF16),
            pltpu.VMEM((rows, rank), jnp.int32),
            pltpu.SemaphoreType.DMA((sum(cuts),)),
        ],
        compiler_params=limit(16),
        cost_estimate=pl.CostEstimate(flops=10**9, bytes_accessed=10**7, transcendentals=0),
        name="wide",
    )(summed, gg, gu, h, flags, inner)


def butterflies(blocks):
    half = 1
    while half < len(blocks):
        done = list(blocks)
        for low in range(len(blocks)):
            if not low & half:
                a, b = blocks[low], blocks[low | half]
                if b is None:
                    done[low], done[low | half] = a, a
                else:
                    done[low], done[low | half] = a + b, a - b
        blocks, half = done, half * 2
    return blocks


def features_kernel(
    aligned, final_scale, summed, x_t, go_t, wide_mix, flags, where, lanes, inner, columns,
    out, b_flags, mix, rows, sems,
):
    first = 2 * x_t.shape[0] + go_t.shape[0]
    wait = fetch((flags.at[:first],), (b_flags,), sems, (2,))
    length, rank = mix.shape
    block = inner.shape[0]
    wait(0)
    pieces = [(piece, lambda: None) for piece in (x_t, x_t, go_t)]
    make_pieces(aligned, pieces, summed, True, b_flags, inner, mix)
    filled = first + wide_mix.shape[0]
    if not aligned:
        mix[first:filled, :] = wide_mix[...]
        mix[filled:, :] = jnp.zeros((length - filled, rank), F32)
        for begin in range(0, length, block):
            mix[begin : begin + block, :] = split_dot(inner[...], mix[begin : begin + block, :], 0)
    number = length // block
    full = -(-filled // block)

    def load(i, begin):
        if not aligned or i * block < first:
            return mix[pl.ds(i * block + begin, 8), :]
        if i >= full:
            return None
        return wide_mix[pl.ds(i * block - first + begin, 8), :]

    def across(step, _):
        begin = pl.multiple_of(step * 8, 8)
        for i, value in enumerate(butterflies([load(i, begin) for i in range(number)])):
            mix[pl.ds(i * block + begin, 8), :] = value
        return _

    if number > 1:
        lax.fori_loop(0, block // 8, across, 0)

    samples = rows.shape[0]
    unroll = 32

    def pick(step, _):
        begin = pl.multiple_of(step * unroll, unroll)
        values = [mix[pl.ds(where[begin + i], 1), :] for i in range(unroll)]
        for i in range(unroll):
            rows[pl.ds(begin + i, 1), :] = values[i]
        return _

    lax.fori_loop(0, samples // unroll, pick, 0)

    device = lax.axis_index("coord") * lax.axis_size("ckpt") + lax.axis_index("ckpt")
    bits = (length * rank).bit_length() - 1
    group = min(512, samples)
    for begin in range(0, samples, group):
        mixed = split_dot(columns[...], rows[begin : begin + group, :], 1)
        index = lanes[:, begin : begin + group]
        here = lax.broadcasted_iota(jnp.int32, mixed.shape, 0) == (index & (rank - 1))
        chosen = jnp.sum(jnp.where(here, mixed, 0.0), axis=0, keepdims=True)
        parity = (index >> bits) & device
        for fold in (16, 8, 4, 2, 1):
            parity = parity ^ (parity >> fold)
        out[:, begin : begin + group] = jnp.where((parity & 1) == 0, chosen, -chosen) * final_scale


def features(aligned, final_scale, summed, x_t, go_t, wide_mix, flags, where, index, inner):
    length, rank = flags.shape
    samples = index.shape[0]
    columns = jnp.asarray(np.concatenate([walsh(rank)] * 2, axis=1), BF16)
    return pl.pallas_call(
        functools.partial(features_kernel, aligned, final_scale),
        out_shape=jax.ShapeDtypeStruct((1, samples), F32),
        in_specs=[VMEM] * 4 + [ANY, SMEM, VMEM, VMEM, VMEM],
        out_specs=VMEM,
        scratch_shapes=[
            pltpu.VMEM((2 * x_t.shape[0] + go_t.shape[0], rank), jnp.int32),
            pltpu.VMEM((length, rank), F32),
            pltpu.VMEM((samples, rank), F32),
            pltpu.SemaphoreType.DMA((2,)),
        ],
        compiler_params=limit(24),
        name="features",
    )(summed, x_t, go_t, wide_mix, flags, where, index.reshape(1, samples), inner, columns)


def shards(x, gg, gu, h, go, a_gate, b_gate, a_up, b_up, a_down, b_down, flags, index):
    x, go, gg, gu, h = [in_hbm(a[0, 0]) for a in (x, go, gg, gu, h)]
    a_gate, b_gate, a_up, b_up, a_down, b_down = [
        in_hbm(a[0]) for a in (a_gate, b_gate, a_up, b_up, a_down, b_down)
    ]
    count = lax.axis_size("coord")
    tokens, rank = x.shape[0], a_gate.shape[1]
    total = flags.shape[0] * count * lax.axis_size("ckpt")
    flags = in_hbm(flags.reshape(-1, rank))
    length = flags.shape[0]
    first = 3 * x.shape[1]
    block = min(256, length)
    aligned = x.shape[1] % block == 0 and gg.shape[0] % block == 0
    inner = jnp.asarray(walsh(block), BF16)
    where = (index >> (rank.bit_length() - 1)) & (length - 1)
    chunk = 16 * -(-3 * tokens // (16 * count))
    short = products(
        "short", chunk, count, ((0, False), (0, False), (1, False)), (2, 2, 1, 1, 1),
        x, go, a_gate, a_up, b_down,
    )
    short = all_sums(*short, count)
    long = products(
        "long", chunk, count, ((0, True), (1, True), (2, True)), (4, 4, 4, 2, 2, 2),
        gg, gu, h, b_gate, b_up, a_down,
    )
    long = all_sums(*long, count)
    x_t, go_t = turn(x, go)
    wide_mix = wide(aligned, first, short, gg, gu, h, flags, inner)
    contrib = features(
        aligned, float(total) ** -0.5, long, x_t, go_t, wide_mix, flags, where, index, inner
    )
    contrib = contrib + exchange(contrib, "ckpt", 1)
    apart = 1
    while apart < count:
        contrib = contrib + exchange(contrib, "coord", apart)
        apart *= 2
    return contrib


def solution(mesh):
    in_specs = (
        P("ckpt", "groups", None, "coord"),
        P("ckpt", "groups", "coord", None),
        P("ckpt", "groups", "coord", None),
        P("ckpt", "groups", "coord", None),
        P("ckpt", "groups", None, "coord"),
        P("ckpt", "coord", None),
        P("ckpt", "coord", None),
        P("ckpt", "coord", None),
        P("ckpt", "coord", None),
        P("ckpt", "coord", None),
        P("ckpt", "coord", None),
        P(("coord", "ckpt")),
        P(),
    )
    out_specs = P("groups", None)
    return jax.shard_map(shards, mesh=mesh, in_specs=in_specs, out_specs=out_specs, check_vma=False)
```

```python
import functools

import jax
import jax.numpy as jnp
from jax import lax
from jax.experimental import pallas as pl
from jax.experimental.pallas import tpu as pltpu
from jax.sharding import PartitionSpec as P

F32 = jnp.float32
BF16 = jnp.bfloat16
MIB = 2**20
adapter_scale = 2.0

ANY = pl.BlockSpec(memory_space=pl.ANY)
VMEM = pl.BlockSpec(memory_space=pltpu.VMEM)
SMEM = pl.BlockSpec(memory_space=pltpu.SMEM)


def limit(size):
    return pltpu.CompilerParams(vmem_limit_bytes=int(size * MIB))


def in_hbm(value):
    return pltpu.with_memory_space_constraint(value, pltpu.HBM)


def exchange(value, axis, apart):
    pairs = [(source, source ^ apart) for source in range(lax.axis_size(axis))]
    return lax.ppermute(value, axis, pairs)


def dot(left, right, contract):
    return lax.dot_general(left, right, (contract, ((), ())), preferred_element_type=F32)


def fetch(sources, targets, sems, cuts):
    groups = []
    slot = 0
    for source, target, cut in zip(sources, targets, cuts, strict=True):
        rows = source.shape[0]
        size = -(-rows // (cut * 16)) * 16
        group = []
        for begin in range(0, rows, size):
            end = min(begin + size, rows)
            copy = pltpu.make_async_copy(
                source.at[begin:end], target.at[begin:end], sems.at[slot]
            )
            copy.start()
            group.append(copy)
            slot += 1
        groups.append(group)

    def wait(which):
        for copy in groups[which]:
            copy.wait()

    return wait


def stages_of(count):
    stages, shift = [], 0
    while count > 1:
        radix = 2 if shift == 0 else min(4, count)
        stages.append((shift, radix))
        shift += radix.bit_length() - 1
        count //= radix
    return stages


def my_digit(stage):
    return (lax.axis_index("coord") >> stage[0]) & (stage[1] - 1)


def hand_out(table, stage, own, sends):
    digit = my_digit(stage)
    size = own.shape[0]
    own[...] = table[pl.ds(pl.multiple_of(digit * size, 16), size), :]
    for step, send in enumerate(sends, 1):
        begin = pl.multiple_of((digit ^ step) * size, 16)
        send[...] = table[pl.ds(begin, size), :].astype(BF16)


def put_together(own, others, stage, table):
    digit = my_digit(stage)
    size = own.shape[0]
    table[pl.ds(pl.multiple_of(digit * size, 16), size), :] = own[...]
    for step, other in enumerate(others, 1):
        table[pl.ds(pl.multiple_of((digit ^ step) * size, 16), size), :] = other[...]


def handed_out(rows, rank, stage):
    size = rows // stage[1]
    sends = [jax.ShapeDtypeStruct((size, rank), BF16)] * (stage[1] - 1)
    return [jax.ShapeDtypeStruct((size, rank), F32)] + sends


def products_kernel(stage, transposed, cuts, *refs):
    count = len(transposed)
    places = sorted(set(place for place, _ in transposed))
    number = len(places) + count
    ins, own, sends, refs = refs[:number], refs[number], refs[number + 1 : -number - 2], refs[-number - 2 :]
    bufs, table, sems = refs[:number], refs[number], refs[number + 1]
    wait = fetch(ins, bufs, sems, cuts)
    rank = table.shape[1]
    arrived = set()
    row = 0
    for slot, (place, turned) in enumerate(transposed):
        for which in (place, len(places) + slot):
            if which not in arrived:
                wait(which)
                arrived.add(which)
        wide, adapter = bufs[place], bufs[len(places) + slot]
        if turned:
            value = dot(adapter[...].T, wide[...], ((1,), (0,)))
            for part in range(value.shape[1] // rank):
                table[row : row + rank, :] = value[:, part * rank : (part + 1) * rank]
                row += rank
        else:
            value = dot(wide[...], adapter[...], ((1,), (0,)))
            table[row : row + value.shape[0], :] = value
            row += value.shape[0]
    if table.shape[0] > row:
        table[row:, :] = jnp.zeros((table.shape[0] - row, rank), F32)
    hand_out(table, stage, own, sends)


def products(name, rows, stage, transposed, cuts, *ins):
    rank = ins[-1].shape[1]
    shapes = handed_out(rows, rank, stage)
    return pl.pallas_call(
        functools.partial(products_kernel, stage, transposed, cuts),
        out_shape=shapes,
        in_specs=[ANY] * len(ins),
        out_specs=[VMEM] * len(shapes),
        scratch_shapes=[pltpu.VMEM(a.shape, a.dtype) for a in ins]
        + [pltpu.VMEM((rows, rank), F32), pltpu.SemaphoreType.DMA((sum(cuts),))],
        compiler_params=limit(12),
        name=name,
    )(*ins)


def add_kernel(following, count, *refs):
    total = refs[0][...]
    for got in refs[1 : 1 + count]:
        total = total + got[...].astype(F32)
    if following is None:
        refs[1 + count][...] = total.astype(BF16)
    else:
        outs, table = refs[1 + count : -1], refs[-1]
        table[...] = total
        hand_out(table, following, outs[0], outs[1:])


def add_up(own, got, following):
    if following is None:
        shapes, scratch = [jax.ShapeDtypeStruct(own.shape, BF16)], []
    else:
        shapes, scratch = handed_out(*own.shape, following), [pltpu.VMEM(own.shape, F32)]
    return pl.pallas_call(
        functools.partial(add_kernel, following, len(got)),
        out_shape=shapes,
        in_specs=[VMEM] * (1 + len(got)),
        out_specs=[VMEM] * len(shapes),
        scratch_shapes=scratch,
        compiler_params=limit(3),
        name="add_up",
    )(own, *got)


def join_kernel(stage, own, *refs):
    put_together(own, refs[:-1], stage, refs[-1])


def join(own, got, stage):
    return pl.pallas_call(
        functools.partial(join_kernel, stage),
        out_shape=jax.ShapeDtypeStruct((own.shape[0] * stage[1], own.shape[1]), BF16),
        in_specs=[VMEM] * (1 + len(got)),
        out_specs=VMEM,
        compiler_params=limit(3),
        name="join",
    )(own, *got)


def swap(sends, stage):
    return [exchange(send, "coord", step << stage[0]) for step, send in enumerate(sends, 1)]


def all_sums(parts, stages):
    own, sends = parts[0], parts[1:]
    for stage, following in zip(stages, stages[1:] + [None], strict=True):
        own, *sends = add_up(own, swap(sends, stage), following)
    for stage in stages[:0:-1]:
        own = join(own, swap([own] * (stage[1] - 1), stage), stage)
    return [own] + swap([own] * (stages[0][1] - 1), stages[0])


def turn_kernel(x, go, x_t, go_t):
    x_t[...] = x[...].T
    go_t[...] = go[...].T


def turn(x, go):
    shape = jax.ShapeDtypeStruct(x.shape[::-1], BF16)
    return pl.pallas_call(
        turn_kernel,
        out_shape=[shape, shape],
        in_specs=[VMEM, VMEM],
        out_specs=[VMEM, VMEM],
        compiler_params=limit(4),
        name="turn",
    )(x, go)


def butterflies(blocks):
    half = 1
    while half < len(blocks):
        done = list(blocks)
        for low in range(len(blocks)):
            if not low & half:
                a, b = blocks[low], blocks[low | half]
                if b is None:
                    done[low], done[low | half] = a, a
                else:
                    done[low], done[low | half] = a + b, a - b
        blocks, half = done, half * 2
    return blocks


def along_block(value, out, row):
    size = value.shape[0]
    tiles = butterflies([value[i : i + 8, :] for i in range(0, size, 8)])
    for i, tile in enumerate(tiles):
        out[row + 8 * i : row + 8 * i + 8, :] = tile
    for begin in range(row, row + size, 64):
        tiles = butterflies([out[pl.ds(begin + j, 8, stride=8), :] for j in range(8)])
        for j, tile in enumerate(tiles):
            out[begin + 8 * j : begin + 8 * j + 8, :] = tile


def signed(value, flags, row):
    return jnp.where(flags[row : row + value.shape[0], :] == 0, value, -value)


def keep(aligned, value, flags, row, out):
    value = signed(value, flags, row)
    if aligned:
        along_block(value, out, row)
    else:
        out[row : row + value.shape[0], :] = value


def wide_kernel(aligned, block, first, stage, cuts, *refs):
    parts, refs = refs[: stage[1]], refs[stage[1] :]
    gg, gu, h, flags, out, b_gg, b_gu, b_h, b_flags, table, sems = refs
    rows = out.shape[0]
    flags = flags.at[first : first + rows]
    wait = fetch((flags, gg, gu, h), (b_flags, b_gg, b_gu, b_h), sems, cuts)
    put_together(parts[0], parts[1:], stage, table)
    tokens = gg.shape[1]
    wait(0)
    row = 0
    for slot, piece in enumerate((b_gg, b_gu, b_h)):
        wait(slot + 1)
        product = table[slot * tokens : (slot + 1) * tokens, :]
        size = block if aligned else piece.shape[0]
        for begin in range(0, piece.shape[0], size):
            value = dot(piece[begin : begin + size, :], product, ((1,), (0,)))
            keep(aligned, value, b_flags, row, out)
            row += size


def wide(aligned, block, first, stage, parts, gg, gu, h, flags):
    rank = flags.shape[1]
    rows = 3 * gg.shape[0]
    cuts = (4, 2, 2, 2)
    return pl.pallas_call(
        functools.partial(wide_kernel, aligned, block, first, stage, cuts),
        out_shape=jax.ShapeDtypeStruct((rows, rank), F32),
        in_specs=[VMEM] * len(parts) + [ANY] * 4,
        out_specs=VMEM,
        scratch_shapes=[
            pltpu.VMEM(gg.shape, BF16),
            pltpu.VMEM(gu.shape, BF16),
            pltpu.VMEM(h.shape, BF16),
            pltpu.VMEM((rows, rank), jnp.int32),
            pltpu.VMEM((parts[0].shape[0] * stage[1], rank), BF16),
            pltpu.SemaphoreType.DMA((sum(cuts),)),
        ],
        compiler_params=limit(12),
        cost_estimate=pl.CostEstimate(flops=10**9, bytes_accessed=10**7, transcendentals=0),
        name="wide",
    )(*parts, gg, gu, h, flags)


def features_kernel(aligned, block, stage, final_scale, *refs):
    parts, refs = refs[: stage[1]], refs[stage[1] :]
    x_t, go_t, wide_mix, flags, where, lanes, out, b_flags, mix, rows, table, sems = refs
    width, tokens = x_t.shape
    first = 3 * width
    wait = fetch((flags.at[:first],), (b_flags,), sems, (2,))
    length, rank = mix.shape
    put_together(parts[0], parts[1:], stage, table)
    product = [
        jnp.concatenate(
            [table[slot * tokens + part : slot * tokens + part + rank, :] for part in range(0, tokens, rank)],
            axis=1,
        )
        for slot in range(3)
    ]
    wait(0)
    size = block if aligned else width
    both = jnp.concatenate(product[:2], axis=0)
    for begin in range(0, width, size):
        value = dot(x_t[begin : begin + size, :], both, ((1,), (1,)))
        keep(aligned, value[:, :rank], b_flags, begin, mix)
        keep(aligned, value[:, rank:], b_flags, width + begin, mix)
        value = dot(go_t[begin : begin + size, :], product[2], ((1,), (1,)))
        keep(aligned, value, b_flags, 2 * width + begin, mix)
    filled = first + wide_mix.shape[0]
    if not aligned:
        mix[first:filled, :] = wide_mix[...]
        mix[filled:, :] = jnp.zeros((length - filled, rank), F32)
        for begin in range(0, length, block):
            along_block(mix[begin : begin + block, :], mix, begin)
    number = length // block
    full = -(-filled // block)

    def load(i, begin):
        if not aligned or i * block < first:
            return mix[pl.ds(i * block + begin, 8), :]
        if i >= full:
            return None
        return wide_mix[pl.ds(i * block - first + begin, 8), :]

    def across(step, _):
        begin = pl.multiple_of(step * 8, 8)
        for i, value in enumerate(butterflies([load(i, begin) for i in range(number)])):
            mix[pl.ds(i * block + begin, 8), :] = value
        return _

    if number > 1:
        lax.fori_loop(0, block // 8, across, 0)

    samples = rows.shape[0]
    unroll = 32

    def pick(step, _):
        begin = pl.multiple_of(step * unroll, unroll)
        values = [mix[pl.ds(where[begin + i], 1), :] for i in range(unroll)]
        for i in range(unroll):
            rows[pl.ds(begin + i, 1), :] = values[i]
        return _

    lax.fori_loop(0, samples // unroll, pick, 0)

    shape = (rank, 2 * rank)
    column = lax.broadcasted_iota(jnp.int32, shape, 0) & lax.broadcasted_iota(jnp.int32, shape, 1)
    columns = (1 - 2 * parity(column & (rank - 1))).astype(F32).astype(BF16)
    device = lax.axis_index("coord") * lax.axis_size("ckpt") + lax.axis_index("ckpt")
    bits = (length * rank).bit_length() - 1
    group = min(512, samples)
    for begin in range(0, samples, group):
        value = rows[begin : begin + group, :]
        high = value.astype(BF16)
        low = (value - high.astype(F32)).astype(BF16)
        mixed = dot(columns, jnp.concatenate([high, low], axis=1), ((1,), (1,)))
        index = lanes[:, begin : begin + group]
        here = lax.broadcasted_iota(jnp.int32, mixed.shape, 0) == (index & (rank - 1))
        chosen = jnp.sum(jnp.where(here, mixed, 0.0), axis=0, keepdims=True)
        chosen = jnp.where(parity((index >> bits) & device) == 0, chosen, -chosen)
        out[:, begin : begin + group] = chosen * final_scale


def parity(value):
    for fold in (16, 8, 4, 2, 1):
        value = value ^ (value >> fold)
    return value & 1


def features(aligned, block, stage, final_scale, parts, x_t, go_t, wide_mix, flags, where, index):
    length, rank = flags.shape
    samples = index.shape[0]
    return pl.pallas_call(
        functools.partial(features_kernel, aligned, block, stage, final_scale),
        out_shape=jax.ShapeDtypeStruct((1, samples), F32),
        in_specs=[VMEM] * (len(parts) + 3) + [ANY, SMEM, VMEM],
        out_specs=VMEM,
        scratch_shapes=[
            pltpu.VMEM((3 * x_t.shape[0], rank), jnp.int32),
            pltpu.VMEM((length, rank), F32),
            pltpu.VMEM((samples, rank), F32),
            pltpu.VMEM((parts[0].shape[0] * stage[1], rank), BF16),
            pltpu.SemaphoreType.DMA((2,)),
        ],
        compiler_params=limit(16),
        name="features",
    )(*parts, x_t, go_t, wide_mix, flags, where, index.reshape(1, samples))


def shards(x, gg, gu, h, go, a_gate, b_gate, a_up, b_up, a_down, b_down, flags, index):
    x, go, gg, gu, h = [in_hbm(a[0, 0]) for a in (x, go, gg, gu, h)]
    a_gate, b_gate, a_up, b_up, a_down, b_down = [
        in_hbm(a[0]) for a in (a_gate, b_gate, a_up, b_up, a_down, b_down)
    ]
    count = lax.axis_size("coord")
    tokens, rank = x.shape[0], a_gate.shape[1]
    total = flags.shape[0] * count * lax.axis_size("ckpt")
    flags = in_hbm(flags.reshape(-1, rank))
    length = flags.shape[0]
    first = 3 * x.shape[1]
    block = min(256, length)
    aligned = x.shape[1] % block == 0 and gg.shape[0] % block == 0
    where = (index >> (rank.bit_length() - 1)) & (length - 1)
    where = (where & ~63) | (where & 7) << 3 | where >> 3 & 7
    stages = stages_of(count)
    rows = 16 * count * -(-3 * tokens // (16 * count))
    short = products(
        "short", rows, stages[0], ((0, False), (0, False), (1, False)), (2, 2, 1, 1, 1),
        x, go, a_gate, a_up, b_down,
    )
    long = products(
        "long", rows, stages[0], ((0, True), (1, True), (2, True)), (4, 4, 4, 2, 2, 2),
        gg, gu, h, b_gate, b_up, a_down,
    )
    short = all_sums(short, stages)
    long = all_sums(long, stages)
    x_t, go_t = turn(x, go)
    wide_mix = wide(aligned, block, first, stages[0], short, gg, gu, h, flags)
    final_scale = adapter_scale * float(total) ** -0.5
    contrib = features(
        aligned, block, stages[0], final_scale, long, x_t, go_t, wide_mix, flags, where, index
    )
    contrib = contrib + exchange(contrib, "ckpt", 1)
    apart = 1
    while apart < count:
        contrib = contrib + exchange(contrib, "coord", apart)
        apart *= 2
    return contrib


def solution(mesh):
    in_specs = (
        P("ckpt", "groups", None, "coord"),
        P("ckpt", "groups", "coord", None),
        P("ckpt", "groups", "coord", None),
        P("ckpt", "groups", "coord", None),
        P("ckpt", "groups", None, "coord"),
        P("ckpt", "coord", None),
        P("ckpt", "coord", None),
        P("ckpt", "coord", None),
        P("ckpt", "coord", None),
        P("ckpt", "coord", None),
        P("ckpt", "coord", None),
        P(("coord", "ckpt")),
        P(),
    )
    out_specs = P("groups", None)
    return jax.shard_map(shards, mesh=mesh, in_specs=in_specs, out_specs=out_specs, check_vma=False)
```

```python
import functools

import jax
import jax.numpy as jnp
from jax import lax
from jax.experimental import pallas as pl
from jax.experimental.pallas import tpu as pltpu
from jax.sharding import PartitionSpec as P

F32 = jnp.float32
BF16 = jnp.bfloat16
MIB = 2**20
adapter_scale = 2.0

ANY = pl.BlockSpec(memory_space=pl.ANY)
VMEM = pl.BlockSpec(memory_space=pltpu.VMEM)
SMEM = pl.BlockSpec(memory_space=pltpu.SMEM)


def limit(size):
    return pltpu.CompilerParams(vmem_limit_bytes=int(size * MIB))


def in_hbm(value):
    return pltpu.with_memory_space_constraint(value, pltpu.HBM)


def exchange(value, axis, apart):
    pairs = [(source, source ^ apart) for source in range(lax.axis_size(axis))]
    return lax.ppermute(value, axis, pairs)


def dot(left, right, contract):
    return lax.dot_general(left, right, (contract, ((), ())), preferred_element_type=F32)


def fetch(sources, targets, sems, cuts):
    groups = []
    slot = 0
    for source, target, cut in zip(sources, targets, cuts, strict=True):
        rows = source.shape[0]
        size = -(-rows // (cut * 16)) * 16
        group = []
        for begin in range(0, rows, size):
            end = min(begin + size, rows)
            copy = pltpu.make_async_copy(
                source.at[begin:end], target.at[begin:end], sems.at[slot]
            )
            copy.start()
            group.append(copy)
            slot += 1
        groups.append(group)

    def wait(which):
        for copy in groups[which]:
            copy.wait()

    return wait


def stages_of(count):
    stages, shift = [], 0
    while count > 1:
        radix = 2 if shift == 0 else min(4, count)
        stages.append((shift, radix))
        shift += radix.bit_length() - 1
        count //= radix
    return stages


def my_digit(stage):
    return (lax.axis_index("coord") >> stage[0]) & (stage[1] - 1)


def hand_out(table, stage, own, sends):
    digit = my_digit(stage)
    size = own.shape[0]
    own[...] = table[pl.ds(pl.multiple_of(digit * size, 16), size), :]
    for step, send in enumerate(sends, 1):
        begin = pl.multiple_of((digit ^ step) * size, 16)
        send[...] = table[pl.ds(begin, size), :].astype(BF16)


def put_together(gathered, stages, table):
    count = 1
    for _, radix in stages:
        count *= radix
    size = table.shape[0] // count
    for device in range(count):
        place = 0
        for shift, radix in stages:
            place = place * radix + (device >> shift & (radix - 1))
        table[place * size : (place + 1) * size, :] = gathered[device * size : (device + 1) * size, :]


def handed_out(rows, rank, stage):
    size = rows // stage[1]
    sends = [jax.ShapeDtypeStruct((size, rank), BF16)] * (stage[1] - 1)
    return [jax.ShapeDtypeStruct((size, rank), F32)] + sends


def products_kernel(stage, transposed, cuts, *refs):
    count = len(transposed)
    places = sorted(set(place for place, _ in transposed))
    number = len(places) + count
    ins, own, sends, refs = refs[:number], refs[number], refs[number + 1 : -number - 2], refs[-number - 2 :]
    bufs, table, sems = refs[:number], refs[number], refs[number + 1]
    wait = fetch(ins, bufs, sems, cuts)
    rank = table.shape[1]
    arrived = set()
    row = 0
    for slot, (place, turned) in enumerate(transposed):
        for which in (place, len(places) + slot):
            if which not in arrived:
                wait(which)
                arrived.add(which)
        wide, adapter = bufs[place], bufs[len(places) + slot]
        if turned:
            value = dot(adapter[...].T, wide[...], ((1,), (0,)))
            for part in range(value.shape[1] // rank):
                table[row : row + rank, :] = value[:, part * rank : (part + 1) * rank]
                row += rank
        else:
            value = dot(wide[...], adapter[...], ((1,), (0,)))
            table[row : row + value.shape[0], :] = value
            row += value.shape[0]
    if table.shape[0] > row:
        table[row:, :] = jnp.zeros((table.shape[0] - row, rank), F32)
    hand_out(table, stage, own, sends)


def products(name, rows, stage, transposed, cuts, *ins):
    rank = ins[-1].shape[1]
    shapes = handed_out(rows, rank, stage)
    return pl.pallas_call(
        functools.partial(products_kernel, stage, transposed, cuts),
        out_shape=shapes,
        in_specs=[ANY] * len(ins),
        out_specs=[VMEM] * len(shapes),
        scratch_shapes=[pltpu.VMEM(a.shape, a.dtype) for a in ins]
        + [pltpu.VMEM((rows, rank), F32), pltpu.SemaphoreType.DMA((sum(cuts),))],
        compiler_params=limit(12),
        name=name,
    )(*ins)


def add_kernel(following, count, *refs):
    total = refs[0][...]
    for got in refs[1 : 1 + count]:
        total = total + got[...].astype(F32)
    if following is None:
        refs[1 + count][...] = total.astype(BF16)
    else:
        outs, table = refs[1 + count : -1], refs[-1]
        table[...] = total
        hand_out(table, following, outs[0], outs[1:])


def add_up(own, got, following):
    if following is None:
        shapes, scratch = [jax.ShapeDtypeStruct(own.shape, BF16)], []
    else:
        shapes, scratch = handed_out(*own.shape, following), [pltpu.VMEM(own.shape, F32)]
    return pl.pallas_call(
        functools.partial(add_kernel, following, len(got)),
        out_shape=shapes,
        in_specs=[VMEM] * (1 + len(got)),
        out_specs=[VMEM] * len(shapes),
        scratch_shapes=scratch,
        compiler_params=limit(3),
        name="add_up",
    )(own, *got)


def swap(sends, stage):
    return [exchange(send, "coord", step << stage[0]) for step, send in enumerate(sends, 1)]


def all_sums(parts, stages):
    own, sends = parts[0], parts[1:]
    for stage, following in zip(stages, stages[1:] + [None], strict=True):
        own, *sends = add_up(own, swap(sends, stage), following)
    return lax.all_gather(own, "coord", axis=0, tiled=True)


def turn_kernel(x, go, x_t, go_t):
    x_t[...] = x[...].T
    go_t[...] = go[...].T


def turn(x, go):
    shape = jax.ShapeDtypeStruct(x.shape[::-1], BF16)
    return pl.pallas_call(
        turn_kernel,
        out_shape=[shape, shape],
        in_specs=[VMEM, VMEM],
        out_specs=[VMEM, VMEM],
        compiler_params=limit(4),
        name="turn",
    )(x, go)


def butterflies(blocks):
    half = 1
    while half < len(blocks):
        done = list(blocks)
        for low in range(len(blocks)):
            if not low & half:
                a, b = blocks[low], blocks[low | half]
                if b is None:
                    done[low], done[low | half] = a, a
                else:
                    done[low], done[low | half] = a + b, a - b
        blocks, half = done, half * 2
    return blocks


def along_block(value, out, row):
    size = value.shape[0]
    tiles = butterflies([value[i : i + 8, :] for i in range(0, size, 8)])
    for i, tile in enumerate(tiles):
        out[row + 8 * i : row + 8 * i + 8, :] = tile
    for begin in range(row, row + size, 64):
        tiles = butterflies([out[pl.ds(begin + j, 8, stride=8), :] for j in range(8)])
        for j, tile in enumerate(tiles):
            out[begin + 8 * j : begin + 8 * j + 8, :] = tile


def signed(value, flags, row):
    return jnp.where(flags[row : row + value.shape[0], :] == 0, value, -value)


def keep(aligned, value, flags, row, out):
    value = signed(value, flags, row)
    if aligned:
        along_block(value, out, row)
    else:
        out[row : row + value.shape[0], :] = value


def wide_kernel(
    aligned, block, first, stages, cuts,
    summed, gg, gu, h, flags, out, b_gg, b_gu, b_h, b_flags, table, sems,
):
    rows = out.shape[0]
    flags = flags.at[first : first + rows]
    wait = fetch((flags, gg, gu, h), (b_flags, b_gg, b_gu, b_h), sems, cuts)
    put_together(summed, stages, table)
    tokens = gg.shape[1]
    wait(0)
    row = 0
    for slot, piece in enumerate((b_gg, b_gu, b_h)):
        wait(slot + 1)
        product = table[slot * tokens : (slot + 1) * tokens, :]
        size = block if aligned else piece.shape[0]
        for begin in range(0, piece.shape[0], size):
            value = dot(piece[begin : begin + size, :], product, ((1,), (0,)))
            keep(aligned, value, b_flags, row, out)
            row += size


def wide(aligned, block, first, stages, summed, gg, gu, h, flags):
    rank = flags.shape[1]
    rows = 3 * gg.shape[0]
    cuts = (4, 2, 2, 2)
    return pl.pallas_call(
        functools.partial(wide_kernel, aligned, block, first, stages, cuts),
        out_shape=jax.ShapeDtypeStruct((rows, rank), F32),
        in_specs=[VMEM] + [ANY] * 4,
        out_specs=VMEM,
        scratch_shapes=[
            pltpu.VMEM(gg.shape, BF16),
            pltpu.VMEM(gu.shape, BF16),
            pltpu.VMEM(h.shape, BF16),
            pltpu.VMEM((rows, rank), jnp.int32),
            pltpu.VMEM(summed.shape, BF16),
            pltpu.SemaphoreType.DMA((sum(cuts),)),
        ],
        compiler_params=limit(12),
        cost_estimate=pl.CostEstimate(flops=10**9, bytes_accessed=10**7, transcendentals=0),
        name="wide",
    )(summed, gg, gu, h, flags)


def features_kernel(
    aligned, block, stages, final_scale,
    summed, x_t, go_t, wide_mix, flags, where, lanes, out, b_flags, mix, rows, table, sems,
):
    width, tokens = x_t.shape
    first = 3 * width
    wait = fetch((flags.at[:first],), (b_flags,), sems, (2,))
    length, rank = mix.shape
    put_together(summed, stages, table)
    product = [
        jnp.concatenate(
            [table[slot * tokens + part : slot * tokens + part + rank, :] for part in range(0, tokens, rank)],
            axis=1,
        )
        for slot in range(3)
    ]
    wait(0)
    size = block if aligned else width
    both = jnp.concatenate(product[:2], axis=0)
    for begin in range(0, width, size):
        value = dot(x_t[begin : begin + size, :], both, ((1,), (1,)))
        keep(aligned, value[:, :rank], b_flags, begin, mix)
        keep(aligned, value[:, rank:], b_flags, width + begin, mix)
        value = dot(go_t[begin : begin + size, :], product[2], ((1,), (1,)))
        keep(aligned, value, b_flags, 2 * width + begin, mix)
    filled = first + wide_mix.shape[0]
    if not aligned:
        mix[first:filled, :] = wide_mix[...]
        mix[filled:, :] = jnp.zeros((length - filled, rank), F32)
        for begin in range(0, length, block):
            along_block(mix[begin : begin + block, :], mix, begin)
    number = length // block
    full = -(-filled // block)

    def load(i, begin):
        if not aligned or i * block < first:
            return mix[pl.ds(i * block + begin, 8), :]
        if i >= full:
            return None
        return wide_mix[pl.ds(i * block - first + begin, 8), :]

    def across(step, _):
        begin = pl.multiple_of(step * 8, 8)
        for i, value in enumerate(butterflies([load(i, begin) for i in range(number)])):
            mix[pl.ds(i * block + begin, 8), :] = value
        return _

    if number > 1:
        lax.fori_loop(0, block // 8, across, 0, unroll=4)

    samples = rows.shape[0]
    unroll, ahead = min(256, samples), 16

    def pick(step, _):
        begin = pl.multiple_of(step * unroll, unroll)
        held = []
        for i in range(unroll):
            held.append(mix[pl.ds(where[begin + i], 1), :])
            if i >= ahead:
                rows[pl.ds(begin + i - ahead, 1), :] = held[i - ahead]
        for i in range(unroll - ahead, unroll):
            rows[pl.ds(begin + i, 1), :] = held[i]
        return _

    lax.fori_loop(0, samples // unroll, pick, 0)

    shape = (rank, 2 * rank)
    column = lax.broadcasted_iota(jnp.int32, shape, 0) & lax.broadcasted_iota(jnp.int32, shape, 1)
    columns = (1 - 2 * parity(column & (rank - 1))).astype(F32).astype(BF16)
    device = lax.axis_index("coord") * lax.axis_size("ckpt") + lax.axis_index("ckpt")
    bits = (length * rank).bit_length() - 1
    group = min(512, samples)
    for begin in range(0, samples, group):
        value = rows[begin : begin + group, :]
        high = value.astype(BF16)
        low = (value - high.astype(F32)).astype(BF16)
        mixed = dot(columns, jnp.concatenate([high, low], axis=1), ((1,), (1,)))
        index = lanes[:, begin : begin + group]
        here = lax.broadcasted_iota(jnp.int32, mixed.shape, 0) == (index & (rank - 1))
        chosen = jnp.sum(jnp.where(here, mixed, 0.0), axis=0, keepdims=True)
        chosen = jnp.where(parity((index >> bits) & device) == 0, chosen, -chosen)
        out[:, begin : begin + group] = chosen * final_scale


def parity(value):
    for fold in (16, 8, 4, 2, 1):
        value = value ^ (value >> fold)
    return value & 1


def features(aligned, block, stages, final_scale, summed, x_t, go_t, wide_mix, flags, where, index):
    length, rank = flags.shape
    samples = index.shape[0]
    return pl.pallas_call(
        functools.partial(features_kernel, aligned, block, stages, final_scale),
        out_shape=jax.ShapeDtypeStruct((1, samples), F32),
        in_specs=[VMEM] * 4 + [ANY, SMEM, VMEM],
        out_specs=VMEM,
        scratch_shapes=[
            pltpu.VMEM((3 * x_t.shape[0], rank), jnp.int32),
            pltpu.VMEM((length, rank), F32),
            pltpu.VMEM((samples, rank), F32),
            pltpu.VMEM(summed.shape, BF16),
            pltpu.SemaphoreType.DMA((2,)),
        ],
        compiler_params=limit(16),
        name="features",
    )(summed, x_t, go_t, wide_mix, flags, where, index.reshape(1, samples))


def shards(x, gg, gu, h, go, a_gate, b_gate, a_up, b_up, a_down, b_down, flags, index):
    x, go, gg, gu, h = [in_hbm(a[0, 0]) for a in (x, go, gg, gu, h)]
    a_gate, b_gate, a_up, b_up, a_down, b_down = [
        in_hbm(a[0]) for a in (a_gate, b_gate, a_up, b_up, a_down, b_down)
    ]
    count = lax.axis_size("coord")
    tokens, rank = x.shape[0], a_gate.shape[1]
    total = flags.shape[0] * count * lax.axis_size("ckpt")
    flags = in_hbm(flags.reshape(-1, rank))
    length = flags.shape[0]
    first = 3 * x.shape[1]
    block = min(256, length)
    aligned = x.shape[1] % block == 0 and gg.shape[0] % block == 0
    where = (index >> (rank.bit_length() - 1)) & (length - 1)
    where = (where & ~63) | (where & 7) << 3 | where >> 3 & 7
    stages = stages_of(count)
    rows = 16 * count * -(-3 * tokens // (16 * count))
    short = products(
        "short", rows, stages[0], ((0, False), (0, False), (1, False)), (2, 2, 1, 1, 1),
        x, go, a_gate, a_up, b_down,
    )
    long = products(
        "long", rows, stages[0], ((0, True), (1, True), (2, True)), (4, 4, 4, 2, 2, 2),
        gg, gu, h, b_gate, b_up, a_down,
    )
    short = all_sums(short, stages)
    long = all_sums(long, stages)
    x_t, go_t = turn(x, go)
    wide_mix = wide(aligned, block, first, stages, short, gg, gu, h, flags)
    final_scale = adapter_scale * float(total) ** -0.5
    contrib = features(
        aligned, block, stages, final_scale, long, x_t, go_t, wide_mix, flags, where, index
    )
    contrib = contrib + exchange(contrib, "ckpt", 1)
    for stage in stages:
        terms = [contrib] + swap([contrib] * (stage[1] - 1), stage)
        while len(terms) > 1:
            terms = [a + b for a, b in zip(terms[::2], terms[1::2], strict=True)]
        contrib = terms[0]
    return contrib


def solution(mesh):
    in_specs = (
        P("ckpt", "groups", None, "coord"),
        P("ckpt", "groups", "coord", None),
        P("ckpt", "groups", "coord", None),
        P("ckpt", "groups", "coord", None),
        P("ckpt", "groups", None, "coord"),
        P("ckpt", "coord", None),
        P("ckpt", "coord", None),
        P("ckpt", "coord", None),
        P("ckpt", "coord", None),
        P("ckpt", "coord", None),
        P("ckpt", "coord", None),
        P(("coord", "ckpt")),
        P(),
    )
    out_specs = P("groups", None)
    return jax.shard_map(shards, mesh=mesh, in_specs=in_specs, out_specs=out_specs, check_vma=False)
```

```python
import functools

import jax
import jax.numpy as jnp
from jax import lax
from jax.experimental import pallas as pl
from jax.experimental.pallas import tpu as pltpu
from jax.sharding import PartitionSpec as P

F32 = jnp.float32
BF16 = jnp.bfloat16
MIB = 2**20
adapter_scale = 2.0

ANY = pl.BlockSpec(memory_space=pl.ANY)
VMEM = pl.BlockSpec(memory_space=pltpu.VMEM)
SMEM = pl.BlockSpec(memory_space=pltpu.SMEM)


def limit(size):
    return pltpu.CompilerParams(vmem_limit_bytes=int(size * MIB))


def in_hbm(value):
    return pltpu.with_memory_space_constraint(value, pltpu.HBM)


def exchange(value, axis, apart):
    pairs = [(source, source ^ apart) for source in range(lax.axis_size(axis))]
    return lax.ppermute(value, axis, pairs)


def dot(left, right, contract):
    return lax.dot_general(left, right, (contract, ((), ())), preferred_element_type=F32)


def fetch(sources, targets, sems, cuts):
    groups = []
    slot = 0
    for source, target, cut in zip(sources, targets, cuts, strict=True):
        rows = source.shape[0]
        size = -(-rows // (cut * 16)) * 16
        group = []
        for begin in range(0, rows, size):
            end = min(begin + size, rows)
            copy = pltpu.make_async_copy(
                source.at[begin:end], target.at[begin:end], sems.at[slot]
            )
            copy.start()
            group.append(copy)
            slot += 1
        groups.append(group)

    def wait(which):
        for copy in groups[which]:
            copy.wait()

    return wait


def stages_of(count):
    stages, shift = [], 0
    while count > 1:
        radix = 2 if shift == 0 else min(4, count)
        stages.append((shift, radix))
        shift += radix.bit_length() - 1
        count //= radix
    return stages


def my_digit(stage):
    return (lax.axis_index("coord") >> stage[0]) & (stage[1] - 1)


def hand_out(table, stage, own, sends):
    digit = my_digit(stage)
    size = own.shape[0]
    own[...] = table[pl.ds(pl.multiple_of(digit * size, 16), size), :]
    for step, send in enumerate(sends, 1):
        begin = pl.multiple_of((digit ^ step) * size, 16)
        send[...] = table[pl.ds(begin, size), :].astype(BF16)


def put_together(own, others, stage, table):
    digit = my_digit(stage)
    size = own.shape[0]
    table[pl.ds(pl.multiple_of(digit * size, 16), size), :] = own[...]
    for step, other in enumerate(others, 1):
        table[pl.ds(pl.multiple_of((digit ^ step) * size, 16), size), :] = other[...]


def handed_out(rows, rank, stage):
    size = rows // stage[1]
    sends = [jax.ShapeDtypeStruct((size, rank), BF16)] * (stage[1] - 1)
    return [jax.ShapeDtypeStruct((size, rank), F32)] + sends


def write_products(pairs, table):
    rank = table.shape[1]
    row = 0
    for wide, adapter, turned in pairs:
        if turned:
            value = dot(adapter[...].T, wide[...], ((1,), (0,)))
            for part in range(value.shape[1] // rank):
                table[row : row + rank, :] = value[:, part * rank : (part + 1) * rank]
                row += rank
        else:
            value = dot(wide[...], adapter[...], ((1,), (0,)))
            table[row : row + value.shape[0], :] = value
            row += value.shape[0]
    if table.shape[0] > row:
        table[row:, :] = jnp.zeros((table.shape[0] - row, rank), F32)


def short_kernel(stage, cuts, *refs):
    number = len(cuts)
    ins, held = refs[:number], refs[number : 2 * number]
    own, sends, table, sems = refs[2 * number], refs[2 * number + 1 : -2], refs[-2], refs[-1]
    wait = fetch(ins, held, sems, cuts)
    for which in range(5):
        wait(which)
    x, go, a_gate, a_up, b_down = held[:5]
    write_products(((x, a_gate, False), (x, a_up, False), (go, b_down, False)), table)
    hand_out(table, stage, own, sends)
    for which in range(5, number):
        wait(which)


def short_products(rows, stage, cuts, *ins):
    rank = ins[2].shape[1]
    shapes = [jax.ShapeDtypeStruct(a.shape, a.dtype) for a in ins]
    shapes = shapes + handed_out(rows, rank, stage)
    outs = pl.pallas_call(
        functools.partial(short_kernel, stage, cuts),
        out_shape=shapes,
        in_specs=[ANY] * len(ins),
        out_specs=[VMEM] * len(shapes),
        scratch_shapes=[pltpu.VMEM((rows, rank), F32), pltpu.SemaphoreType.DMA((sum(cuts),))],
        compiler_params=limit(10),
        name="short",
    )(*ins)
    return outs[: len(ins)], outs[len(ins) :]


def long_kernel(stage, cuts, gg, gu, h, b_gate, b_up, a_down, flags, held, *refs):
    own, sends, table, sems = refs[0], refs[1:-2], refs[-2], refs[-1]
    wait = fetch((flags.at[: held.shape[0]],), (held,), sems, cuts)
    write_products(((gg, b_gate, True), (gu, b_up, True), (h, a_down, True)), table)
    hand_out(table, stage, own, sends)
    wait(0)


def long_products(rows, stage, cuts, filled, *ins):
    rank = ins[3].shape[1]
    shapes = [jax.ShapeDtypeStruct((filled, rank), jnp.int32)] + handed_out(rows, rank, stage)
    outs = pl.pallas_call(
        functools.partial(long_kernel, stage, cuts),
        out_shape=shapes,
        in_specs=[VMEM] * 6 + [ANY],
        out_specs=[VMEM] * len(shapes),
        scratch_shapes=[pltpu.VMEM((rows, rank), F32), pltpu.SemaphoreType.DMA((sum(cuts),))],
        compiler_params=limit(10),
        name="long",
    )(*ins)
    return outs[0], outs[1:]


def add_kernel(following, count, *refs):
    total = refs[0][...]
    for got in refs[1 : 1 + count]:
        total = total + got[...].astype(F32)
    if following is None:
        refs[1 + count][...] = total.astype(BF16)
    else:
        outs, table = refs[1 + count : -1], refs[-1]
        table[...] = total
        hand_out(table, following, outs[0], outs[1:])


def add_up(own, got, following):
    if following is None:
        shapes, scratch = [jax.ShapeDtypeStruct(own.shape, BF16)], []
    else:
        shapes, scratch = handed_out(*own.shape, following), [pltpu.VMEM(own.shape, F32)]
    return pl.pallas_call(
        functools.partial(add_kernel, following, len(got)),
        out_shape=shapes,
        in_specs=[VMEM] * (1 + len(got)),
        out_specs=[VMEM] * len(shapes),
        scratch_shapes=scratch,
        compiler_params=limit(3),
        name="add_up",
    )(own, *got)


def join_kernel(stage, own, *refs):
    put_together(own, refs[:-1], stage, refs[-1])


def join(own, got, stage):
    return pl.pallas_call(
        functools.partial(join_kernel, stage),
        out_shape=jax.ShapeDtypeStruct((own.shape[0] * stage[1], own.shape[1]), BF16),
        in_specs=[VMEM] * (1 + len(got)),
        out_specs=VMEM,
        compiler_params=limit(3),
        name="join",
    )(own, *got)


def swap(sends, stage):
    return [exchange(send, "coord", step << stage[0]) for step, send in enumerate(sends, 1)]


def all_sums(parts, stages, ahead=()):
    own, sends = parts[0], parts[1:]
    for stage, following in zip(stages, stages[1:] + [None], strict=True):
        own, *sends = add_up(own, swap(sends, stage), following)
    for stage in stages[:0:-1]:
        got = swap([own] * (stage[1] - 1), stage)
        if stage is stages[1] and ahead:
            own, *ahead = lax.optimization_barrier((own, *ahead))
        own = join(own, got, stage)
    parts = [own] + swap([own] * (stages[0][1] - 1), stages[0])
    return (parts, *ahead) if ahead else parts


def turn_kernel(x, go, x_t, go_t):
    x_t[...] = x[...].T
    go_t[...] = go[...].T


def turn(x, go):
    shape = jax.ShapeDtypeStruct(x.shape[::-1], BF16)
    return pl.pallas_call(
        turn_kernel,
        out_shape=[shape, shape],
        in_specs=[VMEM, VMEM],
        out_specs=[VMEM, VMEM],
        compiler_params=limit(4),
        name="turn",
    )(x, go)


def butterflies(blocks):
    half = 1
    while half < len(blocks):
        done = list(blocks)
        for low in range(len(blocks)):
            if not low & half:
                a, b = blocks[low], blocks[low | half]
                if b is None:
                    done[low], done[low | half] = a, a
                else:
                    done[low], done[low | half] = a + b, a - b
        blocks, half = done, half * 2
    return blocks


def along_block(value, out, row):
    size = value.shape[0]
    tiles = butterflies([value[i : i + 8, :] for i in range(0, size, 8)])
    for i, tile in enumerate(tiles):
        out[row + 8 * i : row + 8 * i + 8, :] = tile
    for begin in range(row, row + size, 64):
        tiles = butterflies([out[pl.ds(begin + j, 8, stride=8), :] for j in range(8)])
        for j, tile in enumerate(tiles):
            out[begin + 8 * j : begin + 8 * j + 8, :] = tile


def signed(value, flags, row):
    return jnp.where(flags[row : row + value.shape[0], :] == 0, value, -value)


def keep(aligned, value, flags, row, out):
    value = signed(value, flags, row)
    if aligned:
        along_block(value, out, row)
    else:
        out[row : row + value.shape[0], :] = value


def wide_kernel(aligned, block, first, stage, *refs):
    parts, refs = refs[: stage[1]], refs[stage[1] :]
    gg, gu, h, flags, out, table = refs
    put_together(parts[0], parts[1:], stage, table)
    tokens = gg.shape[1]
    flags = flags.at[first : first + out.shape[0]]
    row = 0
    for slot, piece in enumerate((gg, gu, h)):
        product = table[slot * tokens : (slot + 1) * tokens, :]
        size = block if aligned else piece.shape[0]
        for begin in range(0, piece.shape[0], size):
            value = dot(piece[begin : begin + size, :], product, ((1,), (0,)))
            keep(aligned, value, flags, row, out)
            row += size


def wide(aligned, block, first, stage, parts, gg, gu, h, flags):
    rank = flags.shape[1]
    return pl.pallas_call(
        functools.partial(wide_kernel, aligned, block, first, stage),
        out_shape=jax.ShapeDtypeStruct((3 * gg.shape[0], rank), F32),
        in_specs=[VMEM] * (len(parts) + 4),
        out_specs=VMEM,
        scratch_shapes=[pltpu.VMEM((parts[0].shape[0] * stage[1], rank), BF16)],
        compiler_params=limit(6),
        cost_estimate=pl.CostEstimate(flops=10**9, bytes_accessed=10**7, transcendentals=0),
        name="wide",
    )(*parts, gg, gu, h, flags)


def rows_kernel(aligned, block, stage, *refs):
    parts, refs = refs[: stage[1]], refs[stage[1] :]
    x_t, go_t, wide_mix, flags, mix, table = refs
    width, tokens = x_t.shape
    first = 3 * width
    length, rank = mix.shape
    put_together(parts[0], parts[1:], stage, table)
    product = [
        jnp.concatenate(
            [table[slot * tokens + part : slot * tokens + part + rank, :] for part in range(0, tokens, rank)],
            axis=1,
        )
        for slot in range(3)
    ]
    size = block if aligned else width
    both = jnp.concatenate(product[:2], axis=0)
    for begin in range(0, width, size):
        value = dot(x_t[begin : begin + size, :], both, ((1,), (1,)))
        keep(aligned, value[:, :rank], flags, begin, mix)
        keep(aligned, value[:, rank:], flags, width + begin, mix)
        value = dot(go_t[begin : begin + size, :], product[2], ((1,), (1,)))
        keep(aligned, value, flags, 2 * width + begin, mix)
    filled = first + wide_mix.shape[0]
    if not aligned:
        mix[first:filled, :] = wide_mix[...]
        mix[filled:, :] = jnp.zeros((length - filled, rank), F32)
        for begin in range(0, length, block):
            along_block(mix[begin : begin + block, :], mix, begin)
    number = length // block
    full = -(-filled // block)

    def load(i, begin):
        if not aligned or i * block < first:
            return mix[pl.ds(i * block + begin, 8), :]
        if i >= full:
            return None
        return wide_mix[pl.ds(i * block - first + begin, 8), :]

    def across(step, _):
        begin = pl.multiple_of(step * 8, 8)
        for i, value in enumerate(butterflies([load(i, begin) for i in range(number)])):
            mix[pl.ds(i * block + begin, 8), :] = value
        return _

    if number > 1:
        lax.fori_loop(0, block // 8, across, 0, unroll=4)


def along_rows(aligned, block, stage, length, parts, x_t, go_t, wide_mix, flags):
    rank = flags.shape[1]
    return pl.pallas_call(
        functools.partial(rows_kernel, aligned, block, stage),
        out_shape=jax.ShapeDtypeStruct((length, rank), F32),
        in_specs=[VMEM] * (len(parts) + 4),
        out_specs=VMEM,
        scratch_shapes=[pltpu.VMEM((parts[0].shape[0] * stage[1], rank), BF16)],
        compiler_params=limit(6),
        name="along_rows",
    )(*parts, x_t, go_t, wide_mix, flags)


def parity(value):
    for fold in (16, 8, 4, 2, 1):
        value = value ^ (value >> fold)
    return value & 1


def sample_kernel(final_scale, mix, where, lanes, out, rows):
    length, rank = mix.shape
    samples = rows.shape[0]
    unroll, ahead = min(256, samples), 16

    def pick(step, _):
        begin = pl.multiple_of(step * unroll, unroll)
        held = []
        for i in range(unroll):
            held.append(mix[pl.ds(where[begin + i], 1), :])
            if i >= ahead:
                rows[pl.ds(begin + i - ahead, 1), :] = held[i - ahead]
        for i in range(unroll - ahead, unroll):
            rows[pl.ds(begin + i, 1), :] = held[i]
        return _

    lax.fori_loop(0, samples // unroll, pick, 0)

    shape = (rank, 2 * rank)
    column = lax.broadcasted_iota(jnp.int32, shape, 0) & lax.broadcasted_iota(jnp.int32, shape, 1)
    columns = (1 - 2 * parity(column & (rank - 1))).astype(F32).astype(BF16)
    device = lax.axis_index("coord") * lax.axis_size("ckpt") + lax.axis_index("ckpt")
    bits = (length * rank).bit_length() - 1
    group = min(512, samples)
    for begin in range(0, samples, group):
        value = rows[begin : begin + group, :]
        high = value.astype(BF16)
        low = (value - high.astype(F32)).astype(BF16)
        mixed = dot(columns, jnp.concatenate([high, low], axis=1), ((1,), (1,)))
        index = lanes[:, begin : begin + group]
        here = lax.broadcasted_iota(jnp.int32, mixed.shape, 0) == (index & (rank - 1))
        chosen = jnp.sum(jnp.where(here, mixed, 0.0), axis=0, keepdims=True)
        chosen = jnp.where(parity((index >> bits) & device) == 0, chosen, -chosen)
        out[:, begin : begin + group] = chosen * final_scale


def sampled(final_scale, mix, where, index):
    samples = index.shape[0]
    return pl.pallas_call(
        functools.partial(sample_kernel, final_scale),
        out_shape=jax.ShapeDtypeStruct((1, samples), F32),
        in_specs=[VMEM, SMEM, VMEM],
        out_specs=VMEM,
        scratch_shapes=[pltpu.VMEM((samples, mix.shape[1]), F32)],
        compiler_params=limit(6),
        cost_estimate=pl.CostEstimate(flops=10**9, bytes_accessed=10**7, transcendentals=0),
        name="sampled",
    )(mix, where, index.reshape(1, samples))


def shards(x, gg, gu, h, go, a_gate, b_gate, a_up, b_up, a_down, b_down, flags, index):
    x, go, gg, gu, h = [in_hbm(a[0, 0]) for a in (x, go, gg, gu, h)]
    a_gate, b_gate, a_up, b_up, a_down, b_down = [
        in_hbm(a[0]) for a in (a_gate, b_gate, a_up, b_up, a_down, b_down)
    ]
    count = lax.axis_size("coord")
    tokens, rank = x.shape[0], a_gate.shape[1]
    total = flags.shape[0] * count * lax.axis_size("ckpt")
    flags = in_hbm(flags.reshape(-1, rank))
    length = flags.shape[0]
    first = 3 * x.shape[1]
    filled = first + 3 * gg.shape[0]
    block = min(256, length)
    aligned = x.shape[1] % block == 0 and gg.shape[0] % block == 0
    where = (index >> (rank.bit_length() - 1)) & (length - 1)
    where = (where & ~63) | (where & 7) << 3 | where >> 3 & 7
    stages = stages_of(count)
    rows = 16 * count * -(-3 * tokens // (16 * count))
    held, short = short_products(
        rows, stages[0], (2, 2, 1, 1, 1, 4, 4, 4, 1, 1, 1),
        x, go, a_gate, a_up, b_down, gg, gu, h, b_gate, b_up, a_down,
    )
    x, go, gg, gu, h = held[0], held[1], held[5], held[6], held[7]
    flags, long = long_products(rows, stages[0], (4,), filled, *held[5:], flags)
    short = all_sums(short, stages)
    x_t, go_t = turn(x, go)
    long, x_t, go_t = all_sums(long, stages, (x_t, go_t))
    wide_mix = wide(aligned, block, first, stages[0], short, gg, gu, h, flags)
    final_scale = adapter_scale * float(total) ** -0.5
    mix = along_rows(aligned, block, stages[0], length, long, x_t, go_t, wide_mix, flags)
    samples = index.shape[0] // 2
    halves = []
    for begin in (0, samples):
        span = slice(begin, begin + samples)
        contrib = sampled(final_scale, mix, where[span], index[span])
        contrib = contrib + exchange(contrib, "ckpt", 1)
        apart = 1
        while apart < count:
            contrib = contrib + exchange(contrib, "coord", apart)
            apart *= 2
        halves.append(contrib)
    return jnp.concatenate(halves, axis=1)


def solution(mesh):
    in_specs = (
        P("ckpt", "groups", None, "coord"),
        P("ckpt", "groups", "coord", None),
        P("ckpt", "groups", "coord", None),
        P("ckpt", "groups", "coord", None),
        P("ckpt", "groups", None, "coord"),
        P("ckpt", "coord", None),
        P("ckpt", "coord", None),
        P("ckpt", "coord", None),
        P("ckpt", "coord", None),
        P("ckpt", "coord", None),
        P("ckpt", "coord", None),
        P(("coord", "ckpt")),
        P(),
    )
    out_specs = P("groups", None)
    return jax.shard_map(shards, mesh=mesh, in_specs=in_specs, out_specs=out_specs, check_vma=False)
```

```python
import functools

import jax
import jax.numpy as jnp
from jax import lax
from jax.experimental import pallas as pl
from jax.experimental.pallas import tpu as pltpu
from jax.sharding import PartitionSpec as P

F32 = jnp.float32
BF16 = jnp.bfloat16
MIB = 2**20
adapter_scale = 2.0

ANY = pl.BlockSpec(memory_space=pl.ANY)
VMEM = pl.BlockSpec(memory_space=pltpu.VMEM)
SMEM = pl.BlockSpec(memory_space=pltpu.SMEM)


def limit(size):
    return pltpu.CompilerParams(vmem_limit_bytes=int(size * MIB))


def in_hbm(value):
    return pltpu.with_memory_space_constraint(value, pltpu.HBM)


def exchange(value, axis, apart):
    pairs = [(source, source ^ apart) for source in range(lax.axis_size(axis))]
    return lax.ppermute(value, axis, pairs)


def dot(left, right, contract):
    return lax.dot_general(left, right, (contract, ((), ())), preferred_element_type=F32)


def fetch(sources, targets, sems, cuts):
    groups = []
    slot = 0
    for source, target, cut in zip(sources, targets, cuts, strict=True):
        rows = source.shape[0]
        size = -(-rows // (cut * 16)) * 16
        group = []
        for begin in range(0, rows, size):
            end = min(begin + size, rows)
            copy = pltpu.make_async_copy(
                source.at[begin:end], target.at[begin:end], sems.at[slot]
            )
            copy.start()
            group.append(copy)
            slot += 1
        groups.append(group)

    def wait(which):
        for copy in groups[which]:
            copy.wait()

    return wait


def stages_of(count):
    stages, shift = [], 0
    while count > 1:
        radix = 2 if shift == 0 else min(4, count)
        stages.append((shift, radix))
        shift += radix.bit_length() - 1
        count //= radix
    return stages


def my_digit(stage):
    return (lax.axis_index("coord") >> stage[0]) & (stage[1] - 1)


def hand_out(table, stage, own, sends):
    digit = my_digit(stage)
    size = own.shape[0]
    own[...] = table[pl.ds(pl.multiple_of(digit * size, 16), size), :]
    for step, send in enumerate(sends, 1):
        begin = pl.multiple_of((digit ^ step) * size, 16)
        send[...] = table[pl.ds(begin, size), :].astype(BF16)


def put_together(own, others, stage, table):
    digit = my_digit(stage)
    size = own.shape[0]
    table[pl.ds(pl.multiple_of(digit * size, 16), size), :] = own[...]
    for step, other in enumerate(others, 1):
        table[pl.ds(pl.multiple_of((digit ^ step) * size, 16), size), :] = other[...]


def handed_out(rows, rank, stage):
    size = rows // stage[1]
    sends = [jax.ShapeDtypeStruct((size, rank), BF16)] * (stage[1] - 1)
    return [jax.ShapeDtypeStruct((size, rank), F32)] + sends


def fill(table, row):
    if table.shape[0] > row:
        table[row:, :] = jnp.zeros((table.shape[0] - row, table.shape[1]), F32)


def short_kernel(stage, cuts, *refs):
    ins, (x, go), (own, *sends), (a_gate, a_up, b_down, table, sems) = (
        refs[:5], refs[5:7], refs[7:-5], refs[-5:]
    )
    wait = fetch(ins, (x, go, a_gate, a_up, b_down), sems, cuts)
    for which in range(5):
        wait(which)
    tokens = x.shape[0]
    table[:tokens, :] = dot(x[...], a_gate[...], ((1,), (0,)))
    table[tokens : 2 * tokens, :] = dot(x[...], a_up[...], ((1,), (0,)))
    table[2 * tokens : 3 * tokens, :] = dot(go[...], b_down[...], ((1,), (0,)))
    fill(table, 3 * tokens)
    hand_out(table, stage, own, sends)


def short_products(rows, stage, *ins):
    rank = ins[2].shape[1]
    cuts = (2, 2, 1, 1, 1)
    shapes = [jax.ShapeDtypeStruct(a.shape, a.dtype) for a in ins[:2]]
    shapes = shapes + handed_out(rows, rank, stage)
    x, go, *sends = pl.pallas_call(
        functools.partial(short_kernel, stage, cuts),
        out_shape=shapes,
        in_specs=[ANY] * len(ins),
        out_specs=[VMEM] * len(shapes),
        scratch_shapes=[pltpu.VMEM(a.shape, a.dtype) for a in ins[2:]]
        + [pltpu.VMEM((rows, rank), F32), pltpu.SemaphoreType.DMA((sum(cuts),))],
        compiler_params=limit(4),
        cost_estimate=pl.CostEstimate(flops=10**8, bytes_accessed=6 * 10**6, transcendentals=0),
        name="short",
    )(*ins)
    return x, go, sends


def long_kernel(stage, cut, *refs):
    ins, held, (own, *sends), (*adapters, table, sems) = refs[:6], refs[6:9], refs[9:-5], refs[-5:]
    rank = table.shape[1]
    per = cut + 1
    waits = []

    def begin(slot):
        wait = fetch(
            (ins[3 + slot], ins[slot]),
            (adapters[slot], held[slot]),
            sems.at[slot * per : (slot + 1) * per],
            (1, cut),
        )
        waits.append(wait)

    begin(0)
    begin(1)
    row = 0
    for slot in range(3):
        waits[slot](0)
        adapter = adapters[slot][...].T
        waits[slot](1)
        if slot == 0:
            begin(2)
        value = dot(adapter, held[slot][...], ((1,), (0,)))
        for part in range(value.shape[1] // rank):
            table[row : row + rank, :] = value[:, part * rank : (part + 1) * rank]
            row += rank
    fill(table, row)
    hand_out(table, stage, own, sends)


def long_products(rows, stage, *ins):
    rank = ins[3].shape[1]
    cut = 4
    held = [jax.ShapeDtypeStruct(a.shape, a.dtype) for a in ins[:3]]
    shapes = held + handed_out(rows, rank, stage)
    outs = pl.pallas_call(
        functools.partial(long_kernel, stage, cut),
        out_shape=shapes,
        in_specs=[ANY] * 6,
        out_specs=[VMEM] * len(shapes),
        scratch_shapes=[pltpu.VMEM(a.shape, a.dtype) for a in ins[3:]]
        + [pltpu.VMEM((rows, rank), F32), pltpu.SemaphoreType.DMA((3 * (cut + 1),))],
        compiler_params=limit(6),
        cost_estimate=pl.CostEstimate(flops=10**9, bytes_accessed=8 * 10**6, transcendentals=0),
        name="long",
    )(*ins)
    return *outs[:3], outs[3:]


def add_kernel(following, count, *refs):
    total = refs[0][...]
    for got in refs[1 : 1 + count]:
        total = total + got[...].astype(F32)
    if following is None:
        refs[1 + count][...] = total.astype(BF16)
    else:
        outs, table = refs[1 + count : -1], refs[-1]
        table[...] = total
        hand_out(table, following, outs[0], outs[1:])


def add_up(own, got, following):
    if following is None:
        shapes, scratch = [jax.ShapeDtypeStruct(own.shape, BF16)], []
    else:
        shapes, scratch = handed_out(*own.shape, following), [pltpu.VMEM(own.shape, F32)]
    return pl.pallas_call(
        functools.partial(add_kernel, following, len(got)),
        out_shape=shapes,
        in_specs=[VMEM] * (1 + len(got)),
        out_specs=[VMEM] * len(shapes),
        scratch_shapes=scratch,
        compiler_params=limit(3),
        name="add_up",
    )(own, *got)


def join_kernel(stage, own, *refs):
    put_together(own, refs[:-1], stage, refs[-1])


def join(own, got, stage):
    return pl.pallas_call(
        functools.partial(join_kernel, stage),
        out_shape=jax.ShapeDtypeStruct((own.shape[0] * stage[1], own.shape[1]), BF16),
        in_specs=[VMEM] * (1 + len(got)),
        out_specs=VMEM,
        compiler_params=limit(3),
        name="join",
    )(own, *got)


def swap(sends, stage):
    return [exchange(send, "coord", step << stage[0]) for step, send in enumerate(sends, 1)]


def after(first, second):
    return lax.optimization_barrier((first, second))[1]


def all_sums(halves, stages, ahead):
    owns = [half[0] for half in halves]
    sends = [half[1:] for half in halves]
    for stage, following in zip(stages, stages[1:] + [None], strict=True):
        got = [swap(send, stage) for send in sends]
        for i in range(len(owns)):
            own = after(owns[0], owns[i]) if i else owns[i]
            owns[i], *sends[i] = add_up(own, got[i], following)
    for stage in stages[:0:-1]:
        got = [swap([own] * (stage[1] - 1), stage) for own in owns]
        if stage is stages[1]:
            owns[0] = after(ahead, owns[0])
        for i in range(len(owns)):
            own = after(owns[0], owns[i]) if i else owns[i]
            owns[i] = join(own, got[i], stage)
    return [[own] + swap([own] * (stages[0][1] - 1), stages[0]) for own in owns]


def turn_kernel(x, go, x_t, go_t):
    x_t[...] = x[...].T
    go_t[...] = go[...].T


def turn(x, go):
    shape = jax.ShapeDtypeStruct(x.shape[::-1], BF16)
    return pl.pallas_call(
        turn_kernel,
        out_shape=[shape, shape],
        in_specs=[VMEM, VMEM],
        out_specs=[VMEM, VMEM],
        compiler_params=limit(4),
        name="turn",
    )(x, go)


def butterflies(blocks):
    half = 1
    while half < len(blocks):
        done = list(blocks)
        for low in range(len(blocks)):
            if not low & half:
                a, b = blocks[low], blocks[low | half]
                if b is None:
                    done[low], done[low | half] = a, a
                else:
                    done[low], done[low | half] = a + b, a - b
        blocks, half = done, half * 2
    return blocks


def along_block(value, out, row):
    size = value.shape[0]
    tiles = butterflies([value[i : i + 8, :] for i in range(0, size, 8)])
    for i, tile in enumerate(tiles):
        out[row + 8 * i : row + 8 * i + 8, :] = tile
    for begin in range(row, row + size, 64):
        tiles = butterflies([out[pl.ds(begin + j, 8, stride=8), :] for j in range(8)])
        for j, tile in enumerate(tiles):
            out[begin + 8 * j : begin + 8 * j + 8, :] = tile


def signed(value, flags, row):
    return jnp.where(flags[row : row + value.shape[0], :] == 0, value, -value)


def keep(aligned, value, flags, row, out):
    value = signed(value, flags, row)
    if aligned:
        along_block(value, out, row)
    else:
        out[row : row + value.shape[0], :] = value


def wide_kernel(aligned, block, first, stage, *refs):
    parts, refs = refs[: stage[1]], refs[stage[1] :]
    gg, gu, h, flags, out, table = refs
    put_together(parts[0], parts[1:], stage, table)
    tokens = gg.shape[1]
    flags = flags.at[first : first + out.shape[0]]
    row = 0
    for slot, piece in enumerate((gg, gu, h)):
        product = table[slot * tokens : (slot + 1) * tokens, :]
        size = block if aligned else piece.shape[0]
        for begin in range(0, piece.shape[0], size):
            value = dot(piece[begin : begin + size, :], product, ((1,), (0,)))
            keep(aligned, value, flags, row, out)
            row += size


def wide(aligned, block, first, stage, parts, gg, gu, h, flags):
    rank = flags.shape[1]
    return pl.pallas_call(
        functools.partial(wide_kernel, aligned, block, first, stage),
        out_shape=jax.ShapeDtypeStruct((3 * gg.shape[0], rank), F32),
        in_specs=[VMEM] * (len(parts) + 4),
        out_specs=VMEM,
        scratch_shapes=[pltpu.VMEM((parts[0].shape[0] * stage[1], rank), BF16)],
        compiler_params=limit(6),
        cost_estimate=pl.CostEstimate(flops=10**9, bytes_accessed=10**7, transcendentals=0),
        name="wide",
    )(*parts, gg, gu, h, flags)


def rows_kernel(aligned, block, stage, *refs):
    parts, refs = refs[: stage[1]], refs[stage[1] :]
    x_t, go_t, wide_mix, flags, mix, table = refs
    width, tokens = x_t.shape
    first = 3 * width
    length, rank = mix.shape
    put_together(parts[0], parts[1:], stage, table)
    product = [
        jnp.concatenate(
            [table[slot * tokens + part : slot * tokens + part + rank, :] for part in range(0, tokens, rank)],
            axis=1,
        )
        for slot in range(3)
    ]
    size = block if aligned else width
    both = jnp.concatenate(product[:2], axis=0)
    for begin in range(0, width, size):
        value = dot(x_t[begin : begin + size, :], both, ((1,), (1,)))
        keep(aligned, value[:, :rank], flags, begin, mix)
        keep(aligned, value[:, rank:], flags, width + begin, mix)
        value = dot(go_t[begin : begin + size, :], product[2], ((1,), (1,)))
        keep(aligned, value, flags, 2 * width + begin, mix)
    filled = first + wide_mix.shape[0]
    if not aligned:
        mix[first:filled, :] = wide_mix[...]
        mix[filled:, :] = jnp.zeros((length - filled, rank), F32)
        for begin in range(0, length, block):
            along_block(mix[begin : begin + block, :], mix, begin)
    number = length // block
    full = -(-filled // block)

    def load(i, begin):
        if not aligned or i * block < first:
            return mix[pl.ds(i * block + begin, 8), :]
        if i >= full:
            return None
        return wide_mix[pl.ds(i * block - first + begin, 8), :]

    def across(step, _):
        begin = pl.multiple_of(step * 8, 8)
        for i, value in enumerate(butterflies([load(i, begin) for i in range(number)])):
            mix[pl.ds(i * block + begin, 8), :] = value
        return _

    if number > 1:
        lax.fori_loop(0, block // 8, across, 0, unroll=4)


def along_rows(aligned, block, stage, length, parts, x_t, go_t, wide_mix, flags):
    rank = flags.shape[1]
    return pl.pallas_call(
        functools.partial(rows_kernel, aligned, block, stage),
        out_shape=jax.ShapeDtypeStruct((length, rank), F32),
        in_specs=[VMEM] * (len(parts) + 4),
        out_specs=VMEM,
        scratch_shapes=[pltpu.VMEM((parts[0].shape[0] * stage[1], rank), BF16)],
        compiler_params=limit(6),
        name="along_rows",
    )(*parts, x_t, go_t, wide_mix, flags)


def parity(value):
    for fold in (16, 8, 4, 2, 1):
        value = value ^ (value >> fold)
    return value & 1


def sample_kernel(final_scale, mix, where, lanes, out, columns, *rows):
    length, rank = mix.shape
    samples = out.shape[1]
    group = rows[0].shape[0]
    number = samples // group
    ahead = 16
    shape = columns.shape
    column = lax.broadcasted_iota(jnp.int32, shape, 0) & lax.broadcasted_iota(jnp.int32, shape, 1)
    columns[...] = (1 - 2 * parity(column & (rank - 1))).astype(F32).astype(BF16)
    device = lax.axis_index("coord") * lax.axis_size("ckpt") + lax.axis_index("ckpt")
    bits = (length * rank).bit_length() - 1

    def pick(which, target):
        begin = which * group
        held = []
        for i in range(group):
            held.append(mix[pl.ds(where[begin + i], 1), :])
            if i >= ahead:
                target[i - ahead : i - ahead + 1, :] = held[i - ahead]
        for i in range(group - ahead, group):
            target[i : i + 1, :] = held[i]

    def transform(which, source):
        begin = pl.multiple_of(which * group, group)
        value = source[...]
        high = value.astype(BF16)
        low = (value - high.astype(F32)).astype(BF16)
        mixed = dot(columns[...], jnp.concatenate([high, low], axis=1), ((1,), (1,)))
        index = lanes[:, pl.ds(begin, group)]
        here = lax.broadcasted_iota(jnp.int32, mixed.shape, 0) == (index & (rank - 1))
        chosen = jnp.sum(jnp.where(here, mixed, 0.0), axis=0, keepdims=True)
        chosen = jnp.where(parity((index >> bits) & device) == 0, chosen, -chosen)
        out[:, pl.ds(begin, group)] = chosen * final_scale

    pick(0, rows[0])

    def step(turn_of, _):
        first = turn_of * 2
        transform(first, rows[0])
        pick(first + 1, rows[1])
        transform(first + 1, rows[1])
        pick(lax.rem(first + 2, number), rows[0])
        return _

    lax.fori_loop(0, number // 2, step, 0)


def sampled(final_scale, mix, where, index):
    samples, rank = index.shape[0], mix.shape[1]
    group = min(256, samples // 2)
    return pl.pallas_call(
        functools.partial(sample_kernel, final_scale),
        out_shape=jax.ShapeDtypeStruct((1, samples), F32),
        in_specs=[VMEM, SMEM, VMEM],
        out_specs=VMEM,
        scratch_shapes=[pltpu.VMEM((rank, 2 * rank), BF16)] + [pltpu.VMEM((group, rank), F32)] * 2,
        compiler_params=limit(4),
        name="sampled",
    )(mix, where, index.reshape(1, samples))


def shards(x, gg, gu, h, go, a_gate, b_gate, a_up, b_up, a_down, b_down, flags, index):
    x, go, gg, gu, h = [a[0, 0] for a in (x, go, gg, gu, h)]
    a_gate, b_gate, a_up, b_up, a_down, b_down = [
        a[0] for a in (a_gate, b_gate, a_up, b_up, a_down, b_down)
    ]
    count = lax.axis_size("coord")
    tokens, rank = x.shape[0], a_gate.shape[1]
    total = flags.shape[0] * count * lax.axis_size("ckpt")
    flags = flags.reshape(-1, rank)
    length = flags.shape[0]
    first = 3 * x.shape[1]
    block = min(256, length)
    aligned = x.shape[1] % block == 0 and gg.shape[0] % block == 0
    where = (index >> (rank.bit_length() - 1)) & (length - 1)
    where = (where & ~63) | (where & 7) << 3 | where >> 3 & 7
    stages = stages_of(count)
    rows = 16 * count * -(-3 * tokens // (16 * count))
    x, go, short = short_products(
        rows, stages[0], *[in_hbm(a) for a in (x, go, a_gate, a_up, b_down)]
    )
    gg, gu, h, long = long_products(
        rows, stages[0], *[in_hbm(a) for a in (gg, gu, h, b_gate, b_up, a_down)]
    )
    flags = after(long[0], flags)
    x_t, go_t = turn(x, go)
    short, long = all_sums([short, long], stages, go_t)
    wide_mix = wide(aligned, block, first, stages[0], short, gg, gu, h, flags)
    final_scale = adapter_scale * float(total) ** -0.5
    mix = along_rows(aligned, block, stages[0], length, long, x_t, go_t, wide_mix, flags)
    contrib = sampled(final_scale, mix, where, index)
    contrib = contrib + exchange(contrib, "ckpt", 1)
    apart = 1
    while apart < count:
        contrib = contrib + exchange(contrib, "coord", apart)
        apart *= 2
    return contrib


def solution(mesh):
    in_specs = (
        P("ckpt", "groups", None, "coord"),
        P("ckpt", "groups", "coord", None),
        P("ckpt", "groups", "coord", None),
        P("ckpt", "groups", "coord", None),
        P("ckpt", "groups", None, "coord"),
        P("ckpt", "coord", None),
        P("ckpt", "coord", None),
        P("ckpt", "coord", None),
        P("ckpt", "coord", None),
        P("ckpt", "coord", None),
        P("ckpt", "coord", None),
        P(("coord", "ckpt")),
        P(),
    )
    out_specs = P("groups", None)
    return jax.shard_map(shards, mesh=mesh, in_specs=in_specs, out_specs=out_specs, check_vma=False)
```

```python
import functools

import jax
import jax.numpy as jnp
from jax import lax
from jax.experimental import pallas as pl
from jax.experimental.pallas import tpu as pltpu
from jax.sharding import PartitionSpec as P

F32 = jnp.float32
BF16 = jnp.bfloat16
MIB = 2**20
adapter_scale = 2.0

ANY = pl.BlockSpec(memory_space=pl.ANY)
VMEM = pl.BlockSpec(memory_space=pltpu.VMEM)
SMEM = pl.BlockSpec(memory_space=pltpu.SMEM)


def limit(size):
    return pltpu.CompilerParams(vmem_limit_bytes=int(size * MIB))


def in_hbm(value):
    return pltpu.with_memory_space_constraint(value, pltpu.HBM)


def exchange(value, axis, apart):
    pairs = [(source, source ^ apart) for source in range(lax.axis_size(axis))]
    return lax.ppermute(value, axis, pairs)


def dot(left, right, contract):
    return lax.dot_general(left, right, (contract, ((), ())), preferred_element_type=F32)


def fetch(sources, targets, sems, cuts):
    groups = []
    slot = 0
    for source, target, cut in zip(sources, targets, cuts, strict=True):
        rows = source.shape[0]
        size = -(-rows // (cut * 16)) * 16
        group = []
        for begin in range(0, rows, size):
            end = min(begin + size, rows)
            copy = pltpu.make_async_copy(
                source.at[begin:end], target.at[begin:end], sems.at[slot]
            )
            copy.start()
            group.append(copy)
            slot += 1
        groups.append(group)

    def wait(which):
        for copy in groups[which]:
            copy.wait()

    return wait


def stages_of(count):
    stages, shift = [], 0
    while count > 1:
        radix = 2 if shift == 0 else min(4, count)
        stages.append((shift, radix))
        shift += radix.bit_length() - 1
        count //= radix
    return stages


def my_digit(stage):
    return (lax.axis_index("coord") >> stage[0]) & (stage[1] - 1)


def hand_out(table, stage, own, sends):
    digit = my_digit(stage)
    size = own.shape[0]
    own[...] = table[pl.ds(pl.multiple_of(digit * size, 16), size), :]
    for step, send in enumerate(sends, 1):
        begin = pl.multiple_of((digit ^ step) * size, 16)
        send[...] = table[pl.ds(begin, size), :].astype(BF16)


def put_together(own, others, stage, table):
    digit = my_digit(stage)
    size = own.shape[0]
    table[pl.ds(pl.multiple_of(digit * size, 16), size), :] = own[...]
    for step, other in enumerate(others, 1):
        table[pl.ds(pl.multiple_of((digit ^ step) * size, 16), size), :] = other[...]


def handed_out(rows, rank, stage):
    size = rows // stage[1]
    sends = [jax.ShapeDtypeStruct((size, rank), BF16)] * (stage[1] - 1)
    return [jax.ShapeDtypeStruct((size, rank), F32)] + sends


def fill(table, row):
    if table.shape[0] > row:
        table[row:, :] = jnp.zeros((table.shape[0] - row, table.shape[1]), F32)


def short_kernel(stage, cuts, *refs):
    ins, (x, go), (own, *sends), (a_gate, a_up, b_down, table, sems) = (
        refs[:5], refs[5:7], refs[7:-5], refs[-5:]
    )
    wait = fetch(ins, (x, go, a_gate, a_up, b_down), sems, cuts)
    for which in range(5):
        wait(which)
    tokens = x.shape[0]
    table[:tokens, :] = dot(x[...], a_gate[...], ((1,), (0,)))
    table[tokens : 2 * tokens, :] = dot(x[...], a_up[...], ((1,), (0,)))
    table[2 * tokens : 3 * tokens, :] = dot(go[...], b_down[...], ((1,), (0,)))
    fill(table, 3 * tokens)
    hand_out(table, stage, own, sends)


def short_products(rows, stage, *ins):
    rank = ins[2].shape[1]
    cuts = (2, 2, 1, 1, 1)
    shapes = [jax.ShapeDtypeStruct(a.shape, a.dtype) for a in ins[:2]]
    shapes = shapes + handed_out(rows, rank, stage)
    x, go, *sends = pl.pallas_call(
        functools.partial(short_kernel, stage, cuts),
        out_shape=shapes,
        in_specs=[ANY] * len(ins),
        out_specs=[VMEM] * len(shapes),
        scratch_shapes=[pltpu.VMEM(a.shape, a.dtype) for a in ins[2:]]
        + [pltpu.VMEM((rows, rank), F32), pltpu.SemaphoreType.DMA((sum(cuts),))],
        compiler_params=limit(4),
        cost_estimate=pl.CostEstimate(flops=10**8, bytes_accessed=6 * 10**6, transcendentals=0),
        name="short",
    )(*ins)
    return x, go, sends


def long_kernel(stage, cut, *refs):
    ins, held, (own, *sends), (*adapters, table, sems) = refs[:6], refs[6:9], refs[9:-5], refs[-5:]
    rank = table.shape[1]
    per = cut + 1
    waits = []

    def begin(slot):
        wait = fetch(
            (ins[3 + slot], ins[slot]),
            (adapters[slot], held[slot]),
            sems.at[slot * per : (slot + 1) * per],
            (1, cut),
        )
        waits.append(wait)

    begin(0)
    begin(1)
    row = 0
    for slot in range(3):
        waits[slot](0)
        adapter = adapters[slot][...].T
        waits[slot](1)
        if slot == 0:
            begin(2)
        value = dot(adapter, held[slot][...], ((1,), (0,)))
        for part in range(value.shape[1] // rank):
            table[row : row + rank, :] = value[:, part * rank : (part + 1) * rank]
            row += rank
    fill(table, row)
    hand_out(table, stage, own, sends)


def long_products(rows, stage, *ins):
    rank = ins[3].shape[1]
    cut = 4
    held = [jax.ShapeDtypeStruct(a.shape, a.dtype) for a in ins[:3]]
    shapes = held + handed_out(rows, rank, stage)
    outs = pl.pallas_call(
        functools.partial(long_kernel, stage, cut),
        out_shape=shapes,
        in_specs=[ANY] * 6,
        out_specs=[VMEM] * len(shapes),
        scratch_shapes=[pltpu.VMEM(a.shape, a.dtype) for a in ins[3:]]
        + [pltpu.VMEM((rows, rank), F32), pltpu.SemaphoreType.DMA((3 * (cut + 1),))],
        compiler_params=limit(6),
        cost_estimate=pl.CostEstimate(flops=10**9, bytes_accessed=8 * 10**6, transcendentals=0),
        name="long",
    )(*ins)
    return *outs[:3], outs[3:]


def add_kernel(following, count, *refs):
    total = refs[0][...]
    for got in refs[1 : 1 + count]:
        total = total + got[...].astype(F32)
    if following is None:
        refs[1 + count][...] = total.astype(BF16)
    else:
        outs, table = refs[1 + count : -1], refs[-1]
        table[...] = total
        hand_out(table, following, outs[0], outs[1:])


def add_up(own, got, following):
    if following is None:
        shapes, scratch = [jax.ShapeDtypeStruct(own.shape, BF16)], []
    else:
        shapes, scratch = handed_out(*own.shape, following), [pltpu.VMEM(own.shape, F32)]
    return pl.pallas_call(
        functools.partial(add_kernel, following, len(got)),
        out_shape=shapes,
        in_specs=[VMEM] * (1 + len(got)),
        out_specs=[VMEM] * len(shapes),
        scratch_shapes=scratch,
        compiler_params=limit(3),
        name="add_up",
    )(own, *got)


def join_kernel(stage, own, *refs):
    put_together(own, refs[:-1], stage, refs[-1])


def join(own, got, stage):
    return pl.pallas_call(
        functools.partial(join_kernel, stage),
        out_shape=jax.ShapeDtypeStruct((own.shape[0] * stage[1], own.shape[1]), BF16),
        in_specs=[VMEM] * (1 + len(got)),
        out_specs=VMEM,
        compiler_params=limit(3),
        name="join",
    )(own, *got)


def swap(sends, stage):
    return [exchange(send, "coord", step << stage[0]) for step, send in enumerate(sends, 1)]


def after(first, second):
    return lax.optimization_barrier((first, second))[1]


def all_sums(halves, stages, ahead):
    owns = [half[0] for half in halves]
    sends = [half[1:] for half in halves]
    for stage, following in zip(stages, stages[1:] + [None], strict=True):
        got = [swap(send, stage) for send in sends]
        for i in range(len(owns)):
            own = after(owns[0], owns[i]) if i else owns[i]
            owns[i], *sends[i] = add_up(own, got[i], following)
    for stage in stages[:0:-1]:
        got = [swap([own] * (stage[1] - 1), stage) for own in owns]
        if stage is stages[1]:
            owns[0] = after(ahead, owns[0])
        for i in range(len(owns)):
            own = after(owns[0], owns[i]) if i else owns[i]
            owns[i] = join(own, got[i], stage)
    return [[own] + swap([own] * (stages[0][1] - 1), stages[0]) for own in owns]


def total_over(contrib, count):
    members = lax.axis_size("ckpt")
    chief = members - 1
    for other in range(chief):
        contrib = contrib + lax.ppermute(contrib, "ckpt", [(other, chief)])
    apart = 1
    while apart < count:
        pairs = [
            (source * members + chief, (source ^ apart) * members + chief)
            for source in range(count)
        ]
        contrib = contrib + lax.ppermute(contrib, ("coord", "ckpt"), pairs)
        apart *= 2
    for other in range(chief):
        got = lax.ppermute(contrib, "ckpt", [(chief, other)])
        contrib = jnp.where(lax.axis_index("ckpt") == other, got, contrib)
    return contrib


def turn_kernel(x, go, x_t, go_t):
    x_t[...] = x[...].T
    go_t[...] = go[...].T


def turn(x, go):
    shape = jax.ShapeDtypeStruct(x.shape[::-1], BF16)
    return pl.pallas_call(
        turn_kernel,
        out_shape=[shape, shape],
        in_specs=[VMEM, VMEM],
        out_specs=[VMEM, VMEM],
        compiler_params=limit(4),
        name="turn",
    )(x, go)


def butterflies(blocks):
    half = 1
    while half < len(blocks):
        done = list(blocks)
        for low in range(len(blocks)):
            if not low & half:
                a, b = blocks[low], blocks[low | half]
                if b is None:
                    done[low], done[low | half] = a, a
                else:
                    done[low], done[low | half] = a + b, a - b
        blocks, half = done, half * 2
    return blocks


def along_block(value, out, row):
    size = value.shape[0]
    tiles = butterflies([value[i : i + 8, :] for i in range(0, size, 8)])
    for i, tile in enumerate(tiles):
        out[row + 8 * i : row + 8 * i + 8, :] = tile
    for begin in range(row, row + size, 64):
        tiles = butterflies([out[pl.ds(begin + j, 8, stride=8), :] for j in range(8)])
        for j, tile in enumerate(tiles):
            out[begin + 8 * j : begin + 8 * j + 8, :] = tile


def signed(value, flags, row):
    return jnp.where(flags[row : row + value.shape[0], :] == 0, value, -value)


def keep(aligned, value, flags, row, out):
    value = signed(value, flags, row)
    if aligned:
        along_block(value, out, row)
    else:
        out[row : row + value.shape[0], :] = value


def wide_kernel(aligned, block, first, stage, *refs):
    parts, refs = refs[: stage[1]], refs[stage[1] :]
    gg, gu, h, flags, out, table = refs
    put_together(parts[0], parts[1:], stage, table)
    tokens = gg.shape[1]
    flags = flags.at[first : first + out.shape[0]]
    row = 0
    for slot, piece in enumerate((gg, gu, h)):
        product = table[slot * tokens : (slot + 1) * tokens, :]
        size = block if aligned else piece.shape[0]
        for begin in range(0, piece.shape[0], size):
            value = dot(piece[begin : begin + size, :], product, ((1,), (0,)))
            keep(aligned, value, flags, row, out)
            row += size


def wide(aligned, block, first, stage, parts, gg, gu, h, flags):
    rank = flags.shape[1]
    return pl.pallas_call(
        functools.partial(wide_kernel, aligned, block, first, stage),
        out_shape=jax.ShapeDtypeStruct((3 * gg.shape[0], rank), F32),
        in_specs=[VMEM] * (len(parts) + 4),
        out_specs=VMEM,
        scratch_shapes=[pltpu.VMEM((parts[0].shape[0] * stage[1], rank), BF16)],
        compiler_params=limit(6),
        cost_estimate=pl.CostEstimate(flops=10**9, bytes_accessed=10**7, transcendentals=0),
        name="wide",
    )(*parts, gg, gu, h, flags)


def rows_kernel(aligned, block, stage, *refs):
    parts, refs = refs[: stage[1]], refs[stage[1] :]
    x_t, go_t, wide_mix, flags, mix, table = refs
    width, tokens = x_t.shape
    first = 3 * width
    length, rank = mix.shape
    put_together(parts[0], parts[1:], stage, table)
    product = [
        jnp.concatenate(
            [table[slot * tokens + part : slot * tokens + part + rank, :] for part in range(0, tokens, rank)],
            axis=1,
        )
        for slot in range(3)
    ]
    size = block if aligned else width
    both = jnp.concatenate(product[:2], axis=0)
    for begin in range(0, width, size):
        value = dot(x_t[begin : begin + size, :], both, ((1,), (1,)))
        keep(aligned, value[:, :rank], flags, begin, mix)
        keep(aligned, value[:, rank:], flags, width + begin, mix)
        value = dot(go_t[begin : begin + size, :], product[2], ((1,), (1,)))
        keep(aligned, value, flags, 2 * width + begin, mix)
    filled = first + wide_mix.shape[0]
    if not aligned:
        mix[first:filled, :] = wide_mix[...]
        mix[filled:, :] = jnp.zeros((length - filled, rank), F32)
        for begin in range(0, length, block):
            along_block(mix[begin : begin + block, :], mix, begin)
    number = length // block
    full = -(-filled // block)

    def load(i, begin):
        if not aligned or i * block < first:
            return mix[pl.ds(i * block + begin, 8), :]
        if i >= full:
            return None
        return wide_mix[pl.ds(i * block - first + begin, 8), :]

    def across(step, _):
        begin = pl.multiple_of(step * 8, 8)
        for i, value in enumerate(butterflies([load(i, begin) for i in range(number)])):
            mix[pl.ds(i * block + begin, 8), :] = value
        return _

    if number > 1:
        lax.fori_loop(0, block // 8, across, 0, unroll=4)


def along_rows(aligned, block, stage, length, parts, x_t, go_t, wide_mix, flags):
    rank = flags.shape[1]
    return pl.pallas_call(
        functools.partial(rows_kernel, aligned, block, stage),
        out_shape=jax.ShapeDtypeStruct((length, rank), F32),
        in_specs=[VMEM] * (len(parts) + 4),
        out_specs=VMEM,
        scratch_shapes=[pltpu.VMEM((parts[0].shape[0] * stage[1], rank), BF16)],
        compiler_params=limit(6),
        name="along_rows",
    )(*parts, x_t, go_t, wide_mix, flags)


def parity(value):
    for fold in (16, 8, 4, 2, 1):
        value = value ^ (value >> fold)
    return value & 1


def sample_kernel(final_scale, mix, where, lanes, out, columns, *rows):
    length, _, rank = mix.shape
    samples = out.shape[1]
    group = rows[0].shape[0]
    number = samples // group
    ahead = 16
    shape = columns.shape
    column = lax.broadcasted_iota(jnp.int32, shape, 0) & lax.broadcasted_iota(jnp.int32, shape, 1)
    columns[...] = (1 - 2 * parity(column & (rank - 1))).astype(F32).astype(BF16)
    device = lax.axis_index("coord") * lax.axis_size("ckpt") + lax.axis_index("ckpt")
    bits = (length * rank).bit_length() - 1

    def pick(which, target):
        begin = which * group
        held = []
        for i in range(group):
            held.append(mix[where[begin + i]])
            if i >= ahead:
                target[i - ahead] = held[i - ahead]
        for i in range(group - ahead, group):
            target[i] = held[i]

    def transform(which, source):
        begin = pl.multiple_of(which * group, group)
        value = source.reshape(group, rank)[...]
        high = value.astype(BF16)
        low = (value - high.astype(F32)).astype(BF16)
        mixed = dot(columns[...], jnp.concatenate([high, low], axis=1), ((1,), (1,)))
        index = lanes[:, pl.ds(begin, group)]
        here = lax.broadcasted_iota(jnp.int32, mixed.shape, 0) == (index & (rank - 1))
        chosen = jnp.sum(jnp.where(here, mixed, 0.0), axis=0, keepdims=True)
        chosen = jnp.where(parity((index >> bits) & device) == 0, chosen, -chosen)
        out[:, pl.ds(begin, group)] = chosen * final_scale

    pick(0, rows[0])

    def step(turn_of, _):
        first = turn_of * 2
        transform(first, rows[0])
        pick(first + 1, rows[1])
        transform(first + 1, rows[1])
        pick(lax.rem(first + 2, number), rows[0])
        return _

    lax.fori_loop(0, number // 2, step, 0)


def sampled(final_scale, mix, where, index):
    samples, rank = index.shape[0], mix.shape[1]
    group = min(256, samples // 2)
    return pl.pallas_call(
        functools.partial(sample_kernel, final_scale),
        out_shape=jax.ShapeDtypeStruct((1, samples), F32),
        in_specs=[VMEM, SMEM, VMEM],
        out_specs=VMEM,
        scratch_shapes=[pltpu.VMEM((rank, 2 * rank), BF16)] + [pltpu.VMEM((group, 1, rank), F32)] * 2,
        compiler_params=limit(4),
        name="sampled",
    )(mix.reshape(-1, 1, rank), where, index.reshape(1, samples))


def shards(x, gg, gu, h, go, a_gate, b_gate, a_up, b_up, a_down, b_down, flags, index):
    x, go, gg, gu, h = [a[0, 0] for a in (x, go, gg, gu, h)]
    a_gate, b_gate, a_up, b_up, a_down, b_down = [
        a[0] for a in (a_gate, b_gate, a_up, b_up, a_down, b_down)
    ]
    count = lax.axis_size("coord")
    tokens, rank = x.shape[0], a_gate.shape[1]
    total = flags.shape[0] * count * lax.axis_size("ckpt")
    flags = flags.reshape(-1, rank)
    length = flags.shape[0]
    first = 3 * x.shape[1]
    block = min(256, length)
    aligned = x.shape[1] % block == 0 and gg.shape[0] % block == 0
    where = (index >> (rank.bit_length() - 1)) & (length - 1)
    where = (where & ~63) | (where & 7) << 3 | where >> 3 & 7
    stages = stages_of(count)
    rows = 16 * count * -(-3 * tokens // (16 * count))
    x, go, short = short_products(
        rows, stages[0], *[in_hbm(a) for a in (x, go, a_gate, a_up, b_down)]
    )
    gg, gu, h, long = long_products(
        rows, stages[0], *[in_hbm(a) for a in (gg, gu, h, b_gate, b_up, a_down)]
    )
    flags = after(long[0], flags)
    x_t, go_t = turn(x, go)
    short, long = all_sums([short, long], stages, go_t)
    wide_mix = wide(aligned, block, first, stages[0], short, gg, gu, h, flags)
    final_scale = adapter_scale * float(total) ** -0.5
    mix = along_rows(aligned, block, stages[0], length, long, x_t, go_t, wide_mix, flags)
    contrib = sampled(final_scale, mix, where, index)
    return total_over(contrib, count)


def solution(mesh):
    in_specs = (
        P("ckpt", "groups", None, "coord"),
        P("ckpt", "groups", "coord", None),
        P("ckpt", "groups", "coord", None),
        P("ckpt", "groups", "coord", None),
        P("ckpt", "groups", None, "coord"),
        P("ckpt", "coord", None),
        P("ckpt", "coord", None),
        P("ckpt", "coord", None),
        P("ckpt", "coord", None),
        P("ckpt", "coord", None),
        P("ckpt", "coord", None),
        P(("coord", "ckpt")),
        P(),
    )
    out_specs = P("groups", None)
    return jax.shard_map(shards, mesh=mesh, in_specs=in_specs, out_specs=out_specs, check_vma=False)
```

```python
import functools

import jax
import jax.numpy as jnp
from jax import lax
from jax.experimental import pallas as pl
from jax.experimental.pallas import tpu as pltpu
from jax.sharding import PartitionSpec as P

F32 = jnp.float32
BF16 = jnp.bfloat16
MIB = 2**20
adapter_scale = 2.0

ANY = pl.BlockSpec(memory_space=pl.ANY)
VMEM = pl.BlockSpec(memory_space=pltpu.VMEM)
SMEM = pl.BlockSpec(memory_space=pltpu.SMEM)


def limit(size):
    return pltpu.CompilerParams(vmem_limit_bytes=int(size * MIB))


def in_hbm(value):
    return pltpu.with_memory_space_constraint(value, pltpu.HBM)


def exchange(value, axis, apart):
    pairs = [(source, source ^ apart) for source in range(lax.axis_size(axis))]
    return lax.ppermute(value, axis, pairs)


def dot(left, right, contract):
    return lax.dot_general(left, right, (contract, ((), ())), preferred_element_type=F32)


def fetch(sources, targets, sems, cuts):
    groups = []
    slot = 0
    for source, target, cut in zip(sources, targets, cuts, strict=True):
        rows = source.shape[0]
        size = -(-rows // (cut * 16)) * 16
        group = []
        for begin in range(0, rows, size):
            end = min(begin + size, rows)
            copy = pltpu.make_async_copy(
                source.at[begin:end], target.at[begin:end], sems.at[slot]
            )
            copy.start()
            group.append(copy)
            slot += 1
        groups.append(group)

    def wait(which):
        for copy in groups[which]:
            copy.wait()

    return wait


def stages_of(count):
    stages, shift = [], 0
    while count > 1:
        radix = 2 if shift == 0 else min(4, count)
        stages.append((shift, radix))
        shift += radix.bit_length() - 1
        count //= radix
    return stages


def my_digit(stage):
    return (lax.axis_index("coord") >> stage[0]) & (stage[1] - 1)


def hand_out(table, stage, own, sends):
    digit = my_digit(stage)
    size = own.shape[0]
    own[...] = table[pl.ds(pl.multiple_of(digit * size, 16), size), :]
    for step, send in enumerate(sends, 1):
        begin = pl.multiple_of((digit ^ step) * size, 16)
        send[...] = table[pl.ds(begin, size), :].astype(BF16)


def put_together(own, others, stage, table):
    digit = my_digit(stage)
    size = own.shape[0]
    table[pl.ds(pl.multiple_of(digit * size, 16), size), :] = own[...]
    for step, other in enumerate(others, 1):
        table[pl.ds(pl.multiple_of((digit ^ step) * size, 16), size), :] = other[...]


def handed_out(rows, rank, stage):
    size = rows // stage[1]
    sends = [jax.ShapeDtypeStruct((size, rank), BF16)] * (stage[1] - 1)
    return [jax.ShapeDtypeStruct((size, rank), F32)] + sends


def fill(table, row):
    if table.shape[0] > row:
        table[row:, :] = jnp.zeros((table.shape[0] - row, table.shape[1]), F32)


def short_kernel(stage, cuts, *refs):
    ins, (x, go), (own, *sends), (a_gate, a_up, b_down, table, sems) = (
        refs[:5], refs[5:7], refs[7:-5], refs[-5:]
    )
    wait = fetch(ins, (x, go, a_gate, a_up, b_down), sems, cuts)
    for which in range(5):
        wait(which)
    tokens = x.shape[0]
    table[:tokens, :] = dot(x[...], a_gate[...], ((1,), (0,)))
    table[tokens : 2 * tokens, :] = dot(x[...], a_up[...], ((1,), (0,)))
    table[2 * tokens : 3 * tokens, :] = dot(go[...], b_down[...], ((1,), (0,)))
    fill(table, 3 * tokens)
    hand_out(table, stage, own, sends)


def short_products(rows, stage, *ins):
    rank = ins[2].shape[1]
    cuts = (2, 2, 1, 1, 1)
    shapes = [jax.ShapeDtypeStruct(a.shape, a.dtype) for a in ins[:2]]
    shapes = shapes + handed_out(rows, rank, stage)
    x, go, *sends = pl.pallas_call(
        functools.partial(short_kernel, stage, cuts),
        out_shape=shapes,
        in_specs=[ANY] * len(ins),
        out_specs=[VMEM] * len(shapes),
        scratch_shapes=[pltpu.VMEM(a.shape, a.dtype) for a in ins[2:]]
        + [pltpu.VMEM((rows, rank), F32), pltpu.SemaphoreType.DMA((sum(cuts),))],
        compiler_params=limit(4),
        cost_estimate=pl.CostEstimate(flops=10**8, bytes_accessed=6 * 10**6, transcendentals=0),
        name="short",
    )(*ins)
    return x, go, sends


def long_kernel(stage, cut, *refs):
    ins, held, (own, *sends), (*adapters, table, sems) = refs[:6], refs[6:9], refs[9:-5], refs[-5:]
    rank = table.shape[1]
    per = cut + 1
    waits = []

    def begin(slot):
        wait = fetch(
            (ins[3 + slot], ins[slot]),
            (adapters[slot], held[slot]),
            sems.at[slot * per : (slot + 1) * per],
            (1, cut),
        )
        waits.append(wait)

    begin(0)
    begin(1)
    row = 0
    for slot in range(3):
        waits[slot](0)
        adapter = adapters[slot][...].T
        waits[slot](1)
        if slot == 0:
            begin(2)
        value = dot(adapter, held[slot][...], ((1,), (0,)))
        for part in range(value.shape[1] // rank):
            table[row : row + rank, :] = value[:, part * rank : (part + 1) * rank]
            row += rank
    fill(table, row)
    hand_out(table, stage, own, sends)


def long_products(rows, stage, *ins):
    rank = ins[3].shape[1]
    cut = 4
    held = [jax.ShapeDtypeStruct(a.shape, a.dtype) for a in ins[:3]]
    shapes = held + handed_out(rows, rank, stage)
    outs = pl.pallas_call(
        functools.partial(long_kernel, stage, cut),
        out_shape=shapes,
        in_specs=[ANY] * 6,
        out_specs=[VMEM] * len(shapes),
        scratch_shapes=[pltpu.VMEM(a.shape, a.dtype) for a in ins[3:]]
        + [pltpu.VMEM((rows, rank), F32), pltpu.SemaphoreType.DMA((3 * (cut + 1),))],
        compiler_params=limit(6),
        cost_estimate=pl.CostEstimate(flops=10**9, bytes_accessed=8 * 10**6, transcendentals=0),
        name="long",
    )(*ins)
    return *outs[:3], outs[3:]


def add_kernel(following, count, *refs):
    total = refs[0][...]
    for got in refs[1 : 1 + count]:
        total = total + got[...].astype(F32)
    if following is None:
        refs[1 + count][...] = total.astype(BF16)
    else:
        outs, table = refs[1 + count : -1], refs[-1]
        table[...] = total
        hand_out(table, following, outs[0], outs[1:])


def add_up(own, got, following):
    if following is None:
        shapes, scratch = [jax.ShapeDtypeStruct(own.shape, BF16)], []
    else:
        shapes, scratch = handed_out(*own.shape, following), [pltpu.VMEM(own.shape, F32)]
    return pl.pallas_call(
        functools.partial(add_kernel, following, len(got)),
        out_shape=shapes,
        in_specs=[VMEM] * (1 + len(got)),
        out_specs=[VMEM] * len(shapes),
        scratch_shapes=scratch,
        compiler_params=limit(3),
        name="add_up",
    )(own, *got)


def join_kernel(stage, own, *refs):
    put_together(own, refs[:-1], stage, refs[-1])


def join(own, got, stage):
    return pl.pallas_call(
        functools.partial(join_kernel, stage),
        out_shape=jax.ShapeDtypeStruct((own.shape[0] * stage[1], own.shape[1]), BF16),
        in_specs=[VMEM] * (1 + len(got)),
        out_specs=VMEM,
        compiler_params=limit(3),
        name="join",
    )(own, *got)


def swap(sends, stage):
    return [exchange(send, "coord", step << stage[0]) for step, send in enumerate(sends, 1)]


def after(first, second):
    return lax.optimization_barrier((first, second))[1]


def all_sums(halves, stages, ahead):
    beside = []
    owns = [half[0] for half in halves]
    sends = [half[1:] for half in halves]
    for stage, following in zip(stages, stages[1:] + [None], strict=True):
        got = [swap(send, stage) for send in sends]
        for i in range(len(owns)):
            own = after(owns[0], owns[i]) if i else owns[i]
            owns[i], *sends[i] = add_up(own, got[i], following)
    for stage in stages[:0:-1]:
        got = [swap([own] * (stage[1] - 1), stage) for own in owns]
        for i in range(len(owns)):
            own = after(owns[0], owns[i]) if i else owns[i]
            if stage is stages[1]:
                beside.append(ahead[i](owns[0]))
                own = after(beside[i], own)
            owns[i] = join(own, got[i], stage)
    return beside, [[own] + swap([own] * (stages[0][1] - 1), stages[0]) for own in owns]


def total_over(contrib, count):
    members = lax.axis_size("ckpt")
    chief = members - 1
    for other in range(chief):
        contrib = contrib + lax.ppermute(contrib, "ckpt", [(other, chief)])
    apart = 1
    while apart < count:
        pairs = [
            (source * members + chief, (source ^ apart) * members + chief)
            for source in range(count)
        ]
        pairs += [(source,) * 2 for source in range(count * members) if source % members != chief]
        contrib = contrib + lax.ppermute(contrib, ("coord", "ckpt"), pairs)
        apart *= 2
    for other in range(chief):
        got = lax.ppermute(contrib, "ckpt", [(chief, other)])
        contrib = jnp.where(lax.axis_index("ckpt") == other, got, contrib)
    return contrib


def turn_kernel(x, go, x_t, go_t):
    x_t[...] = x[...].T
    go_t[...] = go[...].T


def turn(x, go):
    shape = jax.ShapeDtypeStruct(x.shape[::-1], BF16)
    return pl.pallas_call(
        turn_kernel,
        out_shape=[shape, shape],
        in_specs=[VMEM, VMEM],
        out_specs=[VMEM, VMEM],
        compiler_params=limit(4),
        name="turn",
    )(x, go)


def butterflies(blocks):
    half = 1
    while half < len(blocks):
        done = list(blocks)
        for low in range(len(blocks)):
            if not low & half:
                a, b = blocks[low], blocks[low | half]
                if b is None:
                    done[low], done[low | half] = a, a
                else:
                    done[low], done[low | half] = a + b, a - b
        blocks, half = done, half * 2
    return blocks


def along_block(value, out, row):
    size = value.shape[0]
    tiles = butterflies([value[i : i + 8, :] for i in range(0, size, 8)])
    for i, tile in enumerate(tiles):
        out[row + 8 * i : row + 8 * i + 8, :] = tile
    for begin in range(row, row + size, 64):
        tiles = butterflies([out[pl.ds(begin + j, 8, stride=8), :] for j in range(8)])
        for j, tile in enumerate(tiles):
            out[begin + 8 * j : begin + 8 * j + 8, :] = tile


def signed(value, flags, row):
    return jnp.where(flags[row : row + value.shape[0], :] == 0, value, -value)


def keep(aligned, value, flags, row, out):
    value = signed(value, flags, row)
    if aligned:
        along_block(value, out, row)
    else:
        out[row : row + value.shape[0], :] = value


def wide_kernel(aligned, block, first, stage, *refs):
    parts, refs = refs[: stage[1]], refs[stage[1] :]
    gg, gu, h, flags, out, table = refs
    put_together(parts[0], parts[1:], stage, table)
    tokens = gg.shape[1]
    flags = flags.at[first : first + out.shape[0]]
    row = 0
    for slot, piece in enumerate((gg, gu, h)):
        product = table[slot * tokens : (slot + 1) * tokens, :]
        size = block if aligned else piece.shape[0]
        for begin in range(0, piece.shape[0], size):
            value = dot(piece[begin : begin + size, :], product, ((1,), (0,)))
            keep(aligned, value, flags, row, out)
            row += size


def wide(aligned, block, first, stage, parts, gg, gu, h, flags):
    rank = flags.shape[1]
    return pl.pallas_call(
        functools.partial(wide_kernel, aligned, block, first, stage),
        out_shape=jax.ShapeDtypeStruct((3 * gg.shape[0], rank), F32),
        in_specs=[VMEM] * (len(parts) + 4),
        out_specs=VMEM,
        scratch_shapes=[pltpu.VMEM((parts[0].shape[0] * stage[1], rank), BF16)],
        compiler_params=limit(6),
        cost_estimate=pl.CostEstimate(flops=10**9, bytes_accessed=10**7, transcendentals=0),
        name="wide",
    )(*parts, gg, gu, h, flags)


def rows_kernel(aligned, block, stage, *refs):
    parts, refs = refs[: stage[1]], refs[stage[1] :]
    x_t, go_t, wide_mix, flags, mix, table = refs
    width, tokens = x_t.shape
    first = 3 * width
    length, rank = mix.shape
    put_together(parts[0], parts[1:], stage, table)
    product = [
        jnp.concatenate(
            [table[slot * tokens + part : slot * tokens + part + rank, :] for part in range(0, tokens, rank)],
            axis=1,
        )
        for slot in range(3)
    ]
    size = block if aligned else width
    both = jnp.concatenate(product[:2], axis=0)
    for begin in range(0, width, size):
        value = dot(x_t[begin : begin + size, :], both, ((1,), (1,)))
        keep(aligned, value[:, :rank], flags, begin, mix)
        keep(aligned, value[:, rank:], flags, width + begin, mix)
        value = dot(go_t[begin : begin + size, :], product[2], ((1,), (1,)))
        keep(aligned, value, flags, 2 * width + begin, mix)
    filled = first + wide_mix.shape[0]
    if not aligned:
        mix[first:filled, :] = wide_mix[...]
        mix[filled:, :] = jnp.zeros((length - filled, rank), F32)
        for begin in range(0, length, block):
            along_block(mix[begin : begin + block, :], mix, begin)
    number = length // block
    full = -(-filled // block)

    def load(i, begin):
        if not aligned or i * block < first:
            return mix[pl.ds(i * block + begin, 8), :]
        if i >= full:
            return None
        return wide_mix[pl.ds(i * block - first + begin, 8), :]

    def across(step, _):
        begin = pl.multiple_of(step * 8, 8)
        for i, value in enumerate(butterflies([load(i, begin) for i in range(number)])):
            mix[pl.ds(i * block + begin, 8), :] = value
        return _

    if number > 1:
        lax.fori_loop(0, block // 8, across, 0, unroll=4)


def along_rows(aligned, block, stage, length, parts, x_t, go_t, wide_mix, flags):
    rank = flags.shape[1]
    return pl.pallas_call(
        functools.partial(rows_kernel, aligned, block, stage),
        out_shape=jax.ShapeDtypeStruct((length, rank), F32),
        in_specs=[VMEM] * (len(parts) + 4),
        out_specs=VMEM,
        scratch_shapes=[pltpu.VMEM((parts[0].shape[0] * stage[1], rank), BF16)],
        compiler_params=limit(6),
        name="along_rows",
    )(*parts, x_t, go_t, wide_mix, flags)


def parity(value):
    for fold in (16, 8, 4, 2, 1):
        value = value ^ (value >> fold)
    return value & 1


def signs_kernel(bits, lanes, out):
    rank = out.shape[0]
    device = lax.axis_index("coord") * lax.axis_size("ckpt") + lax.axis_index("ckpt")
    index = lanes[...]

    def sign(bit):
        return (1 - 2 * (bit & 1)).astype(F32)

    low = lax.broadcasted_iota(jnp.int32, (8, index.shape[1]), 0)
    tile = sign(parity((index >> bits) & device))
    for bit in range(3):
        tile = tile * jnp.where((low >> bit & 1) == 0, 1.0, sign(index >> bit))
    tiles = [tile]
    for bit in range(3, rank.bit_length() - 1):
        tiles = tiles + [tile * sign(index >> bit) for tile in tiles]
    out[...] = jnp.concatenate(tiles, axis=0).astype(BF16)


def signs_of(rank, bits, index):
    samples = index.shape[0]
    return pl.pallas_call(
        functools.partial(signs_kernel, bits),
        out_shape=jax.ShapeDtypeStruct((rank, samples), BF16),
        in_specs=[VMEM],
        out_specs=VMEM,
        compiler_params=limit(10),
        name="signs",
    )(index.reshape(1, samples))


def sample_kernel(final_scale, mix, where, signs, out, rows):
    rank = mix.shape[2]
    samples = out.shape[1]
    unroll, ahead = min(256, samples), 16

    def pick(step, _):
        begin = step * unroll
        held = []
        for i in range(unroll):
            held.append(mix[where[begin + i]])
            if i >= ahead:
                rows[begin + i - ahead] = held[i - ahead]
        for i in range(unroll - ahead, unroll):
            rows[begin + i] = held[i]
        return _

    lax.fori_loop(0, samples // unroll, pick, 0)

    flat = rows.reshape(samples, rank)
    shape = (rank, rank)
    diagonal = lax.broadcasted_iota(jnp.int32, shape, 0) == lax.broadcasted_iota(jnp.int32, shape, 1)
    for begin in range(0, samples, rank):
        value = flat[begin : begin + rank, :]
        high = value.astype(BF16)
        low = (value - high.astype(F32)).astype(BF16)
        sign = signs[:, begin : begin + rank]
        mixed = dot(
            jnp.concatenate([high, low], axis=1), jnp.concatenate([sign, sign], axis=0), ((1,), (0,))
        )
        chosen = jnp.sum(jnp.where(diagonal, mixed, 0.0), axis=0, keepdims=True)
        out[:, begin : begin + rank] = chosen * final_scale


def sampled(final_scale, mix, where, signs):
    rank, samples = signs.shape
    return pl.pallas_call(
        functools.partial(sample_kernel, final_scale),
        out_shape=jax.ShapeDtypeStruct((1, samples), F32),
        in_specs=[VMEM, SMEM, VMEM],
        out_specs=VMEM,
        scratch_shapes=[pltpu.VMEM((samples, 1, rank), F32)],
        compiler_params=limit(8),
        name="sampled",
    )(mix.reshape(-1, 1, rank), where, signs)


def shards(x, gg, gu, h, go, a_gate, b_gate, a_up, b_up, a_down, b_down, flags, index):
    x, go, gg, gu, h = [a[0, 0] for a in (x, go, gg, gu, h)]
    a_gate, b_gate, a_up, b_up, a_down, b_down = [
        a[0] for a in (a_gate, b_gate, a_up, b_up, a_down, b_down)
    ]
    count = lax.axis_size("coord")
    tokens, rank = x.shape[0], a_gate.shape[1]
    total = flags.shape[0] * count * lax.axis_size("ckpt")
    flags = flags.reshape(-1, rank)
    length = flags.shape[0]
    first = 3 * x.shape[1]
    block = min(256, length)
    aligned = x.shape[1] % block == 0 and gg.shape[0] % block == 0
    where = (index >> (rank.bit_length() - 1)) & (length - 1)
    where = (where & ~63) | (where & 7) << 3 | where >> 3 & 7
    stages = stages_of(count)
    rows = 16 * count * -(-3 * tokens // (16 * count))
    x, go, short = short_products(
        rows, stages[0], *[in_hbm(a) for a in (x, go, a_gate, a_up, b_down)]
    )
    gg, gu, h, long = long_products(
        rows, stages[0], *[in_hbm(a) for a in (gg, gu, h, b_gate, b_up, a_down)]
    )
    flags = after(long[0], flags)
    bits = (length * rank).bit_length() - 1
    ahead = (
        lambda ready: turn(x, go),
        lambda ready: signs_of(rank, bits, after(ready, index)),
    )
    ((x_t, go_t), signs), (short, long) = all_sums([short, long], stages, ahead)
    wide_mix = wide(aligned, block, first, stages[0], short, gg, gu, h, flags)
    final_scale = adapter_scale * float(total) ** -0.5
    mix = along_rows(aligned, block, stages[0], length, long, x_t, go_t, wide_mix, flags)
    contrib = sampled(final_scale, mix, where, signs)
    return total_over(contrib, count)


def solution(mesh):
    in_specs = (
        P("ckpt", "groups", None, "coord"),
        P("ckpt", "groups", "coord", None),
        P("ckpt", "groups", "coord", None),
        P("ckpt", "groups", "coord", None),
        P("ckpt", "groups", None, "coord"),
        P("ckpt", "coord", None),
        P("ckpt", "coord", None),
        P("ckpt", "coord", None),
        P("ckpt", "coord", None),
        P("ckpt", "coord", None),
        P("ckpt", "coord", None),
        P(("coord", "ckpt")),
        P(),
    )
    out_specs = P("groups", None)
    return jax.shard_map(shards, mesh=mesh, in_specs=in_specs, out_specs=out_specs, check_vma=False)
```

```python
import functools

import jax
import jax.numpy as jnp
from jax import lax
from jax.experimental import pallas as pl
from jax.experimental.pallas import tpu as pltpu
from jax.sharding import PartitionSpec as P

F32 = jnp.float32
BF16 = jnp.bfloat16
MIB = 2**20
adapter_scale = 2.0

ANY = pl.BlockSpec(memory_space=pl.ANY)
VMEM = pl.BlockSpec(memory_space=pltpu.VMEM)
SMEM = pl.BlockSpec(memory_space=pltpu.SMEM)


def limit(size):
    return pltpu.CompilerParams(vmem_limit_bytes=int(size * MIB))


def in_hbm(value):
    return pltpu.with_memory_space_constraint(value, pltpu.HBM)


def exchange(value, axis, apart):
    pairs = [(source, source ^ apart) for source in range(lax.axis_size(axis))]
    return lax.ppermute(value, axis, pairs)


def dot(left, right, contract):
    return lax.dot_general(left, right, (contract, ((), ())), preferred_element_type=F32)


def fetch(sources, targets, sems, cuts):
    groups = []
    slot = 0
    for source, target, cut in zip(sources, targets, cuts, strict=True):
        rows = source.shape[0]
        size = -(-rows // (cut * 16)) * 16
        group = []
        for begin in range(0, rows, size):
            end = min(begin + size, rows)
            copy = pltpu.make_async_copy(
                source.at[begin:end], target.at[begin:end], sems.at[slot]
            )
            copy.start()
            group.append(copy)
            slot += 1
        groups.append(group)

    def wait(which):
        for copy in groups[which]:
            copy.wait()

    return wait


def stages_of(count):
    stages, shift = [], 0
    while count > 1:
        radix = 2 if shift == 0 else min(4, count)
        stages.append((shift, radix))
        shift += radix.bit_length() - 1
        count //= radix
    return stages


def my_digit(stage):
    return (lax.axis_index("coord") >> stage[0]) & (stage[1] - 1)


def hand_out(table, stage, own, sends):
    digit = my_digit(stage)
    size = own.shape[0]
    own[...] = table[pl.ds(pl.multiple_of(digit * size, 16), size), :]
    for step, send in enumerate(sends, 1):
        begin = pl.multiple_of((digit ^ step) * size, 16)
        send[...] = table[pl.ds(begin, size), :].astype(BF16)


def put_together(own, others, stage, table):
    digit = my_digit(stage)
    size = own.shape[0]
    table[pl.ds(pl.multiple_of(digit * size, 16), size), :] = own[...]
    for step, other in enumerate(others, 1):
        table[pl.ds(pl.multiple_of((digit ^ step) * size, 16), size), :] = other[...]


def handed_out(rows, rank, stage):
    size = rows // stage[1]
    sends = [jax.ShapeDtypeStruct((size, rank), BF16)] * (stage[1] - 1)
    return [jax.ShapeDtypeStruct((size, rank), F32)] + sends


def fill(table, row):
    if table.shape[0] > row:
        table[row:, :] = jnp.zeros((table.shape[0] - row, table.shape[1]), F32)


def short_kernel(stage, cuts, *refs):
    ins, (x, go), (own, *sends), (a_gate, a_up, b_down, table, sems) = (
        refs[:5], refs[5:7], refs[7:-5], refs[-5:]
    )
    wait = fetch(ins, (x, go, a_gate, a_up, b_down), sems, cuts)
    for which in range(5):
        wait(which)
    tokens = x.shape[0]
    table[:tokens, :] = dot(x[...], a_gate[...], ((1,), (0,)))
    table[tokens : 2 * tokens, :] = dot(x[...], a_up[...], ((1,), (0,)))
    table[2 * tokens : 3 * tokens, :] = dot(go[...], b_down[...], ((1,), (0,)))
    fill(table, 3 * tokens)
    hand_out(table, stage, own, sends)


def short_products(rows, stage, *ins):
    rank = ins[2].shape[1]
    cuts = (2, 2, 1, 1, 1)
    shapes = [jax.ShapeDtypeStruct(a.shape, a.dtype) for a in ins[:2]]
    shapes = shapes + handed_out(rows, rank, stage)
    x, go, *sends = pl.pallas_call(
        functools.partial(short_kernel, stage, cuts),
        out_shape=shapes,
        in_specs=[ANY] * len(ins),
        out_specs=[VMEM] * len(shapes),
        scratch_shapes=[pltpu.VMEM(a.shape, a.dtype) for a in ins[2:]]
        + [pltpu.VMEM((rows, rank), F32), pltpu.SemaphoreType.DMA((sum(cuts),))],
        compiler_params=limit(4),
        cost_estimate=pl.CostEstimate(flops=10**8, bytes_accessed=6 * 10**6, transcendentals=0),
        name="short",
    )(*ins)
    return x, go, sends


def long_kernel(stage, cut, *refs):
    ins, held, (own, *sends), (*adapters, table, sems) = refs[:6], refs[6:9], refs[9:-5], refs[-5:]
    rank = table.shape[1]
    per = cut + 1
    waits = []

    def begin(slot):
        wait = fetch(
            (ins[3 + slot], ins[slot]),
            (adapters[slot], held[slot]),
            sems.at[slot * per : (slot + 1) * per],
            (1, cut),
        )
        waits.append(wait)

    begin(0)
    begin(1)
    row = 0
    for slot in range(3):
        waits[slot](0)
        adapter = adapters[slot][...].T
        waits[slot](1)
        if slot == 0:
            begin(2)
        value = dot(adapter, held[slot][...], ((1,), (0,)))
        for part in range(value.shape[1] // rank):
            table[row : row + rank, :] = value[:, part * rank : (part + 1) * rank]
            row += rank
    fill(table, row)
    hand_out(table, stage, own, sends)


def long_products(rows, stage, *ins):
    rank = ins[3].shape[1]
    cut = 4
    held = [jax.ShapeDtypeStruct(a.shape, a.dtype) for a in ins[:3]]
    shapes = held + handed_out(rows, rank, stage)
    outs = pl.pallas_call(
        functools.partial(long_kernel, stage, cut),
        out_shape=shapes,
        in_specs=[ANY] * 6,
        out_specs=[VMEM] * len(shapes),
        scratch_shapes=[pltpu.VMEM(a.shape, a.dtype) for a in ins[3:]]
        + [pltpu.VMEM((rows, rank), F32), pltpu.SemaphoreType.DMA((3 * (cut + 1),))],
        compiler_params=limit(6),
        cost_estimate=pl.CostEstimate(flops=10**9, bytes_accessed=8 * 10**6, transcendentals=0),
        name="long",
    )(*ins)
    return *outs[:3], outs[3:]


def add_kernel(following, count, *refs):
    total = refs[0][...]
    for got in refs[1 : 1 + count]:
        total = total + got[...].astype(F32)
    if following is None:
        refs[1 + count][...] = total.astype(BF16)
    else:
        outs, table = refs[1 + count : -1], refs[-1]
        table[...] = total
        hand_out(table, following, outs[0], outs[1:])


def add_up(own, got, following):
    if following is None:
        shapes, scratch = [jax.ShapeDtypeStruct(own.shape, BF16)], []
    else:
        shapes, scratch = handed_out(*own.shape, following), [pltpu.VMEM(own.shape, F32)]
    return pl.pallas_call(
        functools.partial(add_kernel, following, len(got)),
        out_shape=shapes,
        in_specs=[VMEM] * (1 + len(got)),
        out_specs=[VMEM] * len(shapes),
        scratch_shapes=scratch,
        compiler_params=limit(3),
        name="add_up",
    )(own, *got)


def join_kernel(stage, own, *refs):
    put_together(own, refs[:-1], stage, refs[-1])


def join(own, got, stage):
    return pl.pallas_call(
        functools.partial(join_kernel, stage),
        out_shape=jax.ShapeDtypeStruct((own.shape[0] * stage[1], own.shape[1]), BF16),
        in_specs=[VMEM] * (1 + len(got)),
        out_specs=VMEM,
        compiler_params=limit(3),
        name="join",
    )(own, *got)


def swap(sends, stage):
    return [exchange(send, "coord", step << stage[0]) for step, send in enumerate(sends, 1)]


def after(first, second):
    return lax.optimization_barrier((first, second))[1]


def all_sums(halves, stages, ahead):
    beside = []
    owns = [half[0] for half in halves]
    sends = [half[1:] for half in halves]
    for stage, following in zip(stages, stages[1:] + [None], strict=True):
        got = [swap(send, stage) for send in sends]
        for i in range(len(owns)):
            own = after(owns[0], owns[i]) if i else owns[i]
            owns[i], *sends[i] = add_up(own, got[i], following)
    for stage in stages[:0:-1]:
        got = [swap([own] * (stage[1] - 1), stage) for own in owns]
        for i in range(len(owns)):
            own = after(owns[0], owns[i]) if i else owns[i]
            if stage is stages[1]:
                beside.append(ahead[i](owns[0]))
                own = after(beside[i], own)
            owns[i] = join(own, got[i], stage)
    return beside, [[own] + swap([own] * (stages[0][1] - 1), stages[0]) for own in owns]


def total_over(contrib, count):
    members = lax.axis_size("ckpt")
    contrib = contrib + exchange(contrib, "ckpt", 1)
    apart = 1
    while apart < count:
        flip = apart * members + 1
        pairs = [(source, source ^ flip) for source in range(count * members)]
        contrib = contrib + lax.ppermute(contrib, ("coord", "ckpt"), pairs)
        apart *= 2
    return contrib


def turn_kernel(x, go, x_t, go_t):
    x_t[...] = x[...].T
    go_t[...] = go[...].T


def turn(x, go):
    shape = jax.ShapeDtypeStruct(x.shape[::-1], BF16)
    return pl.pallas_call(
        turn_kernel,
        out_shape=[shape, shape],
        in_specs=[VMEM, VMEM],
        out_specs=[VMEM, VMEM],
        compiler_params=limit(4),
        name="turn",
    )(x, go)


def butterflies(blocks):
    half = 1
    while half < len(blocks):
        done = list(blocks)
        for low in range(len(blocks)):
            if not low & half:
                a, b = blocks[low], blocks[low | half]
                if b is None:
                    done[low], done[low | half] = a, a
                else:
                    done[low], done[low | half] = a + b, a - b
        blocks, half = done, half * 2
    return blocks


def along_block(value, out, row):
    size = value.shape[0]
    tiles = butterflies([value[i : i + 8, :] for i in range(0, size, 8)])
    for i, tile in enumerate(tiles):
        out[row + 8 * i : row + 8 * i + 8, :] = tile
    for begin in range(row, row + size, 64):
        tiles = butterflies([out[pl.ds(begin + j, 8, stride=8), :] for j in range(8)])
        for j, tile in enumerate(tiles):
            out[begin + 8 * j : begin + 8 * j + 8, :] = tile


def signed(value, flags, row):
    return jnp.where(flags[row : row + value.shape[0], :] == 0, value, -value)


def keep(aligned, value, flags, row, out):
    value = signed(value, flags, row)
    if aligned:
        along_block(value, out, row)
    else:
        out[row : row + value.shape[0], :] = value


def wide_kernel(aligned, block, first, stage, *refs):
    parts, refs = refs[: stage[1]], refs[stage[1] :]
    gg, gu, h, flags, out, table = refs
    put_together(parts[0], parts[1:], stage, table)
    tokens = gg.shape[1]
    flags = flags.at[first : first + out.shape[0]]
    row = 0
    for slot, piece in enumerate((gg, gu, h)):
        product = table[slot * tokens : (slot + 1) * tokens, :]
        size = block if aligned else piece.shape[0]
        for begin in range(0, piece.shape[0], size):
            value = dot(piece[begin : begin + size, :], product, ((1,), (0,)))
            keep(aligned, value, flags, row, out)
            row += size


def wide(aligned, block, first, stage, parts, gg, gu, h, flags):
    rank = flags.shape[1]
    return pl.pallas_call(
        functools.partial(wide_kernel, aligned, block, first, stage),
        out_shape=jax.ShapeDtypeStruct((3 * gg.shape[0], rank), F32),
        in_specs=[VMEM] * (len(parts) + 4),
        out_specs=VMEM,
        scratch_shapes=[pltpu.VMEM((parts[0].shape[0] * stage[1], rank), BF16)],
        compiler_params=limit(6),
        cost_estimate=pl.CostEstimate(flops=10**9, bytes_accessed=10**7, transcendentals=0),
        name="wide",
    )(*parts, gg, gu, h, flags)


def rows_kernel(aligned, block, stage, *refs):
    parts, refs = refs[: stage[1]], refs[stage[1] :]
    x_t, go_t, wide_mix, flags, mix, table = refs
    width, tokens = x_t.shape
    first = 3 * width
    length, rank = mix.shape
    put_together(parts[0], parts[1:], stage, table)
    product = [
        jnp.concatenate(
            [table[slot * tokens + part : slot * tokens + part + rank, :] for part in range(0, tokens, rank)],
            axis=1,
        )
        for slot in range(3)
    ]
    size = block if aligned else width
    both = jnp.concatenate(product[:2], axis=0)
    for begin in range(0, width, size):
        value = dot(x_t[begin : begin + size, :], both, ((1,), (1,)))
        keep(aligned, value[:, :rank], flags, begin, mix)
        keep(aligned, value[:, rank:], flags, width + begin, mix)
        value = dot(go_t[begin : begin + size, :], product[2], ((1,), (1,)))
        keep(aligned, value, flags, 2 * width + begin, mix)
    filled = first + wide_mix.shape[0]
    if not aligned:
        mix[first:filled, :] = wide_mix[...]
        mix[filled:, :] = jnp.zeros((length - filled, rank), F32)
        for begin in range(0, length, block):
            along_block(mix[begin : begin + block, :], mix, begin)
    number = length // block
    full = -(-filled // block)

    def load(i, begin):
        if not aligned or i * block < first:
            return mix[pl.ds(i * block + begin, 8), :]
        if i >= full:
            return None
        return wide_mix[pl.ds(i * block - first + begin, 8), :]

    def across(step, _):
        begin = pl.multiple_of(step * 8, 8)
        for i, value in enumerate(butterflies([load(i, begin) for i in range(number)])):
            mix[pl.ds(i * block + begin, 8), :] = value
        return _

    if number > 1:
        lax.fori_loop(0, block // 8, across, 0, unroll=4)


def along_rows(aligned, block, stage, length, parts, x_t, go_t, wide_mix, flags):
    rank = flags.shape[1]
    return pl.pallas_call(
        functools.partial(rows_kernel, aligned, block, stage),
        out_shape=jax.ShapeDtypeStruct((length, rank), F32),
        in_specs=[VMEM] * (len(parts) + 4),
        out_specs=VMEM,
        scratch_shapes=[pltpu.VMEM((parts[0].shape[0] * stage[1], rank), BF16)],
        compiler_params=limit(6),
        name="along_rows",
    )(*parts, x_t, go_t, wide_mix, flags)


def parity(value):
    for fold in (16, 8, 4, 2, 1):
        value = value ^ (value >> fold)
    return value & 1


def signs_kernel(bits, lanes, out):
    rank = out.shape[0]
    device = lax.axis_index("coord") * lax.axis_size("ckpt") + lax.axis_index("ckpt")
    index = lanes[...]

    def sign(bit):
        return (1 - 2 * (bit & 1)).astype(F32)

    low = lax.broadcasted_iota(jnp.int32, (8, index.shape[1]), 0)
    tile = sign(parity((index >> bits) & device))
    for bit in range(3):
        tile = tile * jnp.where((low >> bit & 1) == 0, 1.0, sign(index >> bit))
    tiles = [tile]
    for bit in range(3, rank.bit_length() - 1):
        tiles = tiles + [tile * sign(index >> bit) for tile in tiles]
    out[...] = jnp.concatenate(tiles, axis=0).astype(BF16)


def signs_of(rank, bits, index):
    samples = index.shape[0]
    return pl.pallas_call(
        functools.partial(signs_kernel, bits),
        out_shape=jax.ShapeDtypeStruct((rank, samples), BF16),
        in_specs=[VMEM],
        out_specs=VMEM,
        compiler_params=limit(10),
        name="signs",
    )(index.reshape(1, samples))


def sample_kernel(final_scale, unroll, mix, where, signs, out):
    rank = mix.shape[1]
    samples = out.shape[1]
    shape = (rank, rank)
    diagonal = lax.broadcasted_iota(jnp.int32, shape, 0) == lax.broadcasted_iota(jnp.int32, shape, 1)
    place = lax.broadcasted_iota(jnp.int32, (8, rank), 0)
    masks = [place == i for i in range(8)]

    def picked(begin):
        tile = None
        for i in range(8):
            row = jnp.broadcast_to(mix[pl.ds(where[begin + i], 1), :], (8, rank))
            tile = row if tile is None else jnp.where(masks[i], row, tile)
        return tile

    def step(which, _):
        for part in range(unroll):
            begin = pl.multiple_of((which * unroll + part) * rank, rank)
            value = jnp.concatenate([picked(begin + i) for i in range(0, rank, 8)], axis=0)
            high = value.astype(BF16)
            low = (value - high.astype(F32)).astype(BF16)
            sign = signs[:, pl.ds(begin, rank)]
            mixed = dot(
                jnp.concatenate([high, low], axis=1), jnp.concatenate([sign, sign], axis=0), ((1,), (0,))
            )
            chosen = jnp.sum(jnp.where(diagonal, mixed, 0.0), axis=0, keepdims=True)
            out[:, pl.ds(begin, rank)] = chosen * final_scale
        return _

    lax.fori_loop(0, samples // (rank * unroll), step, 0)


def sampled(final_scale, mix, where, signs):
    rank, samples = signs.shape
    unroll = min(4, samples // rank)
    return pl.pallas_call(
        functools.partial(sample_kernel, final_scale, unroll),
        out_shape=jax.ShapeDtypeStruct((1, samples), F32),
        in_specs=[VMEM, SMEM, VMEM],
        out_specs=VMEM,
        compiler_params=limit(4),
        name="sampled",
    )(mix, where, signs)


def shards(x, gg, gu, h, go, a_gate, b_gate, a_up, b_up, a_down, b_down, flags, index):
    x, go, gg, gu, h = [a[0, 0] for a in (x, go, gg, gu, h)]
    a_gate, b_gate, a_up, b_up, a_down, b_down = [
        a[0] for a in (a_gate, b_gate, a_up, b_up, a_down, b_down)
    ]
    count = lax.axis_size("coord")
    tokens, rank = x.shape[0], a_gate.shape[1]
    total = flags.shape[0] * count * lax.axis_size("ckpt")
    flags = flags.reshape(-1, rank)
    length = flags.shape[0]
    first = 3 * x.shape[1]
    block = min(256, length)
    aligned = x.shape[1] % block == 0 and gg.shape[0] % block == 0
    where = (index >> (rank.bit_length() - 1)) & (length - 1)
    where = (where & ~63) | (where & 7) << 3 | where >> 3 & 7
    stages = stages_of(count)
    rows = 16 * count * -(-3 * tokens // (16 * count))
    x, go, short = short_products(
        rows, stages[0], *[in_hbm(a) for a in (x, go, a_gate, a_up, b_down)]
    )
    gg, gu, h, long = long_products(
        rows, stages[0], *[in_hbm(a) for a in (gg, gu, h, b_gate, b_up, a_down)]
    )
    flags = after(long[0], flags)
    bits = (length * rank).bit_length() - 1
    ahead = (
        lambda ready: turn(x, go),
        lambda ready: signs_of(rank, bits, after(ready, index)),
    )
    ((x_t, go_t), signs), (short, long) = all_sums([short, long], stages, ahead)
    wide_mix = wide(aligned, block, first, stages[0], short, gg, gu, h, flags)
    final_scale = adapter_scale * float(total) ** -0.5
    mix = along_rows(aligned, block, stages[0], length, long, x_t, go_t, wide_mix, flags)
    contrib = sampled(final_scale, mix, where, signs)
    return total_over(contrib, count)


def solution(mesh):
    in_specs = (
        P("ckpt", "groups", None, "coord"),
        P("ckpt", "groups", "coord", None),
        P("ckpt", "groups", "coord", None),
        P("ckpt", "groups", "coord", None),
        P("ckpt", "groups", None, "coord"),
        P("ckpt", "coord", None),
        P("ckpt", "coord", None),
        P("ckpt", "coord", None),
        P("ckpt", "coord", None),
        P("ckpt", "coord", None),
        P("ckpt", "coord", None),
        P(("coord", "ckpt")),
        P(),
    )
    out_specs = P("groups", None)
    return jax.shard_map(shards, mesh=mesh, in_specs=in_specs, out_specs=out_specs, check_vma=False)
```

```python
import functools

import jax
import jax.numpy as jnp
from jax import lax
from jax.experimental import pallas as pl
from jax.experimental.pallas import tpu as pltpu
from jax.sharding import PartitionSpec as P

F32 = jnp.float32
BF16 = jnp.bfloat16
MIB = 2**20
adapter_scale = 2.0

ANY = pl.BlockSpec(memory_space=pl.ANY)
VMEM = pl.BlockSpec(memory_space=pltpu.VMEM)
SMEM = pl.BlockSpec(memory_space=pltpu.SMEM)


def limit(size):
    return pltpu.CompilerParams(vmem_limit_bytes=int(size * MIB))


def in_hbm(value):
    return pltpu.with_memory_space_constraint(value, pltpu.HBM)


def exchange(value, axis, apart):
    pairs = [(source, source ^ apart) for source in range(lax.axis_size(axis))]
    return lax.ppermute(value, axis, pairs)


def dot(left, right, contract):
    return lax.dot_general(left, right, (contract, ((), ())), preferred_element_type=F32)


def fetch(sources, targets, sems, cuts):
    groups = []
    slot = 0
    for source, target, cut in zip(sources, targets, cuts, strict=True):
        rows = source.shape[0]
        size = -(-rows // (cut * 16)) * 16
        group = []
        for begin in range(0, rows, size):
            end = min(begin + size, rows)
            copy = pltpu.make_async_copy(
                source.at[begin:end], target.at[begin:end], sems.at[slot]
            )
            copy.start()
            group.append(copy)
            slot += 1
        groups.append(group)

    def wait(which):
        for copy in groups[which]:
            copy.wait()

    return wait


def stages_of(count):
    stages, shift = [], 0
    while count > 1:
        radix = 2 if shift == 0 else min(4, count)
        stages.append((shift, radix))
        shift += radix.bit_length() - 1
        count //= radix
    return stages


def my_digit(stage):
    return (lax.axis_index("coord") >> stage[0]) & (stage[1] - 1)


def hand_out(table, stage, own, sends):
    digit = my_digit(stage)
    size = own.shape[0]
    own[...] = table[pl.ds(pl.multiple_of(digit * size, 16), size), :]
    for step, send in enumerate(sends, 1):
        begin = pl.multiple_of((digit ^ step) * size, 16)
        send[...] = table[pl.ds(begin, size), :].astype(BF16)


def put_together(own, others, stage, table):
    digit = my_digit(stage)
    size = own.shape[0]
    table[pl.ds(pl.multiple_of(digit * size, 16), size), :] = own[...]
    for step, other in enumerate(others[::-1], 1):
        table[pl.ds(pl.multiple_of((digit ^ step) * size, 16), size), :] = other[...]


def handed_out(rows, rank, stage):
    size = rows // stage[1]
    sends = [jax.ShapeDtypeStruct((size, rank), BF16)] * (stage[1] - 1)
    return [jax.ShapeDtypeStruct((size, rank), F32)] + sends


def fill(table, row):
    if table.shape[0] > row:
        table[row:, :] = jnp.zeros((table.shape[0] - row, table.shape[1]), F32)


def short_kernel(stage, cuts, *refs):
    ins, (x, go), (own, *sends), (a_gate, a_up, b_down, table, sems) = (
        refs[:5], refs[5:7], refs[7:-5], refs[-5:]
    )
    wait = fetch(ins, (x, go, a_gate, a_up, b_down), sems, cuts)
    for which in range(5):
        wait(which)
    tokens = x.shape[0]
    table[:tokens, :] = dot(x[...], a_gate[...], ((1,), (0,)))
    table[tokens : 2 * tokens, :] = dot(x[...], a_up[...], ((1,), (0,)))
    table[2 * tokens : 3 * tokens, :] = dot(go[...], b_down[...], ((1,), (0,)))
    fill(table, 3 * tokens)
    hand_out(table, stage, own, sends)


def short_products(rows, stage, *ins):
    rank = ins[2].shape[1]
    cuts = (2, 2, 1, 1, 1)
    shapes = [jax.ShapeDtypeStruct(a.shape, a.dtype) for a in ins[:2]]
    shapes = shapes + handed_out(rows, rank, stage)
    x, go, *sends = pl.pallas_call(
        functools.partial(short_kernel, stage, cuts),
        out_shape=shapes,
        in_specs=[ANY] * len(ins),
        out_specs=[VMEM] * len(shapes),
        scratch_shapes=[pltpu.VMEM(a.shape, a.dtype) for a in ins[2:]]
        + [pltpu.VMEM((rows, rank), F32), pltpu.SemaphoreType.DMA((sum(cuts),))],
        compiler_params=limit(4),
        cost_estimate=pl.CostEstimate(flops=10**8, bytes_accessed=6 * 10**6, transcendentals=0),
        name="short",
    )(*ins)
    return x, go, sends


def long_kernel(stage, size, *refs):
    ins, held, (own, *sends), (*adapters, table, sems) = refs[:6], refs[6:9], refs[9:-5], refs[-5:]
    rank = table.shape[1]
    spans = [(i, min(i + size, ins[0].shape[0])) for i in range(0, ins[0].shape[0], size)]
    copies = {}

    def begin(slot):
        for part, (first, last) in enumerate(spans):
            pair = []
            for kind, (source, target) in enumerate(
                ((ins[3 + slot], adapters[slot]), (ins[slot], held[slot]))
            ):
                copy = pltpu.make_async_copy(
                    source.at[first:last], target.at[first:last], sems.at[slot, part, kind]
                )
                copy.start()
                pair.append(copy)
            copies[slot, part] = pair

    begin(0)
    begin(1)
    row = 0
    for slot in range(3):
        value = None
        for part, (first, last) in enumerate(spans):
            for copy in copies[slot, part]:
                copy.wait()
            term = dot(adapters[slot][first:last, :].T, held[slot][first:last, :], ((1,), (0,)))
            value = term if value is None else value + term
        if slot == 0:
            begin(2)
        for part in range(value.shape[1] // rank):
            table[row : row + rank, :] = value[:, part * rank : (part + 1) * rank]
            row += rank
    fill(table, row)
    hand_out(table, stage, own, sends)


def long_products(rows, stage, *ins):
    rank = ins[3].shape[1]
    size = min(512, ins[0].shape[0])
    held = [jax.ShapeDtypeStruct(a.shape, a.dtype) for a in ins[:3]]
    shapes = held + handed_out(rows, rank, stage)
    outs = pl.pallas_call(
        functools.partial(long_kernel, stage, size),
        out_shape=shapes,
        in_specs=[ANY] * 6,
        out_specs=[VMEM] * len(shapes),
        scratch_shapes=[pltpu.VMEM(a.shape, a.dtype) for a in ins[3:]]
        + [
            pltpu.VMEM((rows, rank), F32),
            pltpu.SemaphoreType.DMA((3, -(-ins[0].shape[0] // size), 2)),
        ],
        compiler_params=limit(6),
        cost_estimate=pl.CostEstimate(flops=10**9, bytes_accessed=8 * 10**6, transcendentals=0),
        name="long",
    )(*ins)
    return *outs[:3], outs[3:]


def add_kernel(following, count, *refs):
    total = refs[0][...]
    for got in refs[1 : 1 + count]:
        total = total + got[...].astype(F32)
    if following is None:
        refs[1 + count][...] = total.astype(BF16)
    else:
        outs, table = refs[1 + count : -1], refs[-1]
        table[...] = total
        hand_out(table, following, outs[0], outs[1:])


def add_up(own, got, following):
    if following is None:
        shapes, scratch = [jax.ShapeDtypeStruct(own.shape, BF16)], []
    else:
        shapes, scratch = handed_out(*own.shape, following), [pltpu.VMEM(own.shape, F32)]
    return pl.pallas_call(
        functools.partial(add_kernel, following, len(got)),
        out_shape=shapes,
        in_specs=[VMEM] * (1 + len(got)),
        out_specs=[VMEM] * len(shapes),
        scratch_shapes=scratch,
        compiler_params=limit(3),
        name="add_up",
    )(own, *got)


def join_kernel(stage, own, *refs):
    put_together(own, refs[:-1], stage, refs[-1])


def join(own, got, stage):
    return pl.pallas_call(
        functools.partial(join_kernel, stage),
        out_shape=jax.ShapeDtypeStruct((own.shape[0] * stage[1], own.shape[1]), BF16),
        in_specs=[VMEM] * (1 + len(got)),
        out_specs=VMEM,
        compiler_params=limit(3),
        name="join",
    )(own, *got)


def swap(sends, stage):
    return [
        exchange(sends[step - 1], "coord", step << stage[0]) for step in range(stage[1] - 1, 0, -1)
    ]


def after(first, second):
    return lax.optimization_barrier((first, second))[1]


def all_sums(halves, stages, ahead):
    beside = []
    owns = [half[0] for half in halves]
    sends = [half[1:] for half in halves]
    for stage, following in zip(stages, stages[1:] + [None], strict=True):
        got = [swap(send, stage) for send in sends]
        for i in range(len(owns)):
            own = after(owns[0], owns[i]) if i else owns[i]
            owns[i], *sends[i] = add_up(own, got[i], following)
    for stage in stages[:0:-1]:
        got = [swap([own] * (stage[1] - 1), stage) for own in owns]
        for i in range(len(owns)):
            own = after(owns[0], owns[i]) if i else owns[i]
            if stage is stages[1]:
                beside.append(ahead[i](owns[0]))
                own = after(beside[i], own)
            owns[i] = join(own, got[i], stage)
    return beside, [[own] + swap([own] * (stages[0][1] - 1), stages[0]) for own in owns]


def total_over(contrib, count):
    members = lax.axis_size("ckpt")
    contrib = contrib + exchange(contrib, "ckpt", 1)
    apart = 1
    while apart < count:
        flip = apart * members + 1
        pairs = [(source, source ^ flip) for source in range(count * members)]
        contrib = contrib + lax.ppermute(contrib, ("coord", "ckpt"), pairs)
        apart *= 2
    return contrib


def turn_kernel(x, go, x_t, go_t):
    x_t[...] = x[...].T
    go_t[...] = go[...].T


def turn(x, go):
    shape = jax.ShapeDtypeStruct(x.shape[::-1], BF16)
    return pl.pallas_call(
        turn_kernel,
        out_shape=[shape, shape],
        in_specs=[VMEM, VMEM],
        out_specs=[VMEM, VMEM],
        compiler_params=limit(4),
        name="turn",
    )(x, go)


def butterflies(blocks):
    half = 1
    while half < len(blocks):
        done = list(blocks)
        for low in range(len(blocks)):
            if not low & half:
                a, b = blocks[low], blocks[low | half]
                if b is None:
                    done[low], done[low | half] = a, a
                else:
                    done[low], done[low | half] = a + b, a - b
        blocks, half = done, half * 2
    return blocks


def along_block(value, out, row):
    size = value.shape[0]
    tiles = butterflies([value[i : i + 8, :] for i in range(0, size, 8)])
    for i, tile in enumerate(tiles):
        out[row + 8 * i : row + 8 * i + 8, :] = tile
    for begin in range(row, row + size, 64):
        tiles = butterflies([out[pl.ds(begin + j, 8, stride=8), :] for j in range(8)])
        for j, tile in enumerate(tiles):
            out[begin + 8 * j : begin + 8 * j + 8, :] = tile


def signed(value, flags, row):
    return jnp.where(flags[row : row + value.shape[0], :] == 0, value, -value)


def keep(aligned, value, flags, row, out):
    value = signed(value, flags, row)
    if aligned:
        along_block(value, out, row)
    else:
        out[row : row + value.shape[0], :] = value


def wide_kernel(aligned, block, first, stage, *refs):
    parts, refs = refs[: stage[1]], refs[stage[1] :]
    gg, gu, h, flags, out, table = refs
    put_together(parts[0], parts[1:], stage, table)
    tokens = gg.shape[1]
    flags = flags.at[first : first + out.shape[0]]
    row = 0
    for slot, piece in enumerate((gg, gu, h)):
        product = table[slot * tokens : (slot + 1) * tokens, :]
        size = block if aligned else piece.shape[0]
        for begin in range(0, piece.shape[0], size):
            value = dot(piece[begin : begin + size, :], product, ((1,), (0,)))
            keep(aligned, value, flags, row, out)
            row += size


def wide(aligned, block, first, stage, parts, gg, gu, h, flags):
    rank = flags.shape[1]
    return pl.pallas_call(
        functools.partial(wide_kernel, aligned, block, first, stage),
        out_shape=jax.ShapeDtypeStruct((3 * gg.shape[0], rank), F32),
        in_specs=[VMEM] * (len(parts) + 4),
        out_specs=VMEM,
        scratch_shapes=[pltpu.VMEM((parts[0].shape[0] * stage[1], rank), BF16)],
        compiler_params=limit(6),
        cost_estimate=pl.CostEstimate(flops=10**9, bytes_accessed=10**7, transcendentals=0),
        name="wide",
    )(*parts, gg, gu, h, flags)


def rows_kernel(aligned, block, stage, *refs):
    parts, refs = refs[: stage[1]], refs[stage[1] :]
    x_t, go_t, wide_mix, flags, mix, table = refs
    width, tokens = x_t.shape
    first = 3 * width
    length, rank = mix.shape
    put_together(parts[0], parts[1:], stage, table)
    product = [
        jnp.concatenate(
            [table[slot * tokens + part : slot * tokens + part + rank, :] for part in range(0, tokens, rank)],
            axis=1,
        )
        for slot in range(3)
    ]
    size = block if aligned else width
    both = jnp.concatenate(product[:2], axis=0)
    for begin in range(0, width, size):
        value = dot(x_t[begin : begin + size, :], both, ((1,), (1,)))
        keep(aligned, value[:, :rank], flags, begin, mix)
        keep(aligned, value[:, rank:], flags, width + begin, mix)
        value = dot(go_t[begin : begin + size, :], product[2], ((1,), (1,)))
        keep(aligned, value, flags, 2 * width + begin, mix)
    filled = first + wide_mix.shape[0]
    if not aligned:
        mix[first:filled, :] = wide_mix[...]
        mix[filled:, :] = jnp.zeros((length - filled, rank), F32)
        for begin in range(0, length, block):
            along_block(mix[begin : begin + block, :], mix, begin)
    number = length // block
    full = -(-filled // block)

    def load(i, begin):
        if not aligned or i * block < first:
            return mix[pl.ds(i * block + begin, 8), :]
        if i >= full:
            return None
        return wide_mix[pl.ds(i * block - first + begin, 8), :]

    def across(step, _):
        begin = pl.multiple_of(step * 8, 8)
        for i, value in enumerate(butterflies([load(i, begin) for i in range(number)])):
            mix[pl.ds(i * block + begin, 8), :] = value
        return _

    if number > 1:
        lax.fori_loop(0, block // 8, across, 0, unroll=4)


def along_rows(aligned, block, stage, length, parts, x_t, go_t, wide_mix, flags):
    rank = flags.shape[1]
    return pl.pallas_call(
        functools.partial(rows_kernel, aligned, block, stage),
        out_shape=jax.ShapeDtypeStruct((length, rank), F32),
        in_specs=[VMEM] * (len(parts) + 4),
        out_specs=VMEM,
        scratch_shapes=[pltpu.VMEM((parts[0].shape[0] * stage[1], rank), BF16)],
        compiler_params=limit(6),
        name="along_rows",
    )(*parts, x_t, go_t, wide_mix, flags)


def parity(value):
    for fold in (16, 8, 4, 2, 1):
        value = value ^ (value >> fold)
    return value & 1


def signs_kernel(bits, lanes, out):
    rank = out.shape[0]
    device = lax.axis_index("coord") * lax.axis_size("ckpt") + lax.axis_index("ckpt")
    index = lanes[...]

    def sign(bit):
        return (1 - 2 * (bit & 1)).astype(F32)

    low = lax.broadcasted_iota(jnp.int32, (8, index.shape[1]), 0)
    tile = sign(parity((index >> bits) & device))
    for bit in range(3):
        tile = tile * jnp.where((low >> bit & 1) == 0, 1.0, sign(index >> bit))
    tiles = [tile]
    for bit in range(3, rank.bit_length() - 1):
        tiles = tiles + [tile * sign(index >> bit) for tile in tiles]
    out[...] = jnp.concatenate(tiles, axis=0).astype(BF16)


def signs_of(rank, bits, index):
    samples = index.shape[0]
    return pl.pallas_call(
        functools.partial(signs_kernel, bits),
        out_shape=jax.ShapeDtypeStruct((rank, samples), BF16),
        in_specs=[VMEM],
        out_specs=VMEM,
        compiler_params=limit(10),
        name="signs",
    )(index.reshape(1, samples))


def pick_kernel(mix, where, rows):
    samples = rows.shape[0]
    unroll, ahead = min(256, samples), 16

    def pick(step, _):
        begin = step * unroll
        held = []
        for i in range(unroll):
            held.append(mix[where[begin + i]])
            if i >= ahead:
                rows[begin + i - ahead] = held[i - ahead]
        for i in range(unroll - ahead, unroll):
            rows[begin + i] = held[i]
        return _

    lax.fori_loop(0, samples // unroll, pick, 0)


def picked(mix, where):
    rank, samples = mix.shape[1], where.shape[0]
    rows = pl.pallas_call(
        pick_kernel,
        out_shape=jax.ShapeDtypeStruct((samples, 1, rank), F32),
        in_specs=[VMEM, SMEM],
        out_specs=VMEM,
        compiler_params=limit(4),
        name="picked",
    )(mix.reshape(-1, 1, rank), where)
    return rows.reshape(samples, rank)


def sample_kernel(final_scale, rows, signs, out):
    samples, rank = rows.shape
    shape = (rank, rank)
    diagonal = lax.broadcasted_iota(jnp.int32, shape, 0) == lax.broadcasted_iota(jnp.int32, shape, 1)
    for begin in range(0, samples, rank):
        value = rows[begin : begin + rank, :]
        high = value.astype(BF16)
        low = (value - high.astype(F32)).astype(BF16)
        sign = signs[:, begin : begin + rank]
        mixed = dot(
            jnp.concatenate([high, low], axis=1), jnp.concatenate([sign, sign], axis=0), ((1,), (0,))
        )
        chosen = jnp.sum(jnp.where(diagonal, mixed, 0.0), axis=0, keepdims=True)
        out[:, begin : begin + rank] = chosen * final_scale


def sampled(final_scale, rows, signs):
    return pl.pallas_call(
        functools.partial(sample_kernel, final_scale),
        out_shape=jax.ShapeDtypeStruct((1, rows.shape[0]), F32),
        in_specs=[VMEM, VMEM],
        out_specs=VMEM,
        compiler_params=limit(4),
        name="sampled",
    )(rows, signs)


def shards(x, gg, gu, h, go, a_gate, b_gate, a_up, b_up, a_down, b_down, flags, index):
    x, go, gg, gu, h = [a[0, 0] for a in (x, go, gg, gu, h)]
    a_gate, b_gate, a_up, b_up, a_down, b_down = [
        a[0] for a in (a_gate, b_gate, a_up, b_up, a_down, b_down)
    ]
    count = lax.axis_size("coord")
    tokens, rank = x.shape[0], a_gate.shape[1]
    total = flags.shape[0] * count * lax.axis_size("ckpt")
    flags = flags.reshape(-1, rank)
    length = flags.shape[0]
    first = 3 * x.shape[1]
    block = min(256, length)
    aligned = x.shape[1] % block == 0 and gg.shape[0] % block == 0
    where = (index >> (rank.bit_length() - 1)) & (length - 1)
    where = (where & ~63) | (where & 7) << 3 | where >> 3 & 7
    stages = stages_of(count)
    rows = 16 * count * -(-3 * tokens // (16 * count))
    x, go, short = short_products(
        rows, stages[0], *[in_hbm(a) for a in (x, go, a_gate, a_up, b_down)]
    )
    gg, gu, h, long = long_products(
        rows, stages[0], *[in_hbm(a) for a in (gg, gu, h, b_gate, b_up, a_down)]
    )
    flags = after(long[0], flags)
    bits = (length * rank).bit_length() - 1
    ahead = (
        lambda ready: turn(x, go),
        lambda ready: signs_of(rank, bits, after(ready, index)),
    )
    ((x_t, go_t), signs), (short, long) = all_sums([short, long], stages, ahead)
    wide_mix = wide(aligned, block, first, stages[0], short, gg, gu, h, flags)
    final_scale = adapter_scale * float(total) ** -0.5
    mix = along_rows(aligned, block, stages[0], length, long, x_t, go_t, wide_mix, flags)
    contrib = sampled(final_scale, picked(mix, where), signs)
    return total_over(contrib, count)


def solution(mesh):
    in_specs = (
        P("ckpt", "groups", None, "coord"),
        P("ckpt", "groups", "coord", None),
        P("ckpt", "groups", "coord", None),
        P("ckpt", "groups", "coord", None),
        P("ckpt", "groups", None, "coord"),
        P("ckpt", "coord", None),
        P("ckpt", "coord", None),
        P("ckpt", "coord", None),
        P("ckpt", "coord", None),
        P("ckpt", "coord", None),
        P("ckpt", "coord", None),
        P(("coord", "ckpt")),
        P(),
    )
    out_specs = P("groups", None)
    return jax.shard_map(shards, mesh=mesh, in_specs=in_specs, out_specs=out_specs, check_vma=False)
```

```python
import functools

import jax
import jax.numpy as jnp
from jax import lax
from jax.experimental import pallas as pl
from jax.experimental.pallas import tpu as pltpu
from jax.sharding import PartitionSpec as P

F32 = jnp.float32
BF16 = jnp.bfloat16
MIB = 2**20
adapter_scale = 2.0

ANY = pl.BlockSpec(memory_space=pl.ANY)
VMEM = pl.BlockSpec(memory_space=pltpu.VMEM)
SMEM = pl.BlockSpec(memory_space=pltpu.SMEM)


def limit(size):
    return pltpu.CompilerParams(vmem_limit_bytes=int(size * MIB))


def in_hbm(value):
    return pltpu.with_memory_space_constraint(value, pltpu.HBM)


def exchange(value, axis, apart):
    pairs = [(source, source ^ apart) for source in range(lax.axis_size(axis))]
    return lax.ppermute(value, axis, pairs)


def dot(left, right, contract):
    return lax.dot_general(left, right, (contract, ((), ())), preferred_element_type=F32)


def fetch(sources, targets, sems, cuts):
    groups = []
    slot = 0
    for source, target, cut in zip(sources, targets, cuts, strict=True):
        rows = source.shape[0]
        size = -(-rows // (cut * 16)) * 16
        group = []
        for begin in range(0, rows, size):
            end = min(begin + size, rows)
            copy = pltpu.make_async_copy(
                source.at[begin:end], target.at[begin:end], sems.at[slot]
            )
            copy.start()
            group.append(copy)
            slot += 1
        groups.append(group)

    def wait(which):
        for copy in groups[which]:
            copy.wait()

    return wait


def stages_of(count):
    stages, shift = [], 0
    while count > 1:
        radix = 2 if shift == 0 else min(4, count)
        stages.append((shift, radix))
        shift += radix.bit_length() - 1
        count //= radix
    return stages


def my_digit(stage):
    return (lax.axis_index("coord") >> stage[0]) & (stage[1] - 1)


def hand_out(table, stage, own, sends):
    digit = my_digit(stage)
    size = own.shape[0]
    own[...] = table[pl.ds(pl.multiple_of(digit * size, 16), size), :]
    for step, send in enumerate(sends, 1):
        begin = pl.multiple_of((digit ^ step) * size, 16)
        send[...] = table[pl.ds(begin, size), :].astype(BF16)


def put_together(own, others, stage, table):
    digit = my_digit(stage)
    size = own.shape[0]
    table[pl.ds(pl.multiple_of(digit * size, 16), size), :] = own[...]
    for step, other in enumerate(others[::-1], 1):
        table[pl.ds(pl.multiple_of((digit ^ step) * size, 16), size), :] = other[...]


def handed_out(rows, rank, stage):
    size = rows // stage[1]
    sends = [jax.ShapeDtypeStruct((size, rank), BF16)] * (stage[1] - 1)
    return [jax.ShapeDtypeStruct((size, rank), F32)] + sends


def fill(table, row):
    if table.shape[0] > row:
        table[row:, :] = jnp.zeros((table.shape[0] - row, table.shape[1]), F32)


def short_kernel(stage, cuts, *refs):
    ins, held, (own, *sends), (a_gate, a_up, b_down, table, sems) = (
        refs[:7], refs[7:11], refs[11:-5], refs[-5:]
    )
    x, go, gg, b_gate = held
    wait = fetch(ins, (x, go, a_gate, a_up, b_down, gg, b_gate), sems, cuts)
    tokens = x.shape[0]
    for place, (which, left, right) in enumerate(((2, x, a_gate), (3, x, a_up), (4, go, b_down))):
        if place != 1:
            wait(place // 2)
        wait(which)
        table[place * tokens : (place + 1) * tokens, :] = dot(left[...], right[...], ((1,), (0,)))
    fill(table, 3 * tokens)
    hand_out(table, stage, own, sends)
    wait(5)
    wait(6)


def short_products(rows, stage, *ins):
    rank = ins[2].shape[1]
    cuts = (2, 2, 1, 1, 1, 4, 1)
    shapes = [jax.ShapeDtypeStruct(ins[i].shape, ins[i].dtype) for i in (0, 1, 5, 6)]
    shapes = shapes + handed_out(rows, rank, stage)
    outs = pl.pallas_call(
        functools.partial(short_kernel, stage, cuts),
        out_shape=shapes,
        in_specs=[ANY] * len(ins),
        out_specs=[VMEM] * len(shapes),
        scratch_shapes=[pltpu.VMEM(a.shape, a.dtype) for a in ins[2:5]]
        + [pltpu.VMEM((rows, rank), F32), pltpu.SemaphoreType.DMA((sum(cuts),))],
        compiler_params=limit(5),
        cost_estimate=pl.CostEstimate(flops=10**8, bytes_accessed=6 * 10**6, transcendentals=0),
        name="short",
    )(*ins)
    return outs[:4], outs[4:]


def long_kernel(stage, cuts, gg, b_gate, gu, b_up, h, a_down, *refs):
    held, (own, *sends), (t_up, t_down, table, sems) = refs[:2], refs[2:-4], refs[-4:]
    wait = fetch((b_up, gu, a_down, h), (t_up, held[0], t_down, held[1]), sems, cuts)
    rank = table.shape[1]
    row = 0
    for slot, (wide_ref, adapter) in enumerate(((gg, b_gate), (held[0], t_up), (held[1], t_down))):
        if slot:
            wait(2 * slot - 2)
        turned = adapter[...].T
        if slot:
            wait(2 * slot - 1)
        value = dot(turned, wide_ref[...], ((1,), (0,)))
        for part in range(value.shape[1] // rank):
            table[row : row + rank, :] = value[:, part * rank : (part + 1) * rank]
            row += rank
    fill(table, row)
    hand_out(table, stage, own, sends)


def long_products(rows, stage, gg, b_gate, *ins):
    rank = b_gate.shape[1]
    cuts = (1, 4, 1, 4)
    shapes = [jax.ShapeDtypeStruct(a.shape, a.dtype) for a in (ins[0], ins[2])]
    shapes = shapes + handed_out(rows, rank, stage)
    outs = pl.pallas_call(
        functools.partial(long_kernel, stage, cuts),
        out_shape=shapes,
        in_specs=[VMEM] * 2 + [ANY] * 4,
        out_specs=[VMEM] * len(shapes),
        scratch_shapes=[pltpu.VMEM(a.shape, a.dtype) for a in (ins[1], ins[3])]
        + [pltpu.VMEM((rows, rank), F32), pltpu.SemaphoreType.DMA((sum(cuts),))],
        compiler_params=limit(6),
        cost_estimate=pl.CostEstimate(flops=10**9, bytes_accessed=8 * 10**6, transcendentals=0),
        name="long",
    )(gg, b_gate, *ins)
    return *outs[:2], outs[2:]


def add_kernel(following, count, *refs):
    total = refs[0][...]
    for got in refs[1 : 1 + count]:
        total = total + got[...].astype(F32)
    if following is None:
        refs[1 + count][...] = total.astype(BF16)
    else:
        outs, table = refs[1 + count : -1], refs[-1]
        table[...] = total
        hand_out(table, following, outs[0], outs[1:])


def add_up(own, got, following):
    if following is None:
        shapes, scratch = [jax.ShapeDtypeStruct(own.shape, BF16)], []
    else:
        shapes, scratch = handed_out(*own.shape, following), [pltpu.VMEM(own.shape, F32)]
    return pl.pallas_call(
        functools.partial(add_kernel, following, len(got)),
        out_shape=shapes,
        in_specs=[VMEM] * (1 + len(got)),
        out_specs=[VMEM] * len(shapes),
        scratch_shapes=scratch,
        compiler_params=limit(3),
        name="add_up",
    )(own, *got)


def join_kernel(stage, own, *refs):
    put_together(own, refs[:-1], stage, refs[-1])


def join(own, got, stage):
    return pl.pallas_call(
        functools.partial(join_kernel, stage),
        out_shape=jax.ShapeDtypeStruct((own.shape[0] * stage[1], own.shape[1]), BF16),
        in_specs=[VMEM] * (1 + len(got)),
        out_specs=VMEM,
        compiler_params=limit(3),
        name="join",
    )(own, *got)


def swap(sends, stage):
    return [
        exchange(sends[step - 1], "coord", step << stage[0]) for step in range(stage[1] - 1, 0, -1)
    ]


def after(first, second):
    return lax.optimization_barrier((first, second))[1]


def all_sums(halves, stages, ahead):
    beside = []
    owns = [half[0] for half in halves]
    sends = [half[1:] for half in halves]
    for stage, following in zip(stages, stages[1:] + [None], strict=True):
        got = [swap(send, stage) for send in sends]
        for i in range(len(owns)):
            own = after(owns[0], owns[i]) if i else owns[i]
            order = got[i][1:] + got[i][:1] if i else got[i]
            owns[i], *sends[i] = add_up(own, order, following)
    for stage in stages[:0:-1]:
        got = [swap([own] * (stage[1] - 1), stage) for own in owns]
        for i in range(len(owns)):
            own = after(owns[0], owns[i]) if i else owns[i]
            if stage is stages[1]:
                beside.append(ahead[i](owns[0]))
                own = after(beside[i], own)
            owns[i] = join(own, got[i], stage)
    return beside, [[own] + swap([own] * (stages[0][1] - 1), stages[0]) for own in owns]


def total_over(contrib, count):
    members = lax.axis_size("ckpt")
    contrib = contrib + exchange(contrib, "ckpt", 1)
    apart = 1
    while apart < count:
        flip = apart * members + 1
        pairs = [(source, source ^ flip) for source in range(count * members)]
        contrib = contrib + lax.ppermute(contrib, ("coord", "ckpt"), pairs)
        apart *= 2
    return contrib


def turn_kernel(x, go, x_t, go_t):
    x_t[...] = x[...].T
    go_t[...] = go[...].T


def turn(x, go):
    shape = jax.ShapeDtypeStruct(x.shape[::-1], BF16)
    return pl.pallas_call(
        turn_kernel,
        out_shape=[shape, shape],
        in_specs=[VMEM, VMEM],
        out_specs=[VMEM, VMEM],
        compiler_params=limit(4),
        name="turn",
    )(x, go)


def butterflies(blocks):
    half = 1
    while half < len(blocks):
        done = list(blocks)
        for low in range(len(blocks)):
            if not low & half:
                a, b = blocks[low], blocks[low | half]
                if b is None:
                    done[low], done[low | half] = a, a
                else:
                    done[low], done[low | half] = a + b, a - b
        blocks, half = done, half * 2
    return blocks


def along_block(value, out, row):
    size = value.shape[0]
    tiles = butterflies([value[i : i + 8, :] for i in range(0, size, 8)])
    for i, tile in enumerate(tiles):
        out[row + 8 * i : row + 8 * i + 8, :] = tile
    for begin in range(row, row + size, 64):
        tiles = butterflies([out[pl.ds(begin + j, 8, stride=8), :] for j in range(8)])
        for j, tile in enumerate(tiles):
            out[begin + 8 * j : begin + 8 * j + 8, :] = tile


def signed(value, flags, row):
    return jnp.where(flags[row : row + value.shape[0], :] == 0, value, -value)


def keep(aligned, value, flags, row, out):
    value = signed(value, flags, row)
    if aligned:
        along_block(value, out, row)
    else:
        out[row : row + value.shape[0], :] = value


def wide_kernel(aligned, block, first, stage, *refs):
    parts, refs = refs[: stage[1]], refs[stage[1] :]
    gg, gu, h, flags, out, table = refs
    put_together(parts[0], parts[1:], stage, table)
    tokens = gg.shape[1]
    flags = flags.at[first : first + out.shape[0]]
    row = 0
    for slot, piece in enumerate((gg, gu, h)):
        product = table[slot * tokens : (slot + 1) * tokens, :]
        size = block if aligned else piece.shape[0]
        for begin in range(0, piece.shape[0], size):
            value = dot(piece[begin : begin + size, :], product, ((1,), (0,)))
            keep(aligned, value, flags, row, out)
            row += size


def wide(aligned, block, first, stage, parts, gg, gu, h, flags):
    rank = flags.shape[1]
    return pl.pallas_call(
        functools.partial(wide_kernel, aligned, block, first, stage),
        out_shape=jax.ShapeDtypeStruct((3 * gg.shape[0], rank), F32),
        in_specs=[VMEM] * (len(parts) + 4),
        out_specs=VMEM,
        scratch_shapes=[pltpu.VMEM((parts[0].shape[0] * stage[1], rank), BF16)],
        compiler_params=limit(6),
        cost_estimate=pl.CostEstimate(flops=10**9, bytes_accessed=10**7, transcendentals=0),
        name="wide",
    )(*parts, gg, gu, h, flags)


def rows_kernel(aligned, block, stage, *refs):
    parts, refs = refs[: stage[1]], refs[stage[1] :]
    x_t, go_t, wide_mix, flags, mix, table = refs
    width, tokens = x_t.shape
    first = 3 * width
    length, rank = mix.shape
    put_together(parts[0], parts[1:], stage, table)
    product = [
        jnp.concatenate(
            [table[slot * tokens + part : slot * tokens + part + rank, :] for part in range(0, tokens, rank)],
            axis=1,
        )
        for slot in range(3)
    ]
    size = block if aligned else width
    both = jnp.concatenate(product[:2], axis=0)
    for begin in range(0, width, size):
        value = dot(x_t[begin : begin + size, :], both, ((1,), (1,)))
        keep(aligned, value[:, :rank], flags, begin, mix)
        keep(aligned, value[:, rank:], flags, width + begin, mix)
        value = dot(go_t[begin : begin + size, :], product[2], ((1,), (1,)))
        keep(aligned, value, flags, 2 * width + begin, mix)
    filled = first + wide_mix.shape[0]
    if not aligned:
        mix[first:filled, :] = wide_mix[...]
        mix[filled:, :] = jnp.zeros((length - filled, rank), F32)
        for begin in range(0, length, block):
            along_block(mix[begin : begin + block, :], mix, begin)
    number = length // block
    full = -(-filled // block)

    def load(i, begin):
        if not aligned or i * block < first:
            return mix[pl.ds(i * block + begin, 8), :]
        if i >= full:
            return None
        return wide_mix[pl.ds(i * block - first + begin, 8), :]

    def across(step, _):
        begin = pl.multiple_of(step * 8, 8)
        for i, value in enumerate(butterflies([load(i, begin) for i in range(number)])):
            mix[pl.ds(i * block + begin, 8), :] = value
        return _

    if number > 1:
        lax.fori_loop(0, block // 8, across, 0, unroll=4)


def along_rows(aligned, block, stage, length, parts, x_t, go_t, wide_mix, flags):
    rank = flags.shape[1]
    return pl.pallas_call(
        functools.partial(rows_kernel, aligned, block, stage),
        out_shape=jax.ShapeDtypeStruct((length, rank), F32),
        in_specs=[VMEM] * (len(parts) + 4),
        out_specs=VMEM,
        scratch_shapes=[pltpu.VMEM((parts[0].shape[0] * stage[1], rank), BF16)],
        compiler_params=limit(6),
        name="along_rows",
    )(*parts, x_t, go_t, wide_mix, flags)


def parity(value):
    for fold in (16, 8, 4, 2, 1):
        value = value ^ (value >> fold)
    return value & 1


def signs_kernel(bits, lanes, out):
    rank = out.shape[0]
    device = lax.axis_index("coord") * lax.axis_size("ckpt") + lax.axis_index("ckpt")
    index = lanes[...]

    def sign(bit):
        return (1 - 2 * (bit & 1)).astype(F32)

    low = lax.broadcasted_iota(jnp.int32, (8, index.shape[1]), 0)
    tile = sign(parity((index >> bits) & device))
    for bit in range(3):
        tile = tile * jnp.where((low >> bit & 1) == 0, 1.0, sign(index >> bit))
    tiles = [tile]
    for bit in range(3, rank.bit_length() - 1):
        tiles = tiles + [tile * sign(index >> bit) for tile in tiles]
    out[...] = jnp.concatenate(tiles, axis=0).astype(BF16)


def signs_of(rank, bits, index):
    samples = index.shape[0]
    return pl.pallas_call(
        functools.partial(signs_kernel, bits),
        out_shape=jax.ShapeDtypeStruct((rank, samples), BF16),
        in_specs=[VMEM],
        out_specs=VMEM,
        compiler_params=limit(10),
        name="signs",
    )(index.reshape(1, samples))


def pick_kernel(mix, where, rows):
    samples = rows.shape[0]
    unroll, ahead = min(256, samples), 16

    def pick(step, _):
        span = pl.ds(pl.multiple_of(step * unroll, unroll), unroll)
        sources, targets = where.at[span], rows.at[span]
        held = []
        for i in range(unroll):
            held.append(mix[sources[i]])
            if i >= ahead:
                targets[i - ahead] = held[i - ahead]
        for i in range(unroll - ahead, unroll):
            targets[i] = held[i]
        return _

    lax.fori_loop(0, samples // unroll, pick, 0)


def picked(mix, where):
    rank, samples = mix.shape[1], where.shape[0]
    rows = pl.pallas_call(
        pick_kernel,
        out_shape=jax.ShapeDtypeStruct((samples, 1, rank), F32),
        in_specs=[VMEM, SMEM],
        out_specs=VMEM,
        compiler_params=limit(4),
        name="picked",
    )(mix.reshape(-1, 1, rank), where)
    return rows.reshape(samples, rank)


def sample_kernel(final_scale, rows, signs, out):
    samples, rank = rows.shape
    shape = (rank, rank)
    diagonal = lax.broadcasted_iota(jnp.int32, shape, 0) == lax.broadcasted_iota(jnp.int32, shape, 1)
    for begin in range(0, samples, rank):
        value = rows[begin : begin + rank, :]
        high = value.astype(BF16)
        low = (value - high.astype(F32)).astype(BF16)
        sign = signs[:, begin : begin + rank]
        mixed = dot(
            jnp.concatenate([high, low], axis=1), jnp.concatenate([sign, sign], axis=0), ((1,), (0,))
        )
        chosen = jnp.sum(jnp.where(diagonal, mixed, 0.0), axis=0, keepdims=True)
        out[:, begin : begin + rank] = chosen * final_scale


def sampled(final_scale, rows, signs):
    return pl.pallas_call(
        functools.partial(sample_kernel, final_scale),
        out_shape=jax.ShapeDtypeStruct((1, rows.shape[0]), F32),
        in_specs=[VMEM, VMEM],
        out_specs=VMEM,
        compiler_params=limit(4),
        name="sampled",
    )(rows, signs)


def shards(x, gg, gu, h, go, a_gate, b_gate, a_up, b_up, a_down, b_down, flags, index):
    x, go, gg, gu, h = [a[0, 0] for a in (x, go, gg, gu, h)]
    a_gate, b_gate, a_up, b_up, a_down, b_down = [
        a[0] for a in (a_gate, b_gate, a_up, b_up, a_down, b_down)
    ]
    count = lax.axis_size("coord")
    tokens, rank = x.shape[0], a_gate.shape[1]
    total = flags.shape[0] * count * lax.axis_size("ckpt")
    flags = flags.reshape(-1, rank)
    length = flags.shape[0]
    first = 3 * x.shape[1]
    block = min(256, length)
    aligned = x.shape[1] % block == 0 and gg.shape[0] % block == 0
    where = (index >> (rank.bit_length() - 1)) & (length - 1)
    where = (where & ~63) | (where & 7) << 3 | where >> 3 & 7
    stages = stages_of(count)
    rows = 16 * count * -(-3 * tokens // (16 * count))
    (x, go, gg, b_gate), short = short_products(
        rows, stages[0], *[in_hbm(a) for a in (x, go, a_gate, a_up, b_down, gg, b_gate)]
    )
    gu, h, long = long_products(
        rows, stages[0], gg, b_gate, *[in_hbm(a) for a in (gu, b_up, h, a_down)]
    )
    flags = after(long[0], flags)
    bits = (length * rank).bit_length() - 1
    ahead = (
        lambda ready: turn(x, go),
        lambda ready: signs_of(rank, bits, after(ready, index)),
    )
    ((x_t, go_t), signs), (short, long) = all_sums([short, long], stages, ahead)
    wide_mix = wide(aligned, block, first, stages[0], short, gg, gu, h, flags)
    final_scale = adapter_scale * float(total) ** -0.5
    mix = along_rows(aligned, block, stages[0], length, long, x_t, go_t, wide_mix, flags)
    contrib = sampled(final_scale, picked(mix, where), signs)
    return total_over(contrib, count)


def solution(mesh):
    in_specs = (
        P("ckpt", "groups", None, "coord"),
        P("ckpt", "groups", "coord", None),
        P("ckpt", "groups", "coord", None),
        P("ckpt", "groups", "coord", None),
        P("ckpt", "groups", None, "coord"),
        P("ckpt", "coord", None),
        P("ckpt", "coord", None),
        P("ckpt", "coord", None),
        P("ckpt", "coord", None),
        P("ckpt", "coord", None),
        P("ckpt", "coord", None),
        P(("coord", "ckpt")),
        P(),
    )
    out_specs = P("groups", None)
    return jax.shard_map(shards, mesh=mesh, in_specs=in_specs, out_specs=out_specs, check_vma=False)
```

```python
import functools

import jax
import jax.numpy as jnp
from jax import lax
from jax.experimental import pallas as pl
from jax.experimental.pallas import tpu as pltpu
from jax.sharding import PartitionSpec as P

F32 = jnp.float32
BF16 = jnp.bfloat16
MIB = 2**20
adapter_scale = 2.0

ANY = pl.BlockSpec(memory_space=pl.ANY)
VMEM = pl.BlockSpec(memory_space=pltpu.VMEM)
SMEM = pl.BlockSpec(memory_space=pltpu.SMEM)


def limit(size):
    return pltpu.CompilerParams(vmem_limit_bytes=int(size * MIB))


def in_hbm(value):
    return pltpu.with_memory_space_constraint(value, pltpu.HBM)


def exchange(value, axis, apart):
    pairs = [(source, source ^ apart) for source in range(lax.axis_size(axis))]
    return lax.ppermute(value, axis, pairs)


def dot(left, right, contract):
    return lax.dot_general(left, right, (contract, ((), ())), preferred_element_type=F32)


def fetch(sources, targets, sems, cuts):
    groups = []
    slot = 0
    for source, target, cut in zip(sources, targets, cuts, strict=True):
        rows = source.shape[0]
        size = -(-rows // (cut * 16)) * 16
        group = []
        for begin in range(0, rows, size):
            end = min(begin + size, rows)
            copy = pltpu.make_async_copy(
                source.at[begin:end], target.at[begin:end], sems.at[slot]
            )
            copy.start()
            group.append(copy)
            slot += 1
        groups.append(group)

    def wait(which):
        for copy in groups[which]:
            copy.wait()

    return wait


def stages_of(count):
    stages, shift = [], 0
    while count > 1:
        radix = 2 if shift == 0 else min(4, count)
        stages.append((shift, radix))
        shift += radix.bit_length() - 1
        count //= radix
    return stages


def my_digit(stage):
    return (lax.axis_index("coord") >> stage[0]) & (stage[1] - 1)


def hand_out(table, stage, own, sends):
    digit = my_digit(stage)
    size = own.shape[0]
    own[...] = table[pl.ds(pl.multiple_of(digit * size, 16), size), :]
    for step, send in enumerate(sends, 1):
        begin = pl.multiple_of((digit ^ step) * size, 16)
        send[...] = table[pl.ds(begin, size), :].astype(BF16)


def put_together(own, others, stage, table):
    digit = my_digit(stage)
    size = own.shape[0]
    table[pl.ds(pl.multiple_of(digit * size, 16), size), :] = own[...]
    for step, other in enumerate(others[::-1], 1):
        table[pl.ds(pl.multiple_of((digit ^ step) * size, 16), size), :] = other[...]


def handed_out(rows, rank, stage):
    size = rows // stage[1]
    sends = [jax.ShapeDtypeStruct((size, rank), BF16)] * (stage[1] - 1)
    return [jax.ShapeDtypeStruct((size, rank), F32)] + sends


def fill(table, row):
    if table.shape[0] > row:
        table[row:, :] = jnp.zeros((table.shape[0] - row, table.shape[1]), F32)


def short_kernel(stage, cuts, *refs):
    ins, (x, go), (own, *sends), (a_gate, a_up, b_down, table, sems) = (
        refs[:5], refs[5:7], refs[7:-5], refs[-5:]
    )
    wait = fetch(ins, (x, go, a_gate, a_up, b_down), sems, cuts)
    for which in range(5):
        wait(which)
    tokens = x.shape[0]
    table[:tokens, :] = dot(x[...], a_gate[...], ((1,), (0,)))
    table[tokens : 2 * tokens, :] = dot(x[...], a_up[...], ((1,), (0,)))
    table[2 * tokens : 3 * tokens, :] = dot(go[...], b_down[...], ((1,), (0,)))
    fill(table, 3 * tokens)
    hand_out(table, stage, own, sends)


def short_products(rows, stage, *ins):
    rank = ins[2].shape[1]
    cuts = (2, 2, 1, 1, 1)
    shapes = [jax.ShapeDtypeStruct(a.shape, a.dtype) for a in ins[:2]]
    shapes = shapes + handed_out(rows, rank, stage)
    x, go, *sends = pl.pallas_call(
        functools.partial(short_kernel, stage, cuts),
        out_shape=shapes,
        in_specs=[ANY] * len(ins),
        out_specs=[VMEM] * len(shapes),
        scratch_shapes=[pltpu.VMEM(a.shape, a.dtype) for a in ins[2:]]
        + [pltpu.VMEM((rows, rank), F32), pltpu.SemaphoreType.DMA((sum(cuts),))],
        compiler_params=limit(4),
        cost_estimate=pl.CostEstimate(flops=10**8, bytes_accessed=6 * 10**6, transcendentals=0),
        name="short",
    )(*ins)
    return x, go, sends


def long_kernel(stage, cut, *refs):
    ins, held, (own, *sends), (*adapters, table, sems) = refs[:6], refs[6:9], refs[9:-5], refs[-5:]
    rank = table.shape[1]
    per = cut + 1
    waits = []

    def begin(slot):
        wait = fetch(
            (ins[3 + slot], ins[slot]),
            (adapters[slot], held[slot]),
            sems.at[slot * per : (slot + 1) * per],
            (1, cut),
        )
        waits.append(wait)

    begin(0)
    begin(1)
    row = 0
    for slot in range(3):
        waits[slot](0)
        adapter = adapters[slot][...].T
        waits[slot](1)
        if slot == 0:
            begin(2)
        value = dot(adapter, held[slot][...], ((1,), (0,)))
        for part in range(value.shape[1] // rank):
            table[row : row + rank, :] = value[:, part * rank : (part + 1) * rank]
            row += rank
    fill(table, row)
    hand_out(table, stage, own, sends)


def long_products(rows, stage, *ins):
    rank = ins[3].shape[1]
    cut = 4
    held = [jax.ShapeDtypeStruct(a.shape, a.dtype) for a in ins[:3]]
    shapes = held + handed_out(rows, rank, stage)
    outs = pl.pallas_call(
        functools.partial(long_kernel, stage, cut),
        out_shape=shapes,
        in_specs=[ANY] * 6,
        out_specs=[VMEM] * len(shapes),
        scratch_shapes=[pltpu.VMEM(a.shape, a.dtype) for a in ins[3:]]
        + [pltpu.VMEM((rows, rank), F32), pltpu.SemaphoreType.DMA((3 * (cut + 1),))],
        compiler_params=limit(6),
        cost_estimate=pl.CostEstimate(flops=10**9, bytes_accessed=8 * 10**6, transcendentals=0),
        name="long",
    )(*ins)
    return *outs[:3], outs[3:]


def add_kernel(following, count, *refs):
    total = refs[0][...]
    for got in refs[1 : 1 + count]:
        total = total + got[...].astype(F32)
    if following is None:
        refs[1 + count][...] = total.astype(BF16)
    else:
        outs, table = refs[1 + count : -1], refs[-1]
        table[...] = total
        hand_out(table, following, outs[0], outs[1:])


def add_up(own, got, following):
    if following is None:
        shapes, scratch = [jax.ShapeDtypeStruct(own.shape, BF16)], []
    else:
        shapes, scratch = handed_out(*own.shape, following), [pltpu.VMEM(own.shape, F32)]
    return pl.pallas_call(
        functools.partial(add_kernel, following, len(got)),
        out_shape=shapes,
        in_specs=[VMEM] * (1 + len(got)),
        out_specs=[VMEM] * len(shapes),
        scratch_shapes=scratch,
        compiler_params=limit(3),
        name="add_up",
    )(own, *got)


def join_kernel(stage, own, *refs):
    put_together(own, refs[:-1], stage, refs[-1])


def join(own, got, stage):
    return pl.pallas_call(
        functools.partial(join_kernel, stage),
        out_shape=jax.ShapeDtypeStruct((own.shape[0] * stage[1], own.shape[1]), BF16),
        in_specs=[VMEM] * (1 + len(got)),
        out_specs=VMEM,
        compiler_params=limit(3),
        name="join",
    )(own, *got)


def swap(sends, stage):
    return [
        exchange(sends[step - 1], "coord", step << stage[0]) for step in range(stage[1] - 1, 0, -1)
    ]


def after(first, second):
    return lax.optimization_barrier((first, second))[1]


def all_sums(halves, stages, ahead):
    beside = []
    owns = [half[0] for half in halves]
    sends = [half[1:] for half in halves]
    for stage, following in zip(stages, stages[1:] + [None], strict=True):
        got = [swap(send, stage) for send in sends]
        for i in range(len(owns)):
            own = after(owns[0], owns[i]) if i else owns[i]
            order = got[i][1:] + got[i][:1] if i else got[i]
            owns[i], *sends[i] = add_up(own, order, following)
    for stage in stages[:0:-1]:
        got = [swap([own] * (stage[1] - 1), stage) for own in owns]
        for i in range(len(owns)):
            own = after(owns[0], owns[i]) if i else owns[i]
            if stage is stages[1]:
                beside.append(ahead[i](owns[0]))
                own = after(beside[i], own)
            owns[i] = join(own, got[i], stage)
    return beside, [[own] + swap([own] * (stages[0][1] - 1), stages[0]) for own in owns]


def total_over(contrib, count):
    members = lax.axis_size("ckpt")
    contrib = contrib + exchange(contrib, "ckpt", 1)
    apart = 1
    while apart < count:
        flip = apart * members + 1
        pairs = [(source, source ^ flip) for source in range(count * members)]
        contrib = contrib + lax.ppermute(contrib, ("coord", "ckpt"), pairs)
        apart *= 2
    return contrib


def turn_kernel(x, go, x_t, go_t):
    x_t[...] = x[...].T
    go_t[...] = go[...].T


def turn(x, go):
    shape = jax.ShapeDtypeStruct(x.shape[::-1], BF16)
    return pl.pallas_call(
        turn_kernel,
        out_shape=[shape, shape],
        in_specs=[VMEM, VMEM],
        out_specs=[VMEM, VMEM],
        compiler_params=limit(4),
        name="turn",
    )(x, go)


def butterflies(blocks):
    half = 1
    while half < len(blocks):
        done = list(blocks)
        for low in range(len(blocks)):
            if not low & half:
                a, b = blocks[low], blocks[low | half]
                if b is None:
                    done[low], done[low | half] = a, a
                else:
                    done[low], done[low | half] = a + b, a - b
        blocks, half = done, half * 2
    return blocks


def along_block(value, out, row):
    size = value.shape[0]
    tiles = butterflies([value[i : i + 8, :] for i in range(0, size, 8)])
    for i, tile in enumerate(tiles):
        out[row + 8 * i : row + 8 * i + 8, :] = tile
    for begin in range(row, row + size, 64):
        tiles = butterflies([out[pl.ds(begin + j, 8, stride=8), :] for j in range(8)])
        for j, tile in enumerate(tiles):
            out[begin + 8 * j : begin + 8 * j + 8, :] = tile


def signed(value, flags, row):
    return jnp.where(flags[row : row + value.shape[0], :] == 0, value, -value)


def keep(aligned, value, flags, row, out):
    value = signed(value, flags, row)
    if aligned:
        along_block(value, out, row)
    else:
        out[row : row + value.shape[0], :] = value


def wide_kernel(aligned, block, first, stage, *refs):
    parts, refs = refs[: stage[1]], refs[stage[1] :]
    gg, gu, h, flags, out, table = refs
    put_together(parts[0], parts[1:], stage, table)
    tokens = gg.shape[1]
    flags = flags.at[first : first + out.shape[0]]
    row = 0
    for slot, piece in enumerate((gg, gu, h)):
        product = table[slot * tokens : (slot + 1) * tokens, :]
        size = block if aligned else piece.shape[0]
        for begin in range(0, piece.shape[0], size):
            value = dot(piece[begin : begin + size, :], product, ((1,), (0,)))
            keep(aligned, value, flags, row, out)
            row += size


def wide(aligned, block, first, stage, parts, gg, gu, h, flags):
    rank = flags.shape[1]
    return pl.pallas_call(
        functools.partial(wide_kernel, aligned, block, first, stage),
        out_shape=jax.ShapeDtypeStruct((3 * gg.shape[0], rank), F32),
        in_specs=[VMEM] * (len(parts) + 4),
        out_specs=VMEM,
        scratch_shapes=[pltpu.VMEM((parts[0].shape[0] * stage[1], rank), BF16)],
        compiler_params=limit(6),
        cost_estimate=pl.CostEstimate(flops=10**9, bytes_accessed=10**7, transcendentals=0),
        name="wide",
    )(*parts, gg, gu, h, flags)


def rows_kernel(aligned, block, stage, *refs):
    parts, refs = refs[: stage[1]], refs[stage[1] :]
    x_t, go_t, wide_mix, flags, mix, table = refs
    width, tokens = x_t.shape
    first = 3 * width
    length, rank = mix.shape
    put_together(parts[0], parts[1:], stage, table)
    product = [
        jnp.concatenate(
            [table[slot * tokens + part : slot * tokens + part + rank, :] for part in range(0, tokens, rank)],
            axis=1,
        )
        for slot in range(3)
    ]
    size = block if aligned else width
    both = jnp.concatenate(product[:2], axis=0)
    for begin in range(0, width, size):
        value = dot(x_t[begin : begin + size, :], both, ((1,), (1,)))
        keep(aligned, value[:, :rank], flags, begin, mix)
        keep(aligned, value[:, rank:], flags, width + begin, mix)
        value = dot(go_t[begin : begin + size, :], product[2], ((1,), (1,)))
        keep(aligned, value, flags, 2 * width + begin, mix)
    filled = first + wide_mix.shape[0]
    if not aligned:
        mix[first:filled, :] = wide_mix[...]
        mix[filled:, :] = jnp.zeros((length - filled, rank), F32)
        for begin in range(0, length, block):
            along_block(mix[begin : begin + block, :], mix, begin)
    number = length // block
    full = -(-filled // block)

    def load(i, begin):
        if not aligned or i * block < first:
            return mix[pl.ds(i * block + begin, 8), :]
        if i >= full:
            return None
        return wide_mix[pl.ds(i * block - first + begin, 8), :]

    def across(step, _):
        begin = pl.multiple_of(step * 8, 8)
        for i, value in enumerate(butterflies([load(i, begin) for i in range(number)])):
            mix[pl.ds(i * block + begin, 8), :] = value
        return _

    if number > 1:
        lax.fori_loop(0, block // 8, across, 0, unroll=4)


def along_rows(aligned, block, stage, length, parts, x_t, go_t, wide_mix, flags):
    rank = flags.shape[1]
    return pl.pallas_call(
        functools.partial(rows_kernel, aligned, block, stage),
        out_shape=jax.ShapeDtypeStruct((length, rank), F32),
        in_specs=[VMEM] * (len(parts) + 4),
        out_specs=VMEM,
        scratch_shapes=[pltpu.VMEM((parts[0].shape[0] * stage[1], rank), BF16)],
        compiler_params=limit(6),
        name="along_rows",
    )(*parts, x_t, go_t, wide_mix, flags)


def parity(value):
    for fold in (16, 8, 4, 2, 1):
        value = value ^ (value >> fold)
    return value & 1


def signs_kernel(bits, lanes, out):
    rank = out.shape[0]
    device = lax.axis_index("coord") * lax.axis_size("ckpt") + lax.axis_index("ckpt")
    index = lanes[...]

    def sign(bit):
        return (1 - 2 * (bit & 1)).astype(F32)

    low = lax.broadcasted_iota(jnp.int32, (8, index.shape[1]), 0)
    tile = sign(parity((index >> bits) & device))
    for bit in range(3):
        tile = tile * jnp.where((low >> bit & 1) == 0, 1.0, sign(index >> bit))
    tiles = [tile]
    for bit in range(3, rank.bit_length() - 1):
        tiles = tiles + [tile * sign(index >> bit) for tile in tiles]
    out[...] = jnp.concatenate(tiles, axis=0).astype(BF16)


def signs_of(rank, bits, index):
    samples = index.shape[0]
    return pl.pallas_call(
        functools.partial(signs_kernel, bits),
        out_shape=jax.ShapeDtypeStruct((rank, samples), BF16),
        in_specs=[VMEM],
        out_specs=VMEM,
        compiler_params=limit(10),
        name="signs",
    )(index.reshape(1, samples))


def sample_kernel(final_scale, unroll, mix, where, signs, out):
    rank = mix.shape[2]
    samples = out.shape[1]
    shape = (rank, rank)
    diagonal = lax.broadcasted_iota(jnp.int32, shape, 0) == lax.broadcasted_iota(jnp.int32, shape, 1)
    place = lax.broadcasted_iota(jnp.int32, (8, rank), 0)
    masks = [place == i for i in range(8)]

    def picked(begin):
        tile = None
        for i in range(8):
            row = jnp.broadcast_to(mix[where[begin + i]], (8, rank))
            tile = row if tile is None else jnp.where(masks[i], row, tile)
        return tile

    def step(which, _):
        for part in range(unroll):
            begin = pl.multiple_of((which * unroll + part) * rank, rank)
            value = jnp.concatenate([picked(begin + i) for i in range(0, rank, 8)], axis=0)
            high = value.astype(BF16)
            low = (value - high.astype(F32)).astype(BF16)
            sign = signs[:, pl.ds(begin, rank)]
            mixed = dot(
                jnp.concatenate([high, low], axis=1), jnp.concatenate([sign, sign], axis=0), ((1,), (0,))
            )
            chosen = jnp.sum(jnp.where(diagonal, mixed, 0.0), axis=0, keepdims=True)
            out[:, pl.ds(begin, rank)] = chosen * final_scale
        return _

    lax.fori_loop(0, samples // (rank * unroll), step, 0)


def sampled(final_scale, mix, where, signs):
    rank, samples = signs.shape
    unroll = min(4, samples // rank)
    return pl.pallas_call(
        functools.partial(sample_kernel, final_scale, unroll),
        out_shape=jax.ShapeDtypeStruct((1, samples), F32),
        in_specs=[VMEM, SMEM, VMEM],
        out_specs=VMEM,
        compiler_params=limit(4),
        name="sampled",
    )(mix.reshape(-1, 1, rank), where, signs)


def shards(x, gg, gu, h, go, a_gate, b_gate, a_up, b_up, a_down, b_down, flags, index):
    x, go, gg, gu, h = [a[0, 0] for a in (x, go, gg, gu, h)]
    a_gate, b_gate, a_up, b_up, a_down, b_down = [
        a[0] for a in (a_gate, b_gate, a_up, b_up, a_down, b_down)
    ]
    count = lax.axis_size("coord")
    tokens, rank = x.shape[0], a_gate.shape[1]
    total = flags.shape[0] * count * lax.axis_size("ckpt")
    flags = flags.reshape(-1, rank)
    length = flags.shape[0]
    first = 3 * x.shape[1]
    block = min(256, length)
    aligned = x.shape[1] % block == 0 and gg.shape[0] % block == 0
    where = (index >> (rank.bit_length() - 1)) & (length - 1)
    where = (where & ~63) | (where & 7) << 3 | where >> 3 & 7
    stages = stages_of(count)
    rows = 16 * count * -(-3 * tokens // (16 * count))
    x, go, short = short_products(
        rows, stages[0], *[in_hbm(a) for a in (x, go, a_gate, a_up, b_down)]
    )
    gg, gu, h, long = long_products(
        rows, stages[0], *[in_hbm(a) for a in (gg, gu, h, b_gate, b_up, a_down)]
    )
    flags = after(long[0], flags)
    bits = (length * rank).bit_length() - 1
    ahead = (
        lambda ready: turn(x, go),
        lambda ready: signs_of(rank, bits, after(ready, index)),
    )
    ((x_t, go_t), signs), (short, long) = all_sums([short, long], stages, ahead)
    wide_mix = wide(aligned, block, first, stages[0], short, gg, gu, h, flags)
    final_scale = adapter_scale * float(total) ** -0.5
    mix = along_rows(aligned, block, stages[0], length, long, x_t, go_t, wide_mix, flags)
    contrib = sampled(final_scale, mix, where, signs)
    return total_over(contrib, count)


def solution(mesh):
    in_specs = (
        P("ckpt", "groups", None, "coord"),
        P("ckpt", "groups", "coord", None),
        P("ckpt", "groups", "coord", None),
        P("ckpt", "groups", "coord", None),
        P("ckpt", "groups", None, "coord"),
        P("ckpt", "coord", None),
        P("ckpt", "coord", None),
        P("ckpt", "coord", None),
        P("ckpt", "coord", None),
        P("ckpt", "coord", None),
        P("ckpt", "coord", None),
        P(("coord", "ckpt")),
        P(),
    )
    out_specs = P("groups", None)
    return jax.shard_map(shards, mesh=mesh, in_specs=in_specs, out_specs=out_specs, check_vma=False)
```

```python
import functools

import jax
import jax.numpy as jnp
from jax import lax
from jax.experimental import pallas as pl
from jax.experimental.pallas import tpu as pltpu
from jax.sharding import PartitionSpec as P

F32 = jnp.float32
BF16 = jnp.bfloat16
MIB = 2**20
adapter_scale = 2.0

ANY = pl.BlockSpec(memory_space=pl.ANY)
VMEM = pl.BlockSpec(memory_space=pltpu.VMEM)
SMEM = pl.BlockSpec(memory_space=pltpu.SMEM)


def limit(size):
    return pltpu.CompilerParams(vmem_limit_bytes=int(size * MIB))


def in_hbm(value):
    return pltpu.with_memory_space_constraint(value, pltpu.HBM)


def exchange(value, axis, apart):
    pairs = [(source, source ^ apart) for source in range(lax.axis_size(axis))]
    return lax.ppermute(value, axis, pairs)


def dot(left, right, contract):
    return lax.dot_general(left, right, (contract, ((), ())), preferred_element_type=F32)


def fetch(sources, targets, sems, cuts):
    groups = []
    slot = 0
    for source, target, cut in zip(sources, targets, cuts, strict=True):
        rows = source.shape[0]
        size = -(-rows // (cut * 16)) * 16
        group = []
        for begin in range(0, rows, size):
            end = min(begin + size, rows)
            copy = pltpu.make_async_copy(
                source.at[begin:end], target.at[begin:end], sems.at[slot]
            )
            copy.start()
            group.append(copy)
            slot += 1
        groups.append(group)

    def wait(which):
        for copy in groups[which]:
            copy.wait()

    return wait


def stages_of(count):
    stages, shift = [], 0
    while count > 1:
        radix = 2 if shift == 0 else min(4, count)
        stages.append((shift, radix))
        shift += radix.bit_length() - 1
        count //= radix
    return stages


def my_digit(stage):
    return (lax.axis_index("coord") >> stage[0]) & (stage[1] - 1)


def hand_out(table, stage, own, sends):
    digit = my_digit(stage)
    size = own.shape[0]
    own[...] = table[pl.ds(pl.multiple_of(digit * size, 16), size), :]
    for step, send in enumerate(sends, 1):
        begin = pl.multiple_of((digit ^ step) * size, 16)
        send[...] = table[pl.ds(begin, size), :].astype(BF16)


def put_together(own, others, stage, table):
    digit = my_digit(stage)
    size = own.shape[0]
    table[pl.ds(pl.multiple_of(digit * size, 16), size), :] = own[...]
    for step, other in enumerate(others[::-1], 1):
        table[pl.ds(pl.multiple_of((digit ^ step) * size, 16), size), :] = other[...]


def handed_out(rows, rank, stage):
    size = rows // stage[1]
    sends = [jax.ShapeDtypeStruct((size, rank), BF16)] * (stage[1] - 1)
    return [jax.ShapeDtypeStruct((size, rank), F32)] + sends


def fill(table, row):
    if table.shape[0] > row:
        table[row:, :] = jnp.zeros((table.shape[0] - row, table.shape[1]), F32)


def short_kernel(stage, cuts, *refs):
    ins, (x, go), (own, *sends), (a_gate, a_up, b_down, table, sems) = (
        refs[:5], refs[5:7], refs[7:-5], refs[-5:]
    )
    wait = fetch(ins, (x, go, a_gate, a_up, b_down), sems, cuts)
    for which in range(5):
        wait(which)
    tokens = x.shape[0]
    table[:tokens, :] = dot(x[...], a_gate[...], ((1,), (0,)))
    table[tokens : 2 * tokens, :] = dot(x[...], a_up[...], ((1,), (0,)))
    table[2 * tokens : 3 * tokens, :] = dot(go[...], b_down[...], ((1,), (0,)))
    fill(table, 3 * tokens)
    hand_out(table, stage, own, sends)


def short_products(rows, stage, *ins):
    rank = ins[2].shape[1]
    cuts = (2, 2, 1, 1, 1)
    shapes = [jax.ShapeDtypeStruct(a.shape, a.dtype) for a in ins[:2]]
    shapes = shapes + handed_out(rows, rank, stage)
    x, go, *sends = pl.pallas_call(
        functools.partial(short_kernel, stage, cuts),
        out_shape=shapes,
        in_specs=[ANY] * len(ins),
        out_specs=[VMEM] * len(shapes),
        scratch_shapes=[pltpu.VMEM(a.shape, a.dtype) for a in ins[2:]]
        + [pltpu.VMEM((rows, rank), F32), pltpu.SemaphoreType.DMA((sum(cuts),))],
        compiler_params=limit(4),
        cost_estimate=pl.CostEstimate(flops=10**8, bytes_accessed=6 * 10**6, transcendentals=0),
        name="short",
    )(*ins)
    return x, go, sends


def long_kernel(stage, cut, *refs):
    ins, held, (own, *sends), (*adapters, table, sems) = refs[:6], refs[6:9], refs[9:-5], refs[-5:]
    rank = table.shape[1]
    per = cut + 1
    waits = []

    def begin(slot):
        wait = fetch(
            (ins[3 + slot], ins[slot]),
            (adapters[slot], held[slot]),
            sems.at[slot * per : (slot + 1) * per],
            (1, cut),
        )
        waits.append(wait)

    begin(0)
    begin(1)
    row = 0
    for slot in range(3):
        waits[slot](0)
        adapter = adapters[slot][...].T
        waits[slot](1)
        if slot == 0:
            begin(2)
        value = dot(adapter, held[slot][...], ((1,), (0,)))
        for part in range(value.shape[1] // rank):
            table[row : row + rank, :] = value[:, part * rank : (part + 1) * rank]
            row += rank
    fill(table, row)
    hand_out(table, stage, own, sends)


def long_products(rows, stage, *ins):
    rank = ins[3].shape[1]
    cut = 4
    held = [jax.ShapeDtypeStruct(a.shape, a.dtype) for a in ins[:3]]
    shapes = held + handed_out(rows, rank, stage)
    outs = pl.pallas_call(
        functools.partial(long_kernel, stage, cut),
        out_shape=shapes,
        in_specs=[ANY] * 6,
        out_specs=[VMEM] * len(shapes),
        scratch_shapes=[pltpu.VMEM(a.shape, a.dtype) for a in ins[3:]]
        + [pltpu.VMEM((rows, rank), F32), pltpu.SemaphoreType.DMA((3 * (cut + 1),))],
        compiler_params=limit(6),
        cost_estimate=pl.CostEstimate(flops=10**9, bytes_accessed=8 * 10**6, transcendentals=0),
        name="long",
    )(*ins)
    return *outs[:3], outs[3:]


def add_kernel(following, count, *refs):
    total = refs[0][...]
    for got in refs[1 : 1 + count]:
        total = total + got[...].astype(F32)
    if following is None:
        refs[1 + count][...] = total.astype(BF16)
    else:
        outs, table = refs[1 + count : -1], refs[-1]
        table[...] = total
        hand_out(table, following, outs[0], outs[1:])


def add_up(own, got, following):
    if following is None:
        shapes, scratch = [jax.ShapeDtypeStruct(own.shape, BF16)], []
    else:
        shapes, scratch = handed_out(*own.shape, following), [pltpu.VMEM(own.shape, F32)]
    return pl.pallas_call(
        functools.partial(add_kernel, following, len(got)),
        out_shape=shapes,
        in_specs=[VMEM] * (1 + len(got)),
        out_specs=[VMEM] * len(shapes),
        scratch_shapes=scratch,
        compiler_params=limit(3),
        name="add_up",
    )(own, *got)


def join_kernel(stage, own, *refs):
    put_together(own, refs[:-1], stage, refs[-1])


def join(own, got, stage):
    return pl.pallas_call(
        functools.partial(join_kernel, stage),
        out_shape=jax.ShapeDtypeStruct((own.shape[0] * stage[1], own.shape[1]), BF16),
        in_specs=[VMEM] * (1 + len(got)),
        out_specs=VMEM,
        compiler_params=limit(3),
        name="join",
    )(own, *got)


def swap(sends, stage):
    return [
        exchange(sends[step - 1], "coord", step << stage[0]) for step in range(stage[1] - 1, 0, -1)
    ]


def after(first, second):
    return lax.optimization_barrier((first, second))[1]


def all_sums(halves, stages, ahead):
    beside = []
    owns = [half[0] for half in halves]
    sends = [half[1:] for half in halves]
    for stage, following in zip(stages, stages[1:] + [None], strict=True):
        got = [swap(send, stage) for send in sends]
        for i in range(len(owns)):
            own = after(owns[0], owns[i]) if i else owns[i]
            order = got[i][1:] + got[i][:1] if i else got[i]
            owns[i], *sends[i] = add_up(own, order, following)
    for stage in stages[:0:-1]:
        got = [swap([own] * (stage[1] - 1), stage) for own in owns]
        for i in range(len(owns)):
            own = after(owns[0], owns[i]) if i else owns[i]
            if stage is stages[1]:
                beside.append(ahead[i](owns[0]))
                own = after(beside[i], own)
            owns[i] = join(own, got[i], stage)
    return beside, [[own] + swap([own] * (stages[0][1] - 1), stages[0]) for own in owns]


def total_over(contrib, count):
    members = lax.axis_size("ckpt")
    contrib = contrib + exchange(contrib, "ckpt", 1)
    apart = 1
    while apart < count:
        flip = apart * members + 1
        pairs = [(source, source ^ flip) for source in range(count * members)]
        contrib = contrib + lax.ppermute(contrib, ("coord", "ckpt"), pairs)
        apart *= 2
    return contrib


def turn_kernel(x, go, x_t, go_t):
    x_t[...] = x[...].T
    go_t[...] = go[...].T


def turn(x, go):
    shape = jax.ShapeDtypeStruct(x.shape[::-1], BF16)
    return pl.pallas_call(
        turn_kernel,
        out_shape=[shape, shape],
        in_specs=[VMEM, VMEM],
        out_specs=[VMEM, VMEM],
        compiler_params=limit(4),
        name="turn",
    )(x, go)


def butterflies(blocks):
    half = 1
    while half < len(blocks):
        done = list(blocks)
        for low in range(len(blocks)):
            if not low & half:
                a, b = blocks[low], blocks[low | half]
                if b is None:
                    done[low], done[low | half] = a, a
                else:
                    done[low], done[low | half] = a + b, a - b
        blocks, half = done, half * 2
    return blocks


def along_block(value, out, row):
    size = value.shape[0]
    tiles = butterflies([value[i : i + 8, :] for i in range(0, size, 8)])
    for i, tile in enumerate(tiles):
        out[row + 8 * i : row + 8 * i + 8, :] = tile
    for begin in range(row, row + size, 64):
        tiles = butterflies([out[pl.ds(begin + j, 8, stride=8), :] for j in range(8)])
        for j, tile in enumerate(tiles):
            out[begin + 8 * j : begin + 8 * j + 8, :] = tile


def signed(value, flags, row):
    return jnp.where(flags[row : row + value.shape[0], :] == 0, value, -value)


def keep(aligned, value, flags, row, out):
    value = signed(value, flags, row)
    if aligned:
        along_block(value, out, row)
    else:
        out[row : row + value.shape[0], :] = value


def wide_kernel(aligned, block, first, stage, *refs):
    parts, refs = refs[: stage[1]], refs[stage[1] :]
    gg, gu, h, flags, out, table = refs
    put_together(parts[0], parts[1:], stage, table)
    tokens = gg.shape[1]
    flags = flags.at[first : first + out.shape[0]]
    row = 0
    for slot, piece in enumerate((gg, gu, h)):
        product = table[slot * tokens : (slot + 1) * tokens, :]
        size = block if aligned else piece.shape[0]
        for begin in range(0, piece.shape[0], size):
            value = dot(piece[begin : begin + size, :], product, ((1,), (0,)))
            keep(aligned, value, flags, row, out)
            row += size


def wide(aligned, block, first, stage, parts, gg, gu, h, flags):
    rank = flags.shape[1]
    return pl.pallas_call(
        functools.partial(wide_kernel, aligned, block, first, stage),
        out_shape=jax.ShapeDtypeStruct((3 * gg.shape[0], rank), F32),
        in_specs=[VMEM] * (len(parts) + 4),
        out_specs=VMEM,
        scratch_shapes=[pltpu.VMEM((parts[0].shape[0] * stage[1], rank), BF16)],
        compiler_params=limit(6),
        cost_estimate=pl.CostEstimate(flops=10**9, bytes_accessed=10**7, transcendentals=0),
        name="wide",
    )(*parts, gg, gu, h, flags)


def rows_kernel(aligned, block, stage, *refs):
    parts, refs = refs[: stage[1]], refs[stage[1] :]
    x_t, go_t, wide_mix, flags, mix, table = refs
    width, tokens = x_t.shape
    first = 3 * width
    length, rank = mix.shape
    put_together(parts[0], parts[1:], stage, table)
    product = [
        jnp.concatenate(
            [table[slot * tokens + part : slot * tokens + part + rank, :] for part in range(0, tokens, rank)],
            axis=1,
        )
        for slot in range(3)
    ]
    size = block if aligned else width
    both = jnp.concatenate(product[:2], axis=0)
    for begin in range(0, width, size):
        value = dot(x_t[begin : begin + size, :], both, ((1,), (1,)))
        keep(aligned, value[:, :rank], flags, begin, mix)
        keep(aligned, value[:, rank:], flags, width + begin, mix)
        value = dot(go_t[begin : begin + size, :], product[2], ((1,), (1,)))
        keep(aligned, value, flags, 2 * width + begin, mix)
    filled = first + wide_mix.shape[0]
    if not aligned:
        mix[first:filled, :] = wide_mix[...]
        mix[filled:, :] = jnp.zeros((length - filled, rank), F32)
        for begin in range(0, length, block):
            along_block(mix[begin : begin + block, :], mix, begin)
    number = length // block
    full = -(-filled // block)

    def load(i, begin):
        if not aligned or i * block < first:
            return mix[pl.ds(i * block + begin, 8), :]
        if i >= full:
            return None
        return wide_mix[pl.ds(i * block - first + begin, 8), :]

    def across(step, _):
        begin = pl.multiple_of(step * 8, 8)
        for i, value in enumerate(butterflies([load(i, begin) for i in range(number)])):
            mix[pl.ds(i * block + begin, 8), :] = value
        return _

    if number > 1:
        lax.fori_loop(0, block // 8, across, 0, unroll=4)


def along_rows(aligned, block, stage, length, parts, x_t, go_t, wide_mix, flags):
    rank = flags.shape[1]
    return pl.pallas_call(
        functools.partial(rows_kernel, aligned, block, stage),
        out_shape=jax.ShapeDtypeStruct((length, rank), F32),
        in_specs=[VMEM] * (len(parts) + 4),
        out_specs=VMEM,
        scratch_shapes=[pltpu.VMEM((parts[0].shape[0] * stage[1], rank), BF16)],
        compiler_params=limit(6),
        name="along_rows",
    )(*parts, x_t, go_t, wide_mix, flags)


def parity(value):
    for fold in (16, 8, 4, 2, 1):
        value = value ^ (value >> fold)
    return value & 1


def signs_kernel(bits, lanes, out):
    rank = out.shape[0]
    device = lax.axis_index("coord") * lax.axis_size("ckpt") + lax.axis_index("ckpt")
    index = lanes[...]

    def sign(bit):
        return (1 - 2 * (bit & 1)).astype(F32)

    low = lax.broadcasted_iota(jnp.int32, (8, index.shape[1]), 0)
    tile = sign(parity((index >> bits) & device))
    for bit in range(3):
        tile = tile * jnp.where((low >> bit & 1) == 0, 1.0, sign(index >> bit))
    tiles = [tile]
    for bit in range(3, rank.bit_length() - 1):
        tiles = tiles + [tile * sign(index >> bit) for tile in tiles]
    out[...] = jnp.concatenate(tiles, axis=0).astype(BF16)


def signs_of(rank, bits, index):
    samples = index.shape[0]
    return pl.pallas_call(
        functools.partial(signs_kernel, bits),
        out_shape=jax.ShapeDtypeStruct((rank, samples), BF16),
        in_specs=[VMEM],
        out_specs=VMEM,
        compiler_params=limit(10),
        name="signs",
    )(index.reshape(1, samples))


PLACE_BITS = 16


def pick_kernel(mix, where, rows):
    pairs = where.shape[0]
    unroll, ahead = min(128, pairs), 8

    def pick(step, _):
        begin = pl.multiple_of(step * unroll, unroll)
        sources = where.at[pl.ds(begin, unroll)]
        targets = (rows.at[pl.ds(begin, unroll)], rows.at[pl.ds(begin + pairs, unroll)])
        held = []
        for i in range(unroll):
            both = sources[i]
            held.append((mix[both & (2**PLACE_BITS - 1)], mix[both >> PLACE_BITS]))
            if i >= ahead:
                for target, row in zip(targets, held[i - ahead], strict=True):
                    target[i - ahead] = row
        for i in range(unroll - ahead, unroll):
            for target, row in zip(targets, held[i], strict=True):
                target[i] = row
        return _

    lax.fori_loop(0, pairs // unroll, pick, 0)


def picked(mix, where):
    length, rank = mix.shape
    samples = where.shape[0]
    assert length < 2 ** (PLACE_BITS - 1)
    where = where[: samples // 2] | where[samples // 2 :] << PLACE_BITS
    rows = pl.pallas_call(
        pick_kernel,
        out_shape=jax.ShapeDtypeStruct((samples, 1, rank), F32),
        in_specs=[VMEM, SMEM],
        out_specs=VMEM,
        compiler_params=limit(4),
        name="picked",
    )(mix.reshape(-1, 1, rank), where)
    return rows.reshape(samples, rank)


def sample_kernel(final_scale, rows, signs, out):
    samples, rank = rows.shape
    shape = (rank, rank)
    diagonal = lax.broadcasted_iota(jnp.int32, shape, 0) == lax.broadcasted_iota(jnp.int32, shape, 1)
    for begin in range(0, samples, rank):
        value = rows[begin : begin + rank, :]
        high = value.astype(BF16)
        low = (value - high.astype(F32)).astype(BF16)
        sign = signs[:, begin : begin + rank]
        mixed = dot(
            jnp.concatenate([high, low], axis=1), jnp.concatenate([sign, sign], axis=0), ((1,), (0,))
        )
        chosen = jnp.sum(jnp.where(diagonal, mixed, 0.0), axis=0, keepdims=True)
        out[:, begin : begin + rank] = chosen * final_scale


def sampled(final_scale, rows, signs):
    return pl.pallas_call(
        functools.partial(sample_kernel, final_scale),
        out_shape=jax.ShapeDtypeStruct((1, rows.shape[0]), F32),
        in_specs=[VMEM, VMEM],
        out_specs=VMEM,
        compiler_params=limit(4),
        name="sampled",
    )(rows, signs)


def shards(x, gg, gu, h, go, a_gate, b_gate, a_up, b_up, a_down, b_down, flags, index):
    x, go, gg, gu, h = [a[0, 0] for a in (x, go, gg, gu, h)]
    a_gate, b_gate, a_up, b_up, a_down, b_down = [
        a[0] for a in (a_gate, b_gate, a_up, b_up, a_down, b_down)
    ]
    count = lax.axis_size("coord")
    tokens, rank = x.shape[0], a_gate.shape[1]
    total = flags.shape[0] * count * lax.axis_size("ckpt")
    flags = flags.reshape(-1, rank)
    length = flags.shape[0]
    first = 3 * x.shape[1]
    block = min(256, length)
    aligned = x.shape[1] % block == 0 and gg.shape[0] % block == 0
    where = (index >> (rank.bit_length() - 1)) & (length - 1)
    where = (where & ~63) | (where & 7) << 3 | where >> 3 & 7
    stages = stages_of(count)
    rows = 16 * count * -(-3 * tokens // (16 * count))
    x, go, short = short_products(
        rows, stages[0], *[in_hbm(a) for a in (x, go, a_gate, a_up, b_down)]
    )
    gg, gu, h, long = long_products(
        rows, stages[0], *[in_hbm(a) for a in (gg, gu, h, b_gate, b_up, a_down)]
    )
    flags = after(long[0], flags)
    bits = (length * rank).bit_length() - 1
    ahead = (
        lambda ready: turn(x, go),
        lambda ready: signs_of(rank, bits, after(ready, index)),
    )
    ((x_t, go_t), signs), (short, long) = all_sums([short, long], stages, ahead)
    wide_mix = wide(aligned, block, first, stages[0], short, gg, gu, h, flags)
    final_scale = adapter_scale * float(total) ** -0.5
    mix = along_rows(aligned, block, stages[0], length, long, x_t, go_t, wide_mix, flags)
    contrib = sampled(final_scale, picked(mix, where), signs)
    return total_over(contrib, count)


def solution(mesh):
    in_specs = (
        P("ckpt", "groups", None, "coord"),
        P("ckpt", "groups", "coord", None),
        P("ckpt", "groups", "coord", None),
        P("ckpt", "groups", "coord", None),
        P("ckpt", "groups", None, "coord"),
        P("ckpt", "coord", None),
        P("ckpt", "coord", None),
        P("ckpt", "coord", None),
        P("ckpt", "coord", None),
        P("ckpt", "coord", None),
        P("ckpt", "coord", None),
        P(("coord", "ckpt")),
        P(),
    )
    out_specs = P("groups", None)
    return jax.shard_map(shards, mesh=mesh, in_specs=in_specs, out_specs=out_specs, check_vma=False)
```

```python
import functools

import jax
import jax.numpy as jnp
from jax import lax
from jax.experimental import pallas as pl
from jax.experimental.pallas import tpu as pltpu
from jax.sharding import PartitionSpec as P

F32 = jnp.float32
BF16 = jnp.bfloat16
MIB = 2**20
adapter_scale = 2.0

ANY = pl.BlockSpec(memory_space=pl.ANY)
VMEM = pl.BlockSpec(memory_space=pltpu.VMEM)
SMEM = pl.BlockSpec(memory_space=pltpu.SMEM)


def limit(size):
    return pltpu.CompilerParams(vmem_limit_bytes=int(size * MIB))


def in_hbm(value):
    return pltpu.with_memory_space_constraint(value, pltpu.HBM)


def exchange(value, axis, apart):
    pairs = [(source, source ^ apart) for source in range(lax.axis_size(axis))]
    return lax.ppermute(value, axis, pairs)


def dot(left, right, contract):
    return lax.dot_general(left, right, (contract, ((), ())), preferred_element_type=F32)


def fetch(sources, targets, sems, cuts):
    groups = []
    slot = 0
    for source, target, cut in zip(sources, targets, cuts, strict=True):
        rows = source.shape[0]
        size = -(-rows // (cut * 16)) * 16
        group = []
        for begin in range(0, rows, size):
            end = min(begin + size, rows)
            copy = pltpu.make_async_copy(
                source.at[begin:end], target.at[begin:end], sems.at[slot]
            )
            copy.start()
            group.append(copy)
            slot += 1
        groups.append(group)

    def wait(which):
        for copy in groups[which]:
            copy.wait()

    return wait


def stages_of(count):
    stages, shift = [], 0
    while count > 1:
        radix = 2 if shift == 0 else min(4, count)
        stages.append((shift, radix))
        shift += radix.bit_length() - 1
        count //= radix
    return stages


def my_digit(stage):
    return (lax.axis_index("coord") >> stage[0]) & (stage[1] - 1)


def hand_out(table, stage, own, sends):
    digit = my_digit(stage)
    size = own.shape[0]
    own[...] = table[pl.ds(pl.multiple_of(digit * size, 16), size), :]
    for step, send in enumerate(sends, 1):
        begin = pl.multiple_of((digit ^ step) * size, 16)
        send[...] = table[pl.ds(begin, size), :].astype(BF16)


def put_together(own, others, stage, table):
    digit = my_digit(stage)
    size = own.shape[0]
    table[pl.ds(pl.multiple_of(digit * size, 16), size), :] = own[...]
    for step, other in enumerate(others[::-1], 1):
        table[pl.ds(pl.multiple_of((digit ^ step) * size, 16), size), :] = other[...]


def handed_out(rows, rank, stage):
    size = rows // stage[1]
    sends = [jax.ShapeDtypeStruct((size, rank), BF16)] * (stage[1] - 1)
    return [jax.ShapeDtypeStruct((size, rank), F32)] + sends


def fill(table, row):
    if table.shape[0] > row:
        table[row:, :] = jnp.zeros((table.shape[0] - row, table.shape[1]), F32)


def short_kernel(stage, cuts, *refs):
    ins, (x, go), (own, *sends), (a_gate, a_up, b_down, table, sems) = (
        refs[:5], refs[5:7], refs[7:-5], refs[-5:]
    )
    wait = fetch(ins, (x, go, a_gate, a_up, b_down), sems, cuts)
    for which in range(5):
        wait(which)
    tokens = x.shape[0]
    table[:tokens, :] = dot(x[...], a_gate[...], ((1,), (0,)))
    table[tokens : 2 * tokens, :] = dot(x[...], a_up[...], ((1,), (0,)))
    table[2 * tokens : 3 * tokens, :] = dot(go[...], b_down[...], ((1,), (0,)))
    fill(table, 3 * tokens)
    hand_out(table, stage, own, sends)


def short_products(rows, stage, *ins):
    rank = ins[2].shape[1]
    cuts = (2, 2, 1, 1, 1)
    shapes = [jax.ShapeDtypeStruct(a.shape, a.dtype) for a in ins[:2]]
    shapes = shapes + handed_out(rows, rank, stage)
    x, go, *sends = pl.pallas_call(
        functools.partial(short_kernel, stage, cuts),
        out_shape=shapes,
        in_specs=[ANY] * len(ins),
        out_specs=[VMEM] * len(shapes),
        scratch_shapes=[pltpu.VMEM(a.shape, a.dtype) for a in ins[2:]]
        + [pltpu.VMEM((rows, rank), F32), pltpu.SemaphoreType.DMA((sum(cuts),))],
        compiler_params=limit(4),
        cost_estimate=pl.CostEstimate(flops=10**8, bytes_accessed=6 * 10**6, transcendentals=0),
        name="short",
    )(*ins)
    return x, go, sends


def long_kernel(stage, cut, *refs):
    ins, held, (own, *sends), (*adapters, table, sems) = refs[:6], refs[6:9], refs[9:-5], refs[-5:]
    rank = table.shape[1]
    per = cut + 1
    waits = []

    def begin(slot):
        wait = fetch(
            (ins[3 + slot], ins[slot]),
            (adapters[slot], held[slot]),
            sems.at[slot * per : (slot + 1) * per],
            (1, cut),
        )
        waits.append(wait)

    begin(0)
    begin(1)
    row = 0
    for slot in range(3):
        waits[slot](0)
        adapter = adapters[slot][...].T
        waits[slot](1)
        if slot == 0:
            begin(2)
        value = dot(adapter, held[slot][...], ((1,), (0,)))
        for part in range(value.shape[1] // rank):
            table[row : row + rank, :] = value[:, part * rank : (part + 1) * rank]
            row += rank
    fill(table, row)
    hand_out(table, stage, own, sends)


def long_products(rows, stage, *ins):
    rank = ins[3].shape[1]
    cut = 4
    held = [jax.ShapeDtypeStruct(a.shape, a.dtype) for a in ins[:3]]
    shapes = held + handed_out(rows, rank, stage)
    outs = pl.pallas_call(
        functools.partial(long_kernel, stage, cut),
        out_shape=shapes,
        in_specs=[ANY] * 6,
        out_specs=[VMEM] * len(shapes),
        scratch_shapes=[pltpu.VMEM(a.shape, a.dtype) for a in ins[3:]]
        + [pltpu.VMEM((rows, rank), F32), pltpu.SemaphoreType.DMA((3 * (cut + 1),))],
        compiler_params=limit(6),
        cost_estimate=pl.CostEstimate(flops=10**9, bytes_accessed=8 * 10**6, transcendentals=0),
        name="long",
    )(*ins)
    return *outs[:3], outs[3:]


def add_kernel(following, count, *refs):
    total = refs[0][...]
    for got in refs[1 : 1 + count]:
        total = total + got[...].astype(F32)
    if following is None:
        refs[1 + count][...] = total.astype(BF16)
    else:
        outs, table = refs[1 + count : -1], refs[-1]
        table[...] = total
        hand_out(table, following, outs[0], outs[1:])


def add_up(own, got, following):
    if following is None:
        shapes, scratch = [jax.ShapeDtypeStruct(own.shape, BF16)], []
    else:
        shapes, scratch = handed_out(*own.shape, following), [pltpu.VMEM(own.shape, F32)]
    return pl.pallas_call(
        functools.partial(add_kernel, following, len(got)),
        out_shape=shapes,
        in_specs=[VMEM] * (1 + len(got)),
        out_specs=[VMEM] * len(shapes),
        scratch_shapes=scratch,
        compiler_params=limit(3),
        name="add_up",
    )(own, *got)


def join_kernel(stage, own, *refs):
    put_together(own, refs[:-1], stage, refs[-1])


def join(own, got, stage):
    return pl.pallas_call(
        functools.partial(join_kernel, stage),
        out_shape=jax.ShapeDtypeStruct((own.shape[0] * stage[1], own.shape[1]), BF16),
        in_specs=[VMEM] * (1 + len(got)),
        out_specs=VMEM,
        compiler_params=limit(3),
        name="join",
    )(own, *got)


def swap(sends, stage):
    return [
        exchange(sends[step - 1], "coord", step << stage[0]) for step in range(stage[1] - 1, 0, -1)
    ]


def after(first, second):
    return lax.optimization_barrier((first, second))[1]


def all_sums(halves, stages, ahead):
    beside = []
    owns = [half[0] for half in halves]
    sends = [half[1:] for half in halves]
    for stage, following in zip(stages, stages[1:] + [None], strict=True):
        got = [swap(send, stage) for send in sends]
        for i in range(len(owns)):
            own = after(owns[0], owns[i]) if i else owns[i]
            order = got[i][1:] + got[i][:1] if i else got[i]
            owns[i], *sends[i] = add_up(own, order, following)
    for stage in stages[:0:-1]:
        got = [swap([own] * (stage[1] - 1), stage) for own in owns]
        for i in range(len(owns)):
            own = after(owns[0], owns[i]) if i else owns[i]
            if stage is stages[1]:
                beside.append(ahead[i](owns[0]))
                own = after(beside[i], own)
            owns[i] = join(own, got[i], stage)
    return beside, [[own] + swap([own] * (stages[0][1] - 1), stages[0]) for own in owns]


def total_over(contrib, count):
    members = lax.axis_size("ckpt")
    contrib = contrib + exchange(contrib, "ckpt", 1)
    apart = 1
    while apart < count:
        flip = apart * members + 1
        pairs = [(source, source ^ flip) for source in range(count * members)]
        contrib = contrib + lax.ppermute(contrib, ("coord", "ckpt"), pairs)
        apart *= 2
    return contrib


def turn_kernel(x, go, x_t, go_t):
    x_t[...] = x[...].T
    go_t[...] = go[...].T


def turn(x, go):
    shape = jax.ShapeDtypeStruct(x.shape[::-1], BF16)
    return pl.pallas_call(
        turn_kernel,
        out_shape=[shape, shape],
        in_specs=[VMEM, VMEM],
        out_specs=[VMEM, VMEM],
        compiler_params=limit(4),
        name="turn",
    )(x, go)


def butterflies(blocks):
    half = 1
    while half < len(blocks):
        done = list(blocks)
        for low in range(len(blocks)):
            if not low & half:
                a, b = blocks[low], blocks[low | half]
                if b is None:
                    done[low], done[low | half] = a, a
                else:
                    done[low], done[low | half] = a + b, a - b
        blocks, half = done, half * 2
    return blocks


def along_block(value, out, row):
    size = value.shape[0]
    tiles = butterflies([value[i : i + 8, :] for i in range(0, size, 8)])
    for i, tile in enumerate(tiles):
        out[row + 8 * i : row + 8 * i + 8, :] = tile
    for begin in range(row, row + size, 64):
        tiles = butterflies([out[pl.ds(begin + j, 8, stride=8), :] for j in range(8)])
        for j, tile in enumerate(tiles):
            out[begin + 8 * j : begin + 8 * j + 8, :] = tile


def signed(value, flags, row):
    return jnp.where(flags[row : row + value.shape[0], :] == 0, value, -value)


def keep(aligned, value, flags, row, out):
    value = signed(value, flags, row)
    if aligned:
        along_block(value, out, row)
    else:
        out[row : row + value.shape[0], :] = value


def wide_kernel(aligned, block, first, stage, *refs):
    parts, refs = refs[: stage[1]], refs[stage[1] :]
    gg, gu, h, flags, out, table = refs
    put_together(parts[0], parts[1:], stage, table)
    tokens = gg.shape[1]
    flags = flags.at[first : first + out.shape[0]]
    row = 0
    for slot, piece in enumerate((gg, gu, h)):
        product = table[slot * tokens : (slot + 1) * tokens, :]
        size = block if aligned else piece.shape[0]
        for begin in range(0, piece.shape[0], size):
            value = dot(piece[begin : begin + size, :], product, ((1,), (0,)))
            keep(aligned, value, flags, row, out)
            row += size


def wide(aligned, block, first, stage, parts, gg, gu, h, flags):
    rank = flags.shape[1]
    return pl.pallas_call(
        functools.partial(wide_kernel, aligned, block, first, stage),
        out_shape=jax.ShapeDtypeStruct((3 * gg.shape[0], rank), F32),
        in_specs=[VMEM] * (len(parts) + 4),
        out_specs=VMEM,
        scratch_shapes=[pltpu.VMEM((parts[0].shape[0] * stage[1], rank), BF16)],
        compiler_params=limit(6),
        cost_estimate=pl.CostEstimate(flops=10**9, bytes_accessed=10**7, transcendentals=0),
        name="wide",
    )(*parts, gg, gu, h, flags)


def rows_kernel(aligned, block, stage, *refs):
    parts, refs = refs[: stage[1]], refs[stage[1] :]
    x_t, go_t, wide_mix, flags, mix, table = refs
    width, tokens = x_t.shape
    first = 3 * width
    length, rank = mix.shape[0] - 2 * SPARE, mix.shape[1]
    mix = mix.at[SPARE : SPARE + length]
    put_together(parts[0], parts[1:], stage, table)
    product = [
        jnp.concatenate(
            [table[slot * tokens + part : slot * tokens + part + rank, :] for part in range(0, tokens, rank)],
            axis=1,
        )
        for slot in range(3)
    ]
    size = block if aligned else width
    both = jnp.concatenate(product[:2], axis=0)
    for begin in range(0, width, size):
        value = dot(x_t[begin : begin + size, :], both, ((1,), (1,)))
        keep(aligned, value[:, :rank], flags, begin, mix)
        keep(aligned, value[:, rank:], flags, width + begin, mix)
        value = dot(go_t[begin : begin + size, :], product[2], ((1,), (1,)))
        keep(aligned, value, flags, 2 * width + begin, mix)
    filled = first + wide_mix.shape[0]
    if not aligned:
        mix[first:filled, :] = wide_mix[...]
        mix[filled:, :] = jnp.zeros((length - filled, rank), F32)
        for begin in range(0, length, block):
            along_block(mix[begin : begin + block, :], mix, begin)
    number = length // block
    full = -(-filled // block)

    def load(i, begin):
        if not aligned or i * block < first:
            return mix[pl.ds(i * block + begin, 8), :]
        if i >= full:
            return None
        return wide_mix[pl.ds(i * block - first + begin, 8), :]

    def across(step, _):
        begin = pl.multiple_of(step * 8, 8)
        for i, value in enumerate(butterflies([load(i, begin) for i in range(number)])):
            mix[pl.ds(i * block + begin, 8), :] = value
        return _

    if number > 1:
        lax.fori_loop(0, block // 8, across, 0, unroll=4)


def along_rows(aligned, block, stage, length, parts, x_t, go_t, wide_mix, flags):
    rank = flags.shape[1]
    return pl.pallas_call(
        functools.partial(rows_kernel, aligned, block, stage),
        out_shape=jax.ShapeDtypeStruct((length + 2 * SPARE, rank), F32),
        in_specs=[VMEM] * (len(parts) + 4),
        out_specs=VMEM,
        scratch_shapes=[pltpu.VMEM((parts[0].shape[0] * stage[1], rank), BF16)],
        compiler_params=limit(6),
        name="along_rows",
    )(*parts, x_t, go_t, wide_mix, flags)


def parity(value):
    for fold in (16, 8, 4, 2, 1):
        value = value ^ (value >> fold)
    return value & 1


def signs_kernel(bits, lanes, out):
    rank = out.shape[0]
    device = lax.axis_index("coord") * lax.axis_size("ckpt") + lax.axis_index("ckpt")
    index = lanes[...]

    def sign(bit):
        return (1 - 2 * (bit & 1)).astype(F32)

    low = lax.broadcasted_iota(jnp.int32, (8, index.shape[1]), 0)
    tile = sign(parity((index >> bits) & device))
    for bit in range(3):
        tile = tile * jnp.where((low >> bit & 1) == 0, 1.0, sign(index >> bit))
    tiles = [tile]
    for bit in range(3, rank.bit_length() - 1):
        tiles = tiles + [tile * sign(index >> bit) for tile in tiles]
    out[...] = jnp.concatenate(tiles, axis=0).astype(BF16)


def signs_of(rank, bits, index):
    samples = index.shape[0]
    return pl.pallas_call(
        functools.partial(signs_kernel, bits),
        out_shape=jax.ShapeDtypeStruct((rank, samples), BF16),
        in_specs=[VMEM],
        out_specs=VMEM,
        compiler_params=limit(10),
        name="signs",
    )(index.reshape(1, samples))


SPARE = 64


def sample_kernel(final_scale, unroll, mix, where, signs, out):
    rank = mix.shape[1]
    samples = out.shape[1]
    shape = (rank, rank)
    diagonal = lax.broadcasted_iota(jnp.int32, shape, 0) == lax.broadcasted_iota(jnp.int32, shape, 1)
    place = lax.broadcasted_iota(jnp.int32, (8, rank), 0)
    masks = [place == i for i in range(8)]
    views = [mix.at[SPARE - 8 * i : mix.shape[0] - 8 * i] for i in range(8)]

    def picked(begin):
        tile = None
        for i in range(8):
            rows = views[i][pl.ds(where[begin + i], 8, stride=8), :]
            tile = rows if tile is None else jnp.where(masks[i], rows, tile)
        return tile

    def step(which, _):
        for part in range(unroll):
            begin = pl.multiple_of((which * unroll + part) * rank, rank)
            value = jnp.concatenate([picked(begin + i) for i in range(0, rank, 8)], axis=0)
            high = value.astype(BF16)
            low = (value - high.astype(F32)).astype(BF16)
            sign = signs[:, pl.ds(begin, rank)]
            mixed = dot(
                jnp.concatenate([high, low], axis=1), jnp.concatenate([sign, sign], axis=0), ((1,), (0,))
            )
            chosen = jnp.sum(jnp.where(diagonal, mixed, 0.0), axis=0, keepdims=True)
            out[:, pl.ds(begin, rank)] = chosen * final_scale
        return _

    lax.fori_loop(0, samples // (rank * unroll), step, 0)


def sampled(final_scale, mix, where, signs):
    rank, samples = signs.shape
    unroll = min(4, samples // rank)
    return pl.pallas_call(
        functools.partial(sample_kernel, final_scale, unroll),
        out_shape=jax.ShapeDtypeStruct((1, samples), F32),
        in_specs=[VMEM, SMEM, VMEM],
        out_specs=VMEM,
        compiler_params=limit(4),
        name="sampled",
    )(mix, where, signs)


def shards(x, gg, gu, h, go, a_gate, b_gate, a_up, b_up, a_down, b_down, flags, index):
    x, go, gg, gu, h = [a[0, 0] for a in (x, go, gg, gu, h)]
    a_gate, b_gate, a_up, b_up, a_down, b_down = [
        a[0] for a in (a_gate, b_gate, a_up, b_up, a_down, b_down)
    ]
    count = lax.axis_size("coord")
    tokens, rank = x.shape[0], a_gate.shape[1]
    total = flags.shape[0] * count * lax.axis_size("ckpt")
    flags = flags.reshape(-1, rank)
    length = flags.shape[0]
    first = 3 * x.shape[1]
    block = min(256, length)
    aligned = x.shape[1] % block == 0 and gg.shape[0] % block == 0
    where = (index >> (rank.bit_length() - 1)) & (length - 1)
    where = (where & ~63) | (where & 7) << 3 | where >> 3 & 7
    stages = stages_of(count)
    rows = 16 * count * -(-3 * tokens // (16 * count))
    x, go, short = short_products(
        rows, stages[0], *[in_hbm(a) for a in (x, go, a_gate, a_up, b_down)]
    )
    gg, gu, h, long = long_products(
        rows, stages[0], *[in_hbm(a) for a in (gg, gu, h, b_gate, b_up, a_down)]
    )
    flags = after(long[0], flags)
    bits = (length * rank).bit_length() - 1
    ahead = (
        lambda ready: turn(x, go),
        lambda ready: signs_of(rank, bits, after(ready, index)),
    )
    ((x_t, go_t), signs), (short, long) = all_sums([short, long], stages, ahead)
    wide_mix = wide(aligned, block, first, stages[0], short, gg, gu, h, flags)
    final_scale = adapter_scale * float(total) ** -0.5
    mix = along_rows(aligned, block, stages[0], length, long, x_t, go_t, wide_mix, flags)
    contrib = sampled(final_scale, mix, where, signs)
    return total_over(contrib, count)


def solution(mesh):
    in_specs = (
        P("ckpt", "groups", None, "coord"),
        P("ckpt", "groups", "coord", None),
        P("ckpt", "groups", "coord", None),
        P("ckpt", "groups", "coord", None),
        P("ckpt", "groups", None, "coord"),
        P("ckpt", "coord", None),
        P("ckpt", "coord", None),
        P("ckpt", "coord", None),
        P("ckpt", "coord", None),
        P("ckpt", "coord", None),
        P("ckpt", "coord", None),
        P(("coord", "ckpt")),
        P(),
    )
    out_specs = P("groups", None)
    return jax.shard_map(shards, mesh=mesh, in_specs=in_specs, out_specs=out_specs, check_vma=False)
```

```python
import functools

import jax
import jax.numpy as jnp
from jax import lax
from jax.experimental import pallas as pl
from jax.experimental.pallas import tpu as pltpu
from jax.sharding import PartitionSpec as P

F32 = jnp.float32
BF16 = jnp.bfloat16
MIB = 2**20
adapter_scale = 2.0

ANY = pl.BlockSpec(memory_space=pl.ANY)
VMEM = pl.BlockSpec(memory_space=pltpu.VMEM)
SMEM = pl.BlockSpec(memory_space=pltpu.SMEM)


def limit(size):
    return pltpu.CompilerParams(vmem_limit_bytes=int(size * MIB))


def in_hbm(value):
    return pltpu.with_memory_space_constraint(value, pltpu.HBM)


def exchange(value, axis, apart):
    pairs = [(source, source ^ apart) for source in range(lax.axis_size(axis))]
    return lax.ppermute(value, axis, pairs)


def dot(left, right, contract):
    return lax.dot_general(left, right, (contract, ((), ())), preferred_element_type=F32)


def fetch(sources, targets, sems, cuts):
    groups = []
    slot = 0
    for source, target, cut in zip(sources, targets, cuts, strict=True):
        rows = source.shape[0]
        size = -(-rows // (cut * 16)) * 16
        group = []
        for begin in range(0, rows, size):
            end = min(begin + size, rows)
            copy = pltpu.make_async_copy(
                source.at[begin:end], target.at[begin:end], sems.at[slot]
            )
            copy.start()
            group.append(copy)
            slot += 1
        groups.append(group)

    def wait(which):
        for copy in groups[which]:
            copy.wait()

    return wait


def stages_of(count):
    stages, shift = [], 0
    while count > 1:
        radix = 2 if shift == 0 else min(4, count)
        stages.append((shift, radix))
        shift += radix.bit_length() - 1
        count //= radix
    return stages


def my_digit(stage):
    return (lax.axis_index("coord") >> stage[0]) & (stage[1] - 1)


def hand_out(table, stage, own, sends):
    digit = my_digit(stage)
    size = own.shape[0]
    own[...] = table[pl.ds(pl.multiple_of(digit * size, 16), size), :]
    for step, send in enumerate(sends, 1):
        begin = pl.multiple_of((digit ^ step) * size, 16)
        send[...] = table[pl.ds(begin, size), :].astype(BF16)


def put_together(own, others, stage, table):
    digit = my_digit(stage)
    size = own.shape[0]
    table[pl.ds(pl.multiple_of(digit * size, 16), size), :] = own[...]
    for step, other in enumerate(others[::-1], 1):
        table[pl.ds(pl.multiple_of((digit ^ step) * size, 16), size), :] = other[...]


def handed_out(rows, rank, stage):
    size = rows // stage[1]
    sends = [jax.ShapeDtypeStruct((size, rank), BF16)] * (stage[1] - 1)
    return [jax.ShapeDtypeStruct((size, rank), F32)] + sends


def fill(table, row):
    if table.shape[0] > row:
        table[row:, :] = jnp.zeros((table.shape[0] - row, table.shape[1]), F32)


def short_kernel(stage, cuts, *refs):
    ins, (x, go), (own, *sends), (a_gate, a_up, b_down, table, sems) = (
        refs[:5], refs[5:7], refs[7:-5], refs[-5:]
    )
    wait = fetch(ins, (x, go, a_gate, a_up, b_down), sems, cuts)
    for which in range(5):
        wait(which)
    tokens = x.shape[0]
    table[:tokens, :] = dot(x[...], a_gate[...], ((1,), (0,)))
    table[tokens : 2 * tokens, :] = dot(x[...], a_up[...], ((1,), (0,)))
    table[2 * tokens : 3 * tokens, :] = dot(go[...], b_down[...], ((1,), (0,)))
    fill(table, 3 * tokens)
    hand_out(table, stage, own, sends)


def short_products(rows, stage, *ins):
    rank = ins[2].shape[1]
    cuts = (2, 2, 1, 1, 1)
    shapes = [jax.ShapeDtypeStruct(a.shape, a.dtype) for a in ins[:2]]
    shapes = shapes + handed_out(rows, rank, stage)
    x, go, *sends = pl.pallas_call(
        functools.partial(short_kernel, stage, cuts),
        out_shape=shapes,
        in_specs=[ANY] * len(ins),
        out_specs=[VMEM] * len(shapes),
        scratch_shapes=[pltpu.VMEM(a.shape, a.dtype) for a in ins[2:]]
        + [pltpu.VMEM((rows, rank), F32), pltpu.SemaphoreType.DMA((sum(cuts),))],
        compiler_params=limit(4),
        cost_estimate=pl.CostEstimate(flops=10**8, bytes_accessed=6 * 10**6, transcendentals=0),
        name="short",
    )(*ins)
    return x, go, sends


def long_kernel(stage, cut, *refs):
    ins, held, (own, *sends), (*adapters, table, sems) = refs[:6], refs[6:9], refs[9:-5], refs[-5:]
    rank = table.shape[1]
    per = cut + 1
    waits = []

    def begin(slot):
        wait = fetch(
            (ins[3 + slot], ins[slot]),
            (adapters[slot], held[slot]),
            sems.at[slot * per : (slot + 1) * per],
            (1, cut),
        )
        waits.append(wait)

    begin(0)
    begin(1)
    row = 0
    for slot in range(3):
        waits[slot](0)
        adapter = adapters[slot][...].T
        waits[slot](1)
        if slot == 0:
            begin(2)
        value = dot(adapter, held[slot][...], ((1,), (0,)))
        for part in range(value.shape[1] // rank):
            table[row : row + rank, :] = value[:, part * rank : (part + 1) * rank]
            row += rank
    fill(table, row)
    hand_out(table, stage, own, sends)


def long_products(rows, stage, *ins):
    rank = ins[3].shape[1]
    cut = 4
    held = [jax.ShapeDtypeStruct(a.shape, a.dtype) for a in ins[:3]]
    shapes = held + handed_out(rows, rank, stage)
    outs = pl.pallas_call(
        functools.partial(long_kernel, stage, cut),
        out_shape=shapes,
        in_specs=[ANY] * 6,
        out_specs=[VMEM] * len(shapes),
        scratch_shapes=[pltpu.VMEM(a.shape, a.dtype) for a in ins[3:]]
        + [pltpu.VMEM((rows, rank), F32), pltpu.SemaphoreType.DMA((3 * (cut + 1),))],
        compiler_params=limit(6),
        cost_estimate=pl.CostEstimate(flops=10**9, bytes_accessed=8 * 10**6, transcendentals=0),
        name="long",
    )(*ins)
    return *outs[:3], outs[3:]


def add_kernel(following, count, *refs):
    total = refs[0][...]
    for got in refs[1 : 1 + count]:
        total = total + got[...].astype(F32)
    if following is None:
        refs[1 + count][...] = total.astype(BF16)
    else:
        outs, table = refs[1 + count : -1], refs[-1]
        table[...] = total
        hand_out(table, following, outs[0], outs[1:])


def add_up(own, got, following):
    if following is None:
        shapes, scratch = [jax.ShapeDtypeStruct(own.shape, BF16)], []
    else:
        shapes, scratch = handed_out(*own.shape, following), [pltpu.VMEM(own.shape, F32)]
    return pl.pallas_call(
        functools.partial(add_kernel, following, len(got)),
        out_shape=shapes,
        in_specs=[VMEM] * (1 + len(got)),
        out_specs=[VMEM] * len(shapes),
        scratch_shapes=scratch,
        compiler_params=limit(3),
        name="add_up",
    )(own, *got)


def join_kernel(stage, own, *refs):
    put_together(own, refs[:-1], stage, refs[-1])


def join(own, got, stage):
    return pl.pallas_call(
        functools.partial(join_kernel, stage),
        out_shape=jax.ShapeDtypeStruct((own.shape[0] * stage[1], own.shape[1]), BF16),
        in_specs=[VMEM] * (1 + len(got)),
        out_specs=VMEM,
        compiler_params=limit(3),
        name="join",
    )(own, *got)


def swap(sends, stage):
    return [
        exchange(sends[step - 1], "coord", step << stage[0]) for step in range(stage[1] - 1, 0, -1)
    ]


def after(first, second):
    return lax.optimization_barrier((first, second))[1]


def all_sums(halves, stages, ahead):
    beside = []
    owns = [half[0] for half in halves]
    sends = [half[1:] for half in halves]
    for stage, following in zip(stages, stages[1:] + [None], strict=True):
        got = [swap(send, stage) for send in sends]
        for i in range(len(owns)):
            own = after(owns[0], owns[i]) if i else owns[i]
            order = got[i][1:] + got[i][:1] if i else got[i]
            owns[i], *sends[i] = add_up(own, order, following)
    for stage in stages[:0:-1]:
        got = [swap([own] * (stage[1] - 1), stage) for own in owns]
        for i in range(len(owns)):
            own = after(owns[0], owns[i]) if i else owns[i]
            if stage is stages[1]:
                beside.append(ahead[i](owns[0]))
                own = after(beside[i], own)
            owns[i] = join(own, got[i], stage)
    return beside, [[own] + swap([own] * (stages[0][1] - 1), stages[0]) for own in owns]


def total_over(contrib, count):
    assert lax.axis_size("ckpt") == 2
    core = lax.axis_index("ckpt")
    total = contrib + exchange(contrib, "ckpt", 1)
    shift = 0
    while 1 << shift < count:
        radix = min(8, count >> shift)
        half = radix // 2
        terms = []
        for step in range(half):
            nearer, further = (step or half) << shift, (half + step) << shift
            pairs = [(2 * c + 1, 2 * (c ^ nearer)) for c in range(count)]
            pairs += [(2 * c, 2 * (c ^ further) + 1) for c in range(count)]
            got = lax.ppermute(total, ("coord", "ckpt"), pairs)
            terms.append(got if step else jnp.where(core == 0, total, got))
        while len(terms) > 1:
            terms = [a + b for a, b in zip(terms[::2], terms[1::2], strict=True)]
        total = terms[0] + exchange(terms[0], "ckpt", 1)
        shift += radix.bit_length() - 1
    return total


def turn_kernel(x, go, x_t, go_t):
    x_t[...] = x[...].T
    go_t[...] = go[...].T


def turn(x, go):
    shape = jax.ShapeDtypeStruct(x.shape[::-1], BF16)
    return pl.pallas_call(
        turn_kernel,
        out_shape=[shape, shape],
        in_specs=[VMEM, VMEM],
        out_specs=[VMEM, VMEM],
        compiler_params=limit(4),
        name="turn",
    )(x, go)


def butterflies(blocks):
    half = 1
    while half < len(blocks):
        done = list(blocks)
        for low in range(len(blocks)):
            if not low & half:
                a, b = blocks[low], blocks[low | half]
                if b is None:
                    done[low], done[low | half] = a, a
                else:
                    done[low], done[low | half] = a + b, a - b
        blocks, half = done, half * 2
    return blocks


def along_block(value, out, row):
    size = value.shape[0]
    tiles = butterflies([value[i : i + 8, :] for i in range(0, size, 8)])
    for i, tile in enumerate(tiles):
        out[row + 8 * i : row + 8 * i + 8, :] = tile
    for begin in range(row, row + size, 64):
        tiles = butterflies([out[pl.ds(begin + j, 8, stride=8), :] for j in range(8)])
        for j, tile in enumerate(tiles):
            out[begin + 8 * j : begin + 8 * j + 8, :] = tile


def signed(value, flags, row):
    return jnp.where(flags[row : row + value.shape[0], :] == 0, value, -value)


def keep(aligned, value, flags, row, out):
    value = signed(value, flags, row)
    if aligned:
        along_block(value, out, row)
    else:
        out[row : row + value.shape[0], :] = value


def wide_kernel(aligned, block, first, stage, *refs):
    parts, refs = refs[: stage[1]], refs[stage[1] :]
    gg, gu, h, flags, out, table = refs
    put_together(parts[0], parts[1:], stage, table)
    tokens = gg.shape[1]
    flags = flags.at[first : first + out.shape[0]]
    row = 0
    for slot, piece in enumerate((gg, gu, h)):
        product = table[slot * tokens : (slot + 1) * tokens, :]
        size = block if aligned else piece.shape[0]
        for begin in range(0, piece.shape[0], size):
            value = dot(piece[begin : begin + size, :], product, ((1,), (0,)))
            keep(aligned, value, flags, row, out)
            row += size


def wide(aligned, block, first, stage, parts, gg, gu, h, flags):
    rank = flags.shape[1]
    return pl.pallas_call(
        functools.partial(wide_kernel, aligned, block, first, stage),
        out_shape=jax.ShapeDtypeStruct((3 * gg.shape[0], rank), F32),
        in_specs=[VMEM] * (len(parts) + 4),
        out_specs=VMEM,
        scratch_shapes=[pltpu.VMEM((parts[0].shape[0] * stage[1], rank), BF16)],
        compiler_params=limit(6),
        cost_estimate=pl.CostEstimate(flops=10**9, bytes_accessed=10**7, transcendentals=0),
        name="wide",
    )(*parts, gg, gu, h, flags)


def rows_kernel(aligned, block, stage, *refs):
    parts, refs = refs[: stage[1]], refs[stage[1] :]
    x_t, go_t, wide_mix, flags, mix, table = refs
    width, tokens = x_t.shape
    first = 3 * width
    length, rank = mix.shape
    put_together(parts[0], parts[1:], stage, table)
    product = [
        jnp.concatenate(
            [table[slot * tokens + part : slot * tokens + part + rank, :] for part in range(0, tokens, rank)],
            axis=1,
        )
        for slot in range(3)
    ]
    size = block if aligned else width
    both = jnp.concatenate(product[:2], axis=0)
    for begin in range(0, width, size):
        value = dot(x_t[begin : begin + size, :], both, ((1,), (1,)))
        keep(aligned, value[:, :rank], flags, begin, mix)
        keep(aligned, value[:, rank:], flags, width + begin, mix)
        value = dot(go_t[begin : begin + size, :], product[2], ((1,), (1,)))
        keep(aligned, value, flags, 2 * width + begin, mix)
    filled = first + wide_mix.shape[0]
    if not aligned:
        mix[first:filled, :] = wide_mix[...]
        mix[filled:, :] = jnp.zeros((length - filled, rank), F32)
        for begin in range(0, length, block):
            along_block(mix[begin : begin + block, :], mix, begin)
    number = length // block
    full = -(-filled // block)

    def load(i, begin):
        if not aligned or i * block < first:
            return mix[pl.ds(i * block + begin, 8), :]
        if i >= full:
            return None
        return wide_mix[pl.ds(i * block - first + begin, 8), :]

    def across(step, _):
        begin = pl.multiple_of(step * 8, 8)
        for i, value in enumerate(butterflies([load(i, begin) for i in range(number)])):
            mix[pl.ds(i * block + begin, 8), :] = value
        return _

    if number > 1:
        lax.fori_loop(0, block // 8, across, 0, unroll=4)


def along_rows(aligned, block, stage, length, parts, x_t, go_t, wide_mix, flags):
    rank = flags.shape[1]
    return pl.pallas_call(
        functools.partial(rows_kernel, aligned, block, stage),
        out_shape=jax.ShapeDtypeStruct((length, rank), F32),
        in_specs=[VMEM] * (len(parts) + 4),
        out_specs=VMEM,
        scratch_shapes=[pltpu.VMEM((parts[0].shape[0] * stage[1], rank), BF16)],
        compiler_params=limit(6),
        name="along_rows",
    )(*parts, x_t, go_t, wide_mix, flags)


def parity(value):
    for fold in (16, 8, 4, 2, 1):
        value = value ^ (value >> fold)
    return value & 1


def signs_kernel(bits, lanes, out):
    rank = out.shape[0]
    device = lax.axis_index("coord") * lax.axis_size("ckpt") + lax.axis_index("ckpt")
    index = lanes[...]

    def sign(bit):
        return (1 - 2 * (bit & 1)).astype(F32)

    low = lax.broadcasted_iota(jnp.int32, (8, index.shape[1]), 0)
    tile = sign(parity((index >> bits) & device))
    for bit in range(3):
        tile = tile * jnp.where((low >> bit & 1) == 0, 1.0, sign(index >> bit))
    tiles = [tile]
    for bit in range(3, rank.bit_length() - 1):
        tiles = tiles + [tile * sign(index >> bit) for tile in tiles]
    out[...] = jnp.concatenate(tiles, axis=0).astype(BF16)


def signs_of(rank, bits, index):
    samples = index.shape[0]
    return pl.pallas_call(
        functools.partial(signs_kernel, bits),
        out_shape=jax.ShapeDtypeStruct((rank, samples), BF16),
        in_specs=[VMEM],
        out_specs=VMEM,
        compiler_params=limit(10),
        name="signs",
    )(index.reshape(1, samples))


def pick_kernel(mix, where, rows):
    samples = rows.shape[0]
    unroll, ahead = min(256, samples), 16

    def pick(step, _):
        begin = step * unroll
        held = []
        for i in range(unroll):
            held.append(mix[where[begin + i]])
            if i >= ahead:
                rows[begin + i - ahead] = held[i - ahead]
        for i in range(unroll - ahead, unroll):
            rows[begin + i] = held[i]
        return _

    lax.fori_loop(0, samples // unroll, pick, 0)


def picked(mix, where):
    rank, samples = mix.shape[1], where.shape[0]
    rows = pl.pallas_call(
        pick_kernel,
        out_shape=jax.ShapeDtypeStruct((samples, 1, rank), F32),
        in_specs=[VMEM, SMEM],
        out_specs=VMEM,
        compiler_params=limit(4),
        name="picked",
    )(mix.reshape(-1, 1, rank), where)
    return rows.reshape(samples, rank)


def sample_kernel(final_scale, rows, signs, out):
    samples, rank = rows.shape
    shape = (rank, rank)
    diagonal = lax.broadcasted_iota(jnp.int32, shape, 0) == lax.broadcasted_iota(jnp.int32, shape, 1)
    for begin in range(0, samples, rank):
        value = rows[begin : begin + rank, :]
        high = value.astype(BF16)
        low = (value - high.astype(F32)).astype(BF16)
        sign = signs[:, begin : begin + rank]
        mixed = dot(
            jnp.concatenate([high, low], axis=1), jnp.concatenate([sign, sign], axis=0), ((1,), (0,))
        )
        chosen = jnp.sum(jnp.where(diagonal, mixed, 0.0), axis=0, keepdims=True)
        out[:, begin : begin + rank] = chosen * final_scale


def sampled(final_scale, rows, signs):
    return pl.pallas_call(
        functools.partial(sample_kernel, final_scale),
        out_shape=jax.ShapeDtypeStruct((1, rows.shape[0]), F32),
        in_specs=[VMEM, VMEM],
        out_specs=VMEM,
        compiler_params=limit(4),
        name="sampled",
    )(rows, signs)


def shards(x, gg, gu, h, go, a_gate, b_gate, a_up, b_up, a_down, b_down, flags, index):
    x, go, gg, gu, h = [a[0, 0] for a in (x, go, gg, gu, h)]
    a_gate, b_gate, a_up, b_up, a_down, b_down = [
        a[0] for a in (a_gate, b_gate, a_up, b_up, a_down, b_down)
    ]
    count = lax.axis_size("coord")
    tokens, rank = x.shape[0], a_gate.shape[1]
    total = flags.shape[0] * count * lax.axis_size("ckpt")
    flags = flags.reshape(-1, rank)
    length = flags.shape[0]
    first = 3 * x.shape[1]
    block = min(256, length)
    aligned = x.shape[1] % block == 0 and gg.shape[0] % block == 0
    where = (index >> (rank.bit_length() - 1)) & (length - 1)
    where = (where & ~63) | (where & 7) << 3 | where >> 3 & 7
    stages = stages_of(count)
    rows = 16 * count * -(-3 * tokens // (16 * count))
    x, go, short = short_products(
        rows, stages[0], *[in_hbm(a) for a in (x, go, a_gate, a_up, b_down)]
    )
    gg, gu, h, long = long_products(
        rows, stages[0], *[in_hbm(a) for a in (gg, gu, h, b_gate, b_up, a_down)]
    )
    flags = after(long[0], flags)
    bits = (length * rank).bit_length() - 1
    ahead = (
        lambda ready: turn(x, go),
        lambda ready: signs_of(rank, bits, after(ready, index)),
    )
    ((x_t, go_t), signs), (short, long) = all_sums([short, long], stages, ahead)
    wide_mix = wide(aligned, block, first, stages[0], short, gg, gu, h, flags)
    final_scale = adapter_scale * float(total) ** -0.5
    mix = along_rows(aligned, block, stages[0], length, long, x_t, go_t, wide_mix, flags)
    contrib = sampled(final_scale, picked(mix, where), signs)
    return total_over(contrib, count)


def solution(mesh):
    in_specs = (
        P("ckpt", "groups", None, "coord"),
        P("ckpt", "groups", "coord", None),
        P("ckpt", "groups", "coord", None),
        P("ckpt", "groups", "coord", None),
        P("ckpt", "groups", None, "coord"),
        P("ckpt", "coord", None),
        P("ckpt", "coord", None),
        P("ckpt", "coord", None),
        P("ckpt", "coord", None),
        P("ckpt", "coord", None),
        P("ckpt", "coord", None),
        P(("coord", "ckpt")),
        P(),
    )
    out_specs = P("groups", None)
    return jax.shard_map(shards, mesh=mesh, in_specs=in_specs, out_specs=out_specs, check_vma=False)
```

```python
import functools

import jax
import jax.numpy as jnp
from jax import lax
from jax.experimental import pallas as pl
from jax.experimental.pallas import tpu as pltpu
from jax.sharding import PartitionSpec as P

F32 = jnp.float32
BF16 = jnp.bfloat16
MIB = 2**20
adapter_scale = 2.0

ANY = pl.BlockSpec(memory_space=pl.ANY)
VMEM = pl.BlockSpec(memory_space=pltpu.VMEM)
SMEM = pl.BlockSpec(memory_space=pltpu.SMEM)


def limit(size):
    return pltpu.CompilerParams(vmem_limit_bytes=int(size * MIB))


def in_hbm(value):
    return pltpu.with_memory_space_constraint(value, pltpu.HBM)


def exchange(value, axis, apart):
    pairs = [(source, source ^ apart) for source in range(lax.axis_size(axis))]
    return lax.ppermute(value, axis, pairs)


def dot(left, right, contract):
    return lax.dot_general(left, right, (contract, ((), ())), preferred_element_type=F32)


def fetch(sources, targets, sems, cuts):
    groups = []
    slot = 0
    for source, target, cut in zip(sources, targets, cuts, strict=True):
        rows = source.shape[0]
        size = -(-rows // (cut * 16)) * 16
        group = []
        for begin in range(0, rows, size):
            end = min(begin + size, rows)
            copy = pltpu.make_async_copy(
                source.at[begin:end], target.at[begin:end], sems.at[slot]
            )
            copy.start()
            group.append(copy)
            slot += 1
        groups.append(group)

    def wait(which):
        for copy in groups[which]:
            copy.wait()

    return wait


def stages_of(count):
    stages, shift = [], 0
    while count > 1:
        radix = 2 if shift == 0 else min(4, count)
        stages.append((shift, radix))
        shift += radix.bit_length() - 1
        count //= radix
    return stages


def my_digit(stage):
    return (lax.axis_index("coord") >> stage[0]) & (stage[1] - 1)


def hand_out(table, stage, own, sends):
    digit = my_digit(stage)
    size = own.shape[0]
    own[...] = table[pl.ds(pl.multiple_of(digit * size, 16), size), :]
    for step, send in enumerate(sends, 1):
        begin = pl.multiple_of((digit ^ step) * size, 16)
        send[...] = table[pl.ds(begin, size), :].astype(BF16)


def put_together(own, others, stage, table):
    digit = my_digit(stage)
    size = own.shape[0]
    table[pl.ds(pl.multiple_of(digit * size, 16), size), :] = own[...]
    for step, other in enumerate(others[::-1], 1):
        table[pl.ds(pl.multiple_of((digit ^ step) * size, 16), size), :] = other[...]


def handed_out(rows, rank, stage):
    size = rows // stage[1]
    sends = [jax.ShapeDtypeStruct((size, rank), BF16)] * (stage[1] - 1)
    return [jax.ShapeDtypeStruct((size, rank), F32)] + sends


def fill(table, row):
    if table.shape[0] > row:
        table[row:, :] = jnp.zeros((table.shape[0] - row, table.shape[1]), F32)


def short_kernel(stage, cuts, *refs):
    ins, (x, go), (own, *sends), (a_gate, a_up, b_down, table, sems) = (
        refs[:5], refs[5:7], refs[7:-5], refs[-5:]
    )
    wait = fetch(ins, (x, go, a_gate, a_up, b_down), sems, cuts)
    for which in range(5):
        wait(which)
    tokens = x.shape[0]
    table[:tokens, :] = dot(x[...], a_gate[...], ((1,), (0,)))
    table[tokens : 2 * tokens, :] = dot(x[...], a_up[...], ((1,), (0,)))
    table[2 * tokens : 3 * tokens, :] = dot(go[...], b_down[...], ((1,), (0,)))
    fill(table, 3 * tokens)
    hand_out(table, stage, own, sends)


def short_products(rows, stage, *ins):
    rank = ins[2].shape[1]
    cuts = (2, 2, 1, 1, 1)
    shapes = [jax.ShapeDtypeStruct(a.shape, a.dtype) for a in ins[:2]]
    shapes = shapes + handed_out(rows, rank, stage)
    x, go, *sends = pl.pallas_call(
        functools.partial(short_kernel, stage, cuts),
        out_shape=shapes,
        in_specs=[ANY] * len(ins),
        out_specs=[VMEM] * len(shapes),
        scratch_shapes=[pltpu.VMEM(a.shape, a.dtype) for a in ins[2:]]
        + [pltpu.VMEM((rows, rank), F32), pltpu.SemaphoreType.DMA((sum(cuts),))],
        compiler_params=limit(4),
        cost_estimate=pl.CostEstimate(flops=10**8, bytes_accessed=6 * 10**6, transcendentals=0),
        name="short",
    )(*ins)
    return x, go, sends


def long_kernel(stage, cut, *refs):
    ins, held, (own, *sends), (*adapters, table, sems) = refs[:6], refs[6:9], refs[9:-5], refs[-5:]
    rank = table.shape[1]
    per = cut + 1
    waits = []

    def begin(slot):
        wait = fetch(
            (ins[3 + slot], ins[slot]),
            (adapters[slot], held[slot]),
            sems.at[slot * per : (slot + 1) * per],
            (1, cut),
        )
        waits.append(wait)

    begin(0)
    begin(1)
    row = 0
    for slot in range(3):
        waits[slot](0)
        adapter = adapters[slot][...].T
        waits[slot](1)
        if slot == 0:
            begin(2)
        value = dot(adapter, held[slot][...], ((1,), (0,)))
        for part in range(value.shape[1] // rank):
            table[row : row + rank, :] = value[:, part * rank : (part + 1) * rank]
            row += rank
    fill(table, row)
    hand_out(table, stage, own, sends)


def long_products(rows, stage, *ins):
    rank = ins[3].shape[1]
    cut = 4
    held = [jax.ShapeDtypeStruct(a.shape, a.dtype) for a in ins[:3]]
    shapes = held + handed_out(rows, rank, stage)
    outs = pl.pallas_call(
        functools.partial(long_kernel, stage, cut),
        out_shape=shapes,
        in_specs=[ANY] * 6,
        out_specs=[VMEM] * len(shapes),
        scratch_shapes=[pltpu.VMEM(a.shape, a.dtype) for a in ins[3:]]
        + [pltpu.VMEM((rows, rank), F32), pltpu.SemaphoreType.DMA((3 * (cut + 1),))],
        compiler_params=limit(6),
        cost_estimate=pl.CostEstimate(flops=10**9, bytes_accessed=8 * 10**6, transcendentals=0),
        name="long",
    )(*ins)
    return *outs[:3], outs[3:]


def add_kernel(following, count, *refs):
    total = refs[0][...]
    for got in refs[1 : 1 + count]:
        total = total + got[...].astype(F32)
    if following is None:
        refs[1 + count][...] = total.astype(BF16)
    else:
        outs, table = refs[1 + count : -1], refs[-1]
        table[...] = total
        hand_out(table, following, outs[0], outs[1:])


def add_up(own, got, following):
    if following is None:
        shapes, scratch = [jax.ShapeDtypeStruct(own.shape, BF16)], []
    else:
        shapes, scratch = handed_out(*own.shape, following), [pltpu.VMEM(own.shape, F32)]
    return pl.pallas_call(
        functools.partial(add_kernel, following, len(got)),
        out_shape=shapes,
        in_specs=[VMEM] * (1 + len(got)),
        out_specs=[VMEM] * len(shapes),
        scratch_shapes=scratch,
        compiler_params=limit(3),
        name="add_up",
    )(own, *got)


def join_kernel(stage, own, *refs):
    put_together(own, refs[:-1], stage, refs[-1])


def join(own, got, stage):
    return pl.pallas_call(
        functools.partial(join_kernel, stage),
        out_shape=jax.ShapeDtypeStruct((own.shape[0] * stage[1], own.shape[1]), BF16),
        in_specs=[VMEM] * (1 + len(got)),
        out_specs=VMEM,
        compiler_params=limit(3),
        name="join",
    )(own, *got)


def swap(sends, stage):
    return [
        exchange(sends[step - 1], "coord", step << stage[0]) for step in range(stage[1] - 1, 0, -1)
    ]


def after(first, second):
    return lax.optimization_barrier((first, second))[1]


def all_sums(halves, stages, ahead):
    beside = []
    owns = [half[0] for half in halves]
    sends = [half[1:] for half in halves]
    for stage, following in zip(stages, stages[1:] + [None], strict=True):
        got = [swap(send, stage) for send in sends]
        for i in range(len(owns)):
            own = after(owns[0], owns[i]) if i else owns[i]
            order = got[i][1:] + got[i][:1] if i else got[i]
            owns[i], *sends[i] = add_up(own, order, following)
    for stage in stages[:0:-1]:
        got = [swap([own] * (stage[1] - 1), stage) for own in owns]
        for i in range(len(owns)):
            own = after(owns[0], owns[i]) if i else owns[i]
            if stage is stages[1]:
                beside.append(ahead[i](owns[0]))
                own = after(beside[i], own)
            owns[i] = join(own, got[i], stage)
    return beside, [[own] + swap([own] * (stages[0][1] - 1), stages[0]) for own in owns]


def total_over(contrib, count):
    assert lax.axis_size("ckpt") == 2
    core = lax.axis_index("ckpt")
    total = contrib + exchange(contrib, "ckpt", 1)
    shift = 0
    while 1 << shift < count:
        radix = min(8, count >> shift)
        half = radix // 2
        terms = []
        for step in range(half - 1, -1, -1):
            nearer, further = (step or half) << shift, (half + step) << shift
            pairs = [(2 * c + 1, 2 * (c ^ nearer)) for c in range(count)]
            pairs += [(2 * c, 2 * (c ^ further) + 1) for c in range(count)]
            got = lax.ppermute(total, ("coord", "ckpt"), pairs)
            terms.append(got if step else jnp.where(core == 0, total, got))
        while len(terms) > 1:
            terms = [a + b for a, b in zip(terms[::2], terms[1::2], strict=True)]
        total = terms[0] + exchange(terms[0], "ckpt", 1)
        shift += radix.bit_length() - 1
    return total


def turn_kernel(x, go, x_t, go_t):
    x_t[...] = x[...].T
    go_t[...] = go[...].T


def turn(x, go):
    shape = jax.ShapeDtypeStruct(x.shape[::-1], BF16)
    return pl.pallas_call(
        turn_kernel,
        out_shape=[shape, shape],
        in_specs=[VMEM, VMEM],
        out_specs=[VMEM, VMEM],
        compiler_params=limit(4),
        name="turn",
    )(x, go)


def butterflies(blocks):
    half = 1
    while half < len(blocks):
        done = list(blocks)
        for low in range(len(blocks)):
            if not low & half:
                a, b = blocks[low], blocks[low | half]
                if b is None:
                    done[low], done[low | half] = a, a
                else:
                    done[low], done[low | half] = a + b, a - b
        blocks, half = done, half * 2
    return blocks


def along_block(value, out, row):
    size = value.shape[0]
    tiles = butterflies([value[i : i + 8, :] for i in range(0, size, 8)])
    for i, tile in enumerate(tiles):
        out[row + 8 * i : row + 8 * i + 8, :] = tile
    for begin in range(row, row + size, 64):
        tiles = butterflies([out[pl.ds(begin + j, 8, stride=8), :] for j in range(8)])
        for j, tile in enumerate(tiles):
            out[begin + 8 * j : begin + 8 * j + 8, :] = tile


def signed(value, flags, row):
    return jnp.where(flags[row : row + value.shape[0], :] == 0, value, -value)


def keep(aligned, value, flags, row, out):
    value = signed(value, flags, row)
    if aligned:
        along_block(value, out, row)
    else:
        out[row : row + value.shape[0], :] = value


def wide_kernel(aligned, block, first, stage, *refs):
    parts, refs = refs[: stage[1]], refs[stage[1] :]
    gg, gu, h, flags, out, table = refs
    put_together(parts[0], parts[1:], stage, table)
    tokens = gg.shape[1]
    flags = flags.at[first : first + out.shape[0]]
    row = 0
    for slot, piece in enumerate((gg, gu, h)):
        product = table[slot * tokens : (slot + 1) * tokens, :]
        size = block if aligned else piece.shape[0]
        for begin in range(0, piece.shape[0], size):
            value = dot(piece[begin : begin + size, :], product, ((1,), (0,)))
            keep(aligned, value, flags, row, out)
            row += size


def wide(aligned, block, first, stage, parts, gg, gu, h, flags):
    rank = flags.shape[1]
    return pl.pallas_call(
        functools.partial(wide_kernel, aligned, block, first, stage),
        out_shape=jax.ShapeDtypeStruct((3 * gg.shape[0], rank), F32),
        in_specs=[VMEM] * (len(parts) + 4),
        out_specs=VMEM,
        scratch_shapes=[pltpu.VMEM((parts[0].shape[0] * stage[1], rank), BF16)],
        compiler_params=limit(6),
        cost_estimate=pl.CostEstimate(flops=10**9, bytes_accessed=10**7, transcendentals=0),
        name="wide",
    )(*parts, gg, gu, h, flags)


def rows_kernel(aligned, block, stage, *refs):
    parts, refs = refs[: stage[1]], refs[stage[1] :]
    x_t, go_t, wide_mix, flags, mix, table = refs
    width, tokens = x_t.shape
    first = 3 * width
    length, rank = mix.shape
    put_together(parts[0], parts[1:], stage, table)
    product = [
        jnp.concatenate(
            [table[slot * tokens + part : slot * tokens + part + rank, :] for part in range(0, tokens, rank)],
            axis=1,
        )
        for slot in range(3)
    ]
    size = block if aligned else width
    both = jnp.concatenate(product[:2], axis=0)
    for begin in range(0, width, size):
        value = dot(x_t[begin : begin + size, :], both, ((1,), (1,)))
        keep(aligned, value[:, :rank], flags, begin, mix)
        keep(aligned, value[:, rank:], flags, width + begin, mix)
        value = dot(go_t[begin : begin + size, :], product[2], ((1,), (1,)))
        keep(aligned, value, flags, 2 * width + begin, mix)
    filled = first + wide_mix.shape[0]
    if not aligned:
        mix[first:filled, :] = wide_mix[...]
        mix[filled:, :] = jnp.zeros((length - filled, rank), F32)
        for begin in range(0, length, block):
            along_block(mix[begin : begin + block, :], mix, begin)
    number = length // block
    full = -(-filled // block)

    def load(i, begin):
        if not aligned or i * block < first:
            return mix[pl.ds(i * block + begin, 8), :]
        if i >= full:
            return None
        return wide_mix[pl.ds(i * block - first + begin, 8), :]

    def across(step, _):
        begin = pl.multiple_of(step * 8, 8)
        for i, value in enumerate(butterflies([load(i, begin) for i in range(number)])):
            mix[pl.ds(i * block + begin, 8), :] = value
        return _

    if number > 1:
        lax.fori_loop(0, block // 8, across, 0, unroll=4)


def along_rows(aligned, block, stage, length, parts, x_t, go_t, wide_mix, flags):
    rank = flags.shape[1]
    return pl.pallas_call(
        functools.partial(rows_kernel, aligned, block, stage),
        out_shape=jax.ShapeDtypeStruct((length, rank), F32),
        in_specs=[VMEM] * (len(parts) + 4),
        out_specs=VMEM,
        scratch_shapes=[pltpu.VMEM((parts[0].shape[0] * stage[1], rank), BF16)],
        compiler_params=limit(6),
        name="along_rows",
    )(*parts, x_t, go_t, wide_mix, flags)


def parity(value):
    for fold in (16, 8, 4, 2, 1):
        value = value ^ (value >> fold)
    return value & 1


def signs_kernel(bits, lanes, out):
    rank = out.shape[0]
    device = lax.axis_index("coord") * lax.axis_size("ckpt") + lax.axis_index("ckpt")
    index = lanes[...]

    def sign(bit):
        return (1 - 2 * (bit & 1)).astype(F32)

    low = lax.broadcasted_iota(jnp.int32, (8, index.shape[1]), 0)
    tile = sign(parity((index >> bits) & device))
    for bit in range(3):
        tile = tile * jnp.where((low >> bit & 1) == 0, 1.0, sign(index >> bit))
    tiles = [tile]
    for bit in range(3, rank.bit_length() - 1):
        tiles = tiles + [tile * sign(index >> bit) for tile in tiles]
    out[...] = jnp.concatenate(tiles, axis=0).astype(BF16)


def signs_of(rank, bits, index):
    samples = index.shape[0]
    return pl.pallas_call(
        functools.partial(signs_kernel, bits),
        out_shape=jax.ShapeDtypeStruct((rank, samples), BF16),
        in_specs=[VMEM],
        out_specs=VMEM,
        compiler_params=limit(10),
        name="signs",
    )(index.reshape(1, samples))


def sample_kernel(final_scale, mix, where, signs, out, *rows):
    rank = mix.shape[2]
    samples = out.shape[1]
    number = samples // rank
    ahead = 16
    shape = (rank, rank)
    diagonal = lax.broadcasted_iota(jnp.int32, shape, 0) == lax.broadcasted_iota(jnp.int32, shape, 1)

    def pick(which, target):
        begin = which * rank
        held = []
        for i in range(rank):
            held.append(mix[where[begin + i]])
            if i >= ahead:
                target[i - ahead] = held[i - ahead]
        for i in range(rank - ahead, rank):
            target[i] = held[i]

    def multiplied(which, source):
        value = source.reshape(rank, rank)[...]
        high = value.astype(BF16)
        low = (value - high.astype(F32)).astype(BF16)
        sign = signs[:, pl.ds(pl.multiple_of(which * rank, rank), rank)]
        return dot(
            jnp.concatenate([high, low], axis=1), jnp.concatenate([sign, sign], axis=0), ((1,), (0,))
        )

    def finish(which, mixed):
        chosen = jnp.sum(jnp.where(diagonal, mixed, 0.0), axis=0, keepdims=True)
        out[:, pl.ds(pl.multiple_of(which * rank, rank), rank)] = chosen * final_scale

    pick(0, rows[0])

    def step(pair, _):
        first = pair * 2
        mixed = multiplied(first, rows[0])
        pick(first + 1, rows[1])
        finish(first, mixed)
        mixed = multiplied(first + 1, rows[1])
        pick(lax.rem(first + 2, number), rows[0])
        finish(first + 1, mixed)
        return _

    lax.fori_loop(0, number // 2, step, 0)


def sampled(final_scale, mix, where, signs):
    rank, samples = signs.shape
    return pl.pallas_call(
        functools.partial(sample_kernel, final_scale),
        out_shape=jax.ShapeDtypeStruct((1, samples), F32),
        in_specs=[VMEM, SMEM, VMEM],
        out_specs=VMEM,
        scratch_shapes=[pltpu.VMEM((rank, 1, rank), F32)] * 2,
        compiler_params=limit(4),
        name="sampled",
    )(mix.reshape(-1, 1, rank), where, signs)


def shards(x, gg, gu, h, go, a_gate, b_gate, a_up, b_up, a_down, b_down, flags, index):
    x, go, gg, gu, h = [a[0, 0] for a in (x, go, gg, gu, h)]
    a_gate, b_gate, a_up, b_up, a_down, b_down = [
        a[0] for a in (a_gate, b_gate, a_up, b_up, a_down, b_down)
    ]
    count = lax.axis_size("coord")
    tokens, rank = x.shape[0], a_gate.shape[1]
    total = flags.shape[0] * count * lax.axis_size("ckpt")
    flags = flags.reshape(-1, rank)
    length = flags.shape[0]
    first = 3 * x.shape[1]
    block = min(256, length)
    aligned = x.shape[1] % block == 0 and gg.shape[0] % block == 0
    where = (index >> (rank.bit_length() - 1)) & (length - 1)
    where = (where & ~63) | (where & 7) << 3 | where >> 3 & 7
    stages = stages_of(count)
    rows = 16 * count * -(-3 * tokens // (16 * count))
    x, go, short = short_products(
        rows, stages[0], *[in_hbm(a) for a in (x, go, a_gate, a_up, b_down)]
    )
    gg, gu, h, long = long_products(
        rows, stages[0], *[in_hbm(a) for a in (gg, gu, h, b_gate, b_up, a_down)]
    )
    flags = after(long[0], flags)
    bits = (length * rank).bit_length() - 1
    ahead = (
        lambda ready: turn(x, go),
        lambda ready: signs_of(rank, bits, after(ready, index)),
    )
    ((x_t, go_t), signs), (short, long) = all_sums([short, long], stages, ahead)
    wide_mix = wide(aligned, block, first, stages[0], short, gg, gu, h, flags)
    final_scale = adapter_scale * float(total) ** -0.5
    mix = along_rows(aligned, block, stages[0], length, long, x_t, go_t, wide_mix, flags)
    contrib = sampled(final_scale, mix, where, signs)
    return total_over(contrib, count)


def solution(mesh):
    in_specs = (
        P("ckpt", "groups", None, "coord"),
        P("ckpt", "groups", "coord", None),
        P("ckpt", "groups", "coord", None),
        P("ckpt", "groups", "coord", None),
        P("ckpt", "groups", None, "coord"),
        P("ckpt", "coord", None),
        P("ckpt", "coord", None),
        P("ckpt", "coord", None),
        P("ckpt", "coord", None),
        P("ckpt", "coord", None),
        P("ckpt", "coord", None),
        P(("coord", "ckpt")),
        P(),
    )
    out_specs = P("groups", None)
    return jax.shard_map(shards, mesh=mesh, in_specs=in_specs, out_specs=out_specs, check_vma=False)
```

```python
import functools

import jax
import jax.numpy as jnp
from jax import lax
from jax.experimental import pallas as pl
from jax.experimental.pallas import tpu as pltpu
from jax.sharding import PartitionSpec as P

F32 = jnp.float32
BF16 = jnp.bfloat16
MIB = 2**20
adapter_scale = 2.0

ANY = pl.BlockSpec(memory_space=pl.ANY)
VMEM = pl.BlockSpec(memory_space=pltpu.VMEM)
SMEM = pl.BlockSpec(memory_space=pltpu.SMEM)


def limit(size):
    return pltpu.CompilerParams(vmem_limit_bytes=int(size * MIB))


def in_hbm(value):
    return pltpu.with_memory_space_constraint(value, pltpu.HBM)


def exchange(value, axis, apart):
    pairs = [(source, source ^ apart) for source in range(lax.axis_size(axis))]
    return lax.ppermute(value, axis, pairs)


def dot(left, right, contract):
    return lax.dot_general(left, right, (contract, ((), ())), preferred_element_type=F32)


def fetch(sources, targets, sems, cuts):
    groups = []
    slot = 0
    for source, target, cut in zip(sources, targets, cuts, strict=True):
        rows = source.shape[0]
        size = -(-rows // (cut * 16)) * 16
        group = []
        for begin in range(0, rows, size):
            end = min(begin + size, rows)
            copy = pltpu.make_async_copy(
                source.at[begin:end], target.at[begin:end], sems.at[slot]
            )
            copy.start()
            group.append(copy)
            slot += 1
        groups.append(group)

    def wait(which):
        for copy in groups[which]:
            copy.wait()

    return wait


def stages_of(count):
    stages, shift = [], 0
    while count > 1:
        radix = 2 if shift == 0 else min(4, count)
        stages.append((shift, radix))
        shift += radix.bit_length() - 1
        count //= radix
    return stages


def my_digit(stage):
    return (lax.axis_index("coord") >> stage[0]) & (stage[1] - 1)


def hand_out(table, stage, own, sends):
    digit = my_digit(stage)
    size = own.shape[0]
    own[...] = table[pl.ds(pl.multiple_of(digit * size, 16), size), :]
    for step, send in enumerate(sends, 1):
        begin = pl.multiple_of((digit ^ step) * size, 16)
        send[...] = table[pl.ds(begin, size), :].astype(BF16)


def put_together(own, others, stage, table):
    digit = my_digit(stage)
    size = own.shape[0]
    table[pl.ds(pl.multiple_of(digit * size, 16), size), :] = own[...]
    for step, other in enumerate(others[::-1], 1):
        table[pl.ds(pl.multiple_of((digit ^ step) * size, 16), size), :] = other[...]


def handed_out(rows, rank, stage):
    size = rows // stage[1]
    sends = [jax.ShapeDtypeStruct((size, rank), BF16)] * (stage[1] - 1)
    return [jax.ShapeDtypeStruct((size, rank), F32)] + sends


def fill(table, row):
    if table.shape[0] > row:
        table[row:, :] = jnp.zeros((table.shape[0] - row, table.shape[1]), F32)


def short_kernel(stage, cuts, *refs):
    ins, (x, go), (own, *sends), (a_gate, a_up, b_down, table, sems) = (
        refs[:5], refs[5:7], refs[7:-5], refs[-5:]
    )
    wait = fetch(ins, (x, go, a_gate, a_up, b_down), sems, cuts)
    for which in range(5):
        wait(which)
    tokens = x.shape[0]
    table[:tokens, :] = dot(x[...], a_gate[...], ((1,), (0,)))
    table[tokens : 2 * tokens, :] = dot(x[...], a_up[...], ((1,), (0,)))
    table[2 * tokens : 3 * tokens, :] = dot(go[...], b_down[...], ((1,), (0,)))
    fill(table, 3 * tokens)
    hand_out(table, stage, own, sends)


def short_products(rows, stage, *ins):
    rank = ins[2].shape[1]
    cuts = (2, 2, 1, 1, 1)
    shapes = [jax.ShapeDtypeStruct(a.shape, a.dtype) for a in ins[:2]]
    shapes = shapes + handed_out(rows, rank, stage)
    x, go, *sends = pl.pallas_call(
        functools.partial(short_kernel, stage, cuts),
        out_shape=shapes,
        in_specs=[ANY] * len(ins),
        out_specs=[VMEM] * len(shapes),
        scratch_shapes=[pltpu.VMEM(a.shape, a.dtype) for a in ins[2:]]
        + [pltpu.VMEM((rows, rank), F32), pltpu.SemaphoreType.DMA((sum(cuts),))],
        compiler_params=limit(4),
        cost_estimate=pl.CostEstimate(flops=10**8, bytes_accessed=6 * 10**6, transcendentals=0),
        name="short",
    )(*ins)
    return x, go, sends


def long_kernel(stage, cut, *refs):
    ins, held, (own, *sends), (*adapters, table, sems) = refs[:6], refs[6:9], refs[9:-5], refs[-5:]
    rank = table.shape[1]
    per = cut + 1
    waits = []

    def begin(slot):
        wait = fetch(
            (ins[3 + slot], ins[slot]),
            (adapters[slot], held[slot]),
            sems.at[slot * per : (slot + 1) * per],
            (1, cut),
        )
        waits.append(wait)

    begin(0)
    begin(1)
    row = 0
    for slot in range(3):
        waits[slot](0)
        adapter = adapters[slot][...].T
        waits[slot](1)
        if slot == 0:
            begin(2)
        value = dot(adapter, held[slot][...], ((1,), (0,)))
        for part in range(value.shape[1] // rank):
            table[row : row + rank, :] = value[:, part * rank : (part + 1) * rank]
            row += rank
    fill(table, row)
    hand_out(table, stage, own, sends)


def long_products(rows, stage, *ins):
    rank = ins[3].shape[1]
    cut = 4
    held = [jax.ShapeDtypeStruct(a.shape, a.dtype) for a in ins[:3]]
    shapes = held + handed_out(rows, rank, stage)
    outs = pl.pallas_call(
        functools.partial(long_kernel, stage, cut),
        out_shape=shapes,
        in_specs=[ANY] * 6,
        out_specs=[VMEM] * len(shapes),
        scratch_shapes=[pltpu.VMEM(a.shape, a.dtype) for a in ins[3:]]
        + [pltpu.VMEM((rows, rank), F32), pltpu.SemaphoreType.DMA((3 * (cut + 1),))],
        compiler_params=limit(6),
        cost_estimate=pl.CostEstimate(flops=10**9, bytes_accessed=8 * 10**6, transcendentals=0),
        name="long",
    )(*ins)
    return *outs[:3], outs[3:]


def add_kernel(following, count, *refs):
    total = refs[0][...]
    for got in refs[1 : 1 + count]:
        total = total + got[...].astype(F32)
    if following is None:
        refs[1 + count][...] = total.astype(BF16)
    else:
        outs, table = refs[1 + count : -1], refs[-1]
        table[...] = total
        hand_out(table, following, outs[0], outs[1:])


def add_up(own, got, following):
    if following is None:
        shapes, scratch = [jax.ShapeDtypeStruct(own.shape, BF16)], []
    else:
        shapes, scratch = handed_out(*own.shape, following), [pltpu.VMEM(own.shape, F32)]
    return pl.pallas_call(
        functools.partial(add_kernel, following, len(got)),
        out_shape=shapes,
        in_specs=[VMEM] * (1 + len(got)),
        out_specs=[VMEM] * len(shapes),
        scratch_shapes=scratch,
        compiler_params=limit(3),
        name="add_up",
    )(own, *got)


def join_kernel(stage, own, *refs):
    put_together(own, refs[:-1], stage, refs[-1])


def join(own, got, stage):
    return pl.pallas_call(
        functools.partial(join_kernel, stage),
        out_shape=jax.ShapeDtypeStruct((own.shape[0] * stage[1], own.shape[1]), BF16),
        in_specs=[VMEM] * (1 + len(got)),
        out_specs=VMEM,
        compiler_params=limit(3),
        name="join",
    )(own, *got)


def swap(sends, stage):
    return [
        exchange(sends[step - 1], "coord", step << stage[0]) for step in range(stage[1] - 1, 0, -1)
    ]


def after(first, second):
    return lax.optimization_barrier((first, second))[1]


def all_sums(halves, stages, ahead):
    beside = []
    owns = [half[0] for half in halves]
    sends = [half[1:] for half in halves]
    for stage, following in zip(stages, stages[1:] + [None], strict=True):
        got = [swap(send, stage) for send in sends]
        for i in range(len(owns)):
            own = after(owns[0], owns[i]) if i else owns[i]
            order = got[i][1:] + got[i][:1] if i else got[i]
            owns[i], *sends[i] = add_up(own, order, following)
    for stage in stages[:0:-1]:
        got = [swap([own] * (stage[1] - 1), stage) for own in owns]
        for i in range(len(owns)):
            own = after(owns[0], owns[i]) if i else owns[i]
            if stage is stages[1]:
                beside.append(ahead[i](owns[0]))
                own = after(beside[i], own)
            owns[i] = join(own, got[i], stage)
    return beside, [[own] + swap([own] * (stages[0][1] - 1), stages[0]) for own in owns]


def total_over(contrib, count):
    assert lax.axis_size("ckpt") == 2
    core = lax.axis_index("ckpt")
    total = contrib + exchange(contrib, "ckpt", 1)
    shift = 0
    while 1 << shift < count:
        radix = min(8, count >> shift)
        half = radix // 2
        terms = []
        for step in range(half):
            nearer, further = (step or half) << shift, (half + step) << shift
            pairs = [(2 * c + 1, 2 * (c ^ nearer)) for c in range(count)]
            pairs += [(2 * c, 2 * (c ^ further) + 1) for c in range(count)]
            got = lax.ppermute(total, ("coord", "ckpt"), pairs)
            terms.append(got if step else jnp.where(core == 0, total, got))
        while len(terms) > 1:
            terms = [a + b for a, b in zip(terms[::2], terms[1::2], strict=True)]
        total = terms[0] + exchange(terms[0], "ckpt", 1)
        shift += radix.bit_length() - 1
    return total


def turn_kernel(x, go, x_t, go_t):
    x_t[...] = x[...].T
    go_t[...] = go[...].T


def turn(x, go):
    shape = jax.ShapeDtypeStruct(x.shape[::-1], BF16)
    return pl.pallas_call(
        turn_kernel,
        out_shape=[shape, shape],
        in_specs=[VMEM, VMEM],
        out_specs=[VMEM, VMEM],
        compiler_params=limit(4),
        name="turn",
    )(x, go)


def butterflies(blocks):
    half = 1
    while half < len(blocks):
        done = list(blocks)
        for low in range(len(blocks)):
            if not low & half:
                a, b = blocks[low], blocks[low | half]
                if b is None:
                    done[low], done[low | half] = a, a
                else:
                    done[low], done[low | half] = a + b, a - b
        blocks, half = done, half * 2
    return blocks


def along_block(value, out, row):
    size = value.shape[0]
    tiles = butterflies([value[i : i + 8, :] for i in range(0, size, 8)])
    for i, tile in enumerate(tiles):
        out[row + 8 * i : row + 8 * i + 8, :] = tile
    for begin in range(row, row + size, 64):
        tiles = butterflies([out[pl.ds(begin + j, 8, stride=8), :] for j in range(8)])
        for j, tile in enumerate(tiles):
            out[begin + 8 * j : begin + 8 * j + 8, :] = tile


def signed(value, flags, row):
    return jnp.where(flags[row : row + value.shape[0], :] == 0, value, -value)


def keep(aligned, value, flags, row, out):
    value = signed(value, flags, row)
    if aligned:
        along_block(value, out, row)
    else:
        out[row : row + value.shape[0], :] = value


def wide_kernel(aligned, block, first, stage, *refs):
    parts, refs = refs[: stage[1]], refs[stage[1] :]
    gg, gu, h, flags, out, table = refs
    put_together(parts[0], parts[1:], stage, table)
    tokens = gg.shape[1]
    flags = flags.at[first : first + out.shape[0]]
    row = 0
    for slot, piece in enumerate((gg, gu, h)):
        product = table[slot * tokens : (slot + 1) * tokens, :]
        size = block if aligned else piece.shape[0]
        for begin in range(0, piece.shape[0], size):
            value = dot(piece[begin : begin + size, :], product, ((1,), (0,)))
            keep(aligned, value, flags, row, out)
            row += size


def wide(aligned, block, first, stage, parts, gg, gu, h, flags):
    rank = flags.shape[1]
    return pl.pallas_call(
        functools.partial(wide_kernel, aligned, block, first, stage),
        out_shape=jax.ShapeDtypeStruct((3 * gg.shape[0], rank), F32),
        in_specs=[VMEM] * (len(parts) + 4),
        out_specs=VMEM,
        scratch_shapes=[pltpu.VMEM((parts[0].shape[0] * stage[1], rank), BF16)],
        compiler_params=limit(6),
        cost_estimate=pl.CostEstimate(flops=10**9, bytes_accessed=10**7, transcendentals=0),
        name="wide",
    )(*parts, gg, gu, h, flags)


def rows_kernel(aligned, block, stage, *refs):
    parts, refs = refs[: stage[1]], refs[stage[1] :]
    x_t, go_t, wide_mix, flags, mix, table = refs
    width, tokens = x_t.shape
    first = 3 * width
    length, rank = mix.shape
    put_together(parts[0], parts[1:], stage, table)
    product = [
        jnp.concatenate(
            [table[slot * tokens + part : slot * tokens + part + rank, :] for part in range(0, tokens, rank)],
            axis=1,
        )
        for slot in range(3)
    ]
    size = block if aligned else width
    both = jnp.concatenate(product[:2], axis=0)
    for begin in range(0, width, size):
        value = dot(x_t[begin : begin + size, :], both, ((1,), (1,)))
        keep(aligned, value[:, :rank], flags, begin, mix)
        keep(aligned, value[:, rank:], flags, width + begin, mix)
        value = dot(go_t[begin : begin + size, :], product[2], ((1,), (1,)))
        keep(aligned, value, flags, 2 * width + begin, mix)
    filled = first + wide_mix.shape[0]
    if not aligned:
        mix[first:filled, :] = wide_mix[...]
        mix[filled:, :] = jnp.zeros((length - filled, rank), F32)
        for begin in range(0, length, block):
            along_block(mix[begin : begin + block, :], mix, begin)
    number = length // block
    full = -(-filled // block)

    def load(i, begin):
        if not aligned or i * block < first:
            return mix[pl.ds(i * block + begin, 8), :]
        if i >= full:
            return None
        return wide_mix[pl.ds(i * block - first + begin, 8), :]

    for begin in range(0, block, 8):
        for i, value in enumerate(butterflies([load(i, begin) for i in range(number)])):
            mix[i * block + begin : i * block + begin + 8, :] = value


def along_rows(aligned, block, stage, length, parts, x_t, go_t, wide_mix, flags):
    rank = flags.shape[1]
    return pl.pallas_call(
        functools.partial(rows_kernel, aligned, block, stage),
        out_shape=jax.ShapeDtypeStruct((length, rank), F32),
        in_specs=[VMEM] * (len(parts) + 4),
        out_specs=VMEM,
        scratch_shapes=[pltpu.VMEM((parts[0].shape[0] * stage[1], rank), BF16)],
        compiler_params=limit(6),
        name="along_rows",
    )(*parts, x_t, go_t, wide_mix, flags)


def parity(value):
    for fold in (16, 8, 4, 2, 1):
        value = value ^ (value >> fold)
    return value & 1


def signs_kernel(bits, lanes, out):
    rank = out.shape[0]
    device = lax.axis_index("coord") * lax.axis_size("ckpt") + lax.axis_index("ckpt")
    index = lanes[...]

    def sign(bit):
        return (1 - 2 * (bit & 1)).astype(F32)

    low = lax.broadcasted_iota(jnp.int32, (8, index.shape[1]), 0)
    tile = sign(parity((index >> bits) & device))
    for bit in range(3):
        tile = tile * jnp.where((low >> bit & 1) == 0, 1.0, sign(index >> bit))
    tiles = [tile]
    for bit in range(3, rank.bit_length() - 1):
        tiles = tiles + [tile * sign(index >> bit) for tile in tiles]
    out[...] = jnp.concatenate(tiles, axis=0).astype(BF16)


def signs_of(rank, bits, index):
    samples = index.shape[0]
    return pl.pallas_call(
        functools.partial(signs_kernel, bits),
        out_shape=jax.ShapeDtypeStruct((rank, samples), BF16),
        in_specs=[VMEM],
        out_specs=VMEM,
        compiler_params=limit(10),
        name="signs",
    )(index.reshape(1, samples))


def pick_kernel(mix, where, rows):
    samples, rank = rows.shape
    group = min(128, samples)
    unroll = min(2, samples // group)
    place = lax.broadcasted_iota(jnp.int32, (8, rank), 0)
    masks = [place == i for i in range(8)]

    def picked_tile(sources, begin):
        tile = None
        for i in range(8):
            row = jnp.broadcast_to(mix[pl.ds(sources[begin + i], 1), :], (8, rank))
            tile = row if tile is None else jnp.where(masks[i], row, tile)
        return tile

    def pick(step, _):
        for part in range(unroll):
            span = pl.ds(pl.multiple_of((step * unroll + part) * group, group), group)
            sources, targets = where.at[span], rows.at[span]
            tiles = [picked_tile(sources, begin) for begin in range(0, group, 8)]
            for i, tile in enumerate(tiles):
                targets[8 * i : 8 * i + 8, :] = tile
        return _

    lax.fori_loop(0, samples // (group * unroll), pick, 0)


def picked(mix, where):
    return pl.pallas_call(
        pick_kernel,
        out_shape=jax.ShapeDtypeStruct((where.shape[0], mix.shape[1]), F32),
        in_specs=[VMEM, SMEM],
        out_specs=VMEM,
        compiler_params=limit(4),
        name="picked",
    )(mix, where)


def sample_kernel(final_scale, rows, signs, out):
    samples, rank = rows.shape
    shape = (rank, rank)
    diagonal = lax.broadcasted_iota(jnp.int32, shape, 0) == lax.broadcasted_iota(jnp.int32, shape, 1)
    for begin in range(0, samples, rank):
        value = rows[begin : begin + rank, :]
        high = value.astype(BF16)
        low = (value - high.astype(F32)).astype(BF16)
        sign = signs[:, begin : begin + rank]
        mixed = dot(
            jnp.concatenate([high, low], axis=1), jnp.concatenate([sign, sign], axis=0), ((1,), (0,))
        )
        chosen = jnp.sum(jnp.where(diagonal, mixed, 0.0), axis=0, keepdims=True)
        out[:, begin : begin + rank] = chosen * final_scale


def sampled(final_scale, rows, signs):
    return pl.pallas_call(
        functools.partial(sample_kernel, final_scale),
        out_shape=jax.ShapeDtypeStruct((1, rows.shape[0]), F32),
        in_specs=[VMEM, VMEM],
        out_specs=VMEM,
        compiler_params=limit(4),
        name="sampled",
    )(rows, signs)


def shards(x, gg, gu, h, go, a_gate, b_gate, a_up, b_up, a_down, b_down, flags, index):
    x, go, gg, gu, h = [a[0, 0] for a in (x, go, gg, gu, h)]
    a_gate, b_gate, a_up, b_up, a_down, b_down = [
        a[0] for a in (a_gate, b_gate, a_up, b_up, a_down, b_down)
    ]
    count = lax.axis_size("coord")
    tokens, rank = x.shape[0], a_gate.shape[1]
    total = flags.shape[0] * count * lax.axis_size("ckpt")
    flags = flags.reshape(-1, rank)
    length = flags.shape[0]
    first = 3 * x.shape[1]
    block = min(256, length)
    aligned = x.shape[1] % block == 0 and gg.shape[0] % block == 0
    where = (index >> (rank.bit_length() - 1)) & (length - 1)
    where = (where & ~63) | (where & 7) << 3 | where >> 3 & 7
    stages = stages_of(count)
    rows = 16 * count * -(-3 * tokens // (16 * count))
    x, go, short = short_products(
        rows, stages[0], *[in_hbm(a) for a in (x, go, a_gate, a_up, b_down)]
    )
    gg, gu, h, long = long_products(
        rows, stages[0], *[in_hbm(a) for a in (gg, gu, h, b_gate, b_up, a_down)]
    )
    flags = after(long[0], flags)
    bits = (length * rank).bit_length() - 1
    ahead = (
        lambda ready: turn(x, go),
        lambda ready: signs_of(rank, bits, after(ready, index)),
    )
    ((x_t, go_t), signs), (short, long) = all_sums([short, long], stages, ahead)
    wide_mix = wide(aligned, block, first, stages[0], short, gg, gu, h, flags)
    final_scale = adapter_scale * float(total) ** -0.5
    mix = along_rows(aligned, block, stages[0], length, long, x_t, go_t, wide_mix, flags)
    contrib = sampled(final_scale, picked(mix, where), signs)
    return total_over(contrib, count)


def solution(mesh):
    in_specs = (
        P("ckpt", "groups", None, "coord"),
        P("ckpt", "groups", "coord", None),
        P("ckpt", "groups", "coord", None),
        P("ckpt", "groups", "coord", None),
        P("ckpt", "groups", None, "coord"),
        P("ckpt", "coord", None),
        P("ckpt", "coord", None),
        P("ckpt", "coord", None),
        P("ckpt", "coord", None),
        P("ckpt", "coord", None),
        P("ckpt", "coord", None),
        P(("coord", "ckpt")),
        P(),
    )
    out_specs = P("groups", None)
    return jax.shard_map(shards, mesh=mesh, in_specs=in_specs, out_specs=out_specs, check_vma=False)
```

```python
import functools

import jax
import jax.numpy as jnp
from jax import lax
from jax.experimental import pallas as pl
from jax.experimental.pallas import tpu as pltpu
from jax.sharding import PartitionSpec as P

F32 = jnp.float32
BF16 = jnp.bfloat16
MIB = 2**20
adapter_scale = 2.0

ANY = pl.BlockSpec(memory_space=pl.ANY)
VMEM = pl.BlockSpec(memory_space=pltpu.VMEM)
SMEM = pl.BlockSpec(memory_space=pltpu.SMEM)


def limit(size):
    return pltpu.CompilerParams(vmem_limit_bytes=int(size * MIB))


def in_hbm(value):
    return pltpu.with_memory_space_constraint(value, pltpu.HBM)


def exchange(value, axis, apart):
    pairs = [(source, source ^ apart) for source in range(lax.axis_size(axis))]
    return lax.ppermute(value, axis, pairs)


def dot(left, right, contract):
    return lax.dot_general(left, right, (contract, ((), ())), preferred_element_type=F32)


def fetch(sources, targets, sems, cuts):
    groups = []
    slot = 0
    for source, target, cut in zip(sources, targets, cuts, strict=True):
        rows = source.shape[0]
        size = -(-rows // (cut * 16)) * 16
        group = []
        for begin in range(0, rows, size):
            end = min(begin + size, rows)
            copy = pltpu.make_async_copy(
                source.at[begin:end], target.at[begin:end], sems.at[slot]
            )
            copy.start()
            group.append(copy)
            slot += 1
        groups.append(group)

    def wait(which):
        for copy in groups[which]:
            copy.wait()

    return wait


def stages_of(count):
    stages, shift = [], 0
    while count > 1:
        radix = 2 if shift == 0 else min(4, count)
        stages.append((shift, radix))
        shift += radix.bit_length() - 1
        count //= radix
    return stages


def my_digit(stage):
    return (lax.axis_index("coord") >> stage[0]) & (stage[1] - 1)


def hand_out(table, stage, own, sends):
    digit = my_digit(stage)
    size = own.shape[0]
    own[...] = table[pl.ds(pl.multiple_of(digit * size, 16), size), :]
    for step, send in enumerate(sends, 1):
        begin = pl.multiple_of((digit ^ step) * size, 16)
        send[...] = table[pl.ds(begin, size), :].astype(BF16)


def put_together(own, others, stage, table):
    digit = my_digit(stage)
    size = own.shape[0]
    table[pl.ds(pl.multiple_of(digit * size, 16), size), :] = own[...]
    for step, other in enumerate(others[::-1], 1):
        table[pl.ds(pl.multiple_of((digit ^ step) * size, 16), size), :] = other[...]


def handed_out(rows, rank, stage):
    size = rows // stage[1]
    sends = [jax.ShapeDtypeStruct((size, rank), BF16)] * (stage[1] - 1)
    return [jax.ShapeDtypeStruct((size, rank), F32)] + sends


def fill(table, row):
    if table.shape[0] > row:
        table[row:, :] = jnp.zeros((table.shape[0] - row, table.shape[1]), F32)


def short_kernel(stage, cuts, *refs):
    ins, (x, go), (own, *sends), (a_gate, a_up, b_down, table, sems) = (
        refs[:5], refs[5:7], refs[7:-5], refs[-5:]
    )
    wait = fetch(ins, (x, go, a_gate, a_up, b_down), sems, cuts)
    tokens, rank = x.shape[0], table.shape[1]
    for which in (0, 2, 3):
        wait(which)
    both = dot(x[...], jnp.concatenate([a_gate[...], a_up[...]], axis=1), ((1,), (0,)))
    table[:tokens, :] = both[:, :rank]
    table[tokens : 2 * tokens, :] = both[:, rank:]
    for which in (1, 4):
        wait(which)
    table[2 * tokens : 3 * tokens, :] = dot(go[...], b_down[...], ((1,), (0,)))
    fill(table, 3 * tokens)
    hand_out(table, stage, own, sends)


def short_products(rows, stage, *ins):
    rank = ins[2].shape[1]
    cuts = (2, 2, 1, 1, 1)
    shapes = [jax.ShapeDtypeStruct(a.shape, a.dtype) for a in ins[:2]]
    shapes = shapes + handed_out(rows, rank, stage)
    x, go, *sends = pl.pallas_call(
        functools.partial(short_kernel, stage, cuts),
        out_shape=shapes,
        in_specs=[ANY] * len(ins),
        out_specs=[VMEM] * len(shapes),
        scratch_shapes=[pltpu.VMEM(a.shape, a.dtype) for a in ins[2:]]
        + [pltpu.VMEM((rows, rank), F32), pltpu.SemaphoreType.DMA((sum(cuts),))],
        compiler_params=limit(4),
        cost_estimate=pl.CostEstimate(flops=10**8, bytes_accessed=6 * 10**6, transcendentals=0),
        name="short",
    )(*ins)
    return x, go, sends


def long_kernel(stage, cut, *refs):
    ins, held, (own, *sends), (*adapters, table, sems) = refs[:6], refs[6:9], refs[9:-5], refs[-5:]
    rank = table.shape[1]
    per = cut + 1
    waits = []

    def begin(slot):
        wait = fetch(
            (ins[3 + slot], ins[slot]),
            (adapters[slot], held[slot]),
            sems.at[slot * per : (slot + 1) * per],
            (1, cut),
        )
        waits.append(wait)

    begin(0)
    begin(1)
    row = 0
    for slot in range(3):
        waits[slot](0)
        adapter = adapters[slot][...].T
        waits[slot](1)
        if slot == 0:
            begin(2)
        value = dot(adapter, held[slot][...], ((1,), (0,)))
        for part in range(value.shape[1] // rank):
            table[row : row + rank, :] = value[:, part * rank : (part + 1) * rank]
            row += rank
    fill(table, row)
    hand_out(table, stage, own, sends)


def long_products(rows, stage, *ins):
    rank = ins[3].shape[1]
    cut = 4
    held = [jax.ShapeDtypeStruct(a.shape, a.dtype) for a in ins[:3]]
    shapes = held + handed_out(rows, rank, stage)
    outs = pl.pallas_call(
        functools.partial(long_kernel, stage, cut),
        out_shape=shapes,
        in_specs=[ANY] * 6,
        out_specs=[VMEM] * len(shapes),
        scratch_shapes=[pltpu.VMEM(a.shape, a.dtype) for a in ins[3:]]
        + [pltpu.VMEM((rows, rank), F32), pltpu.SemaphoreType.DMA((3 * (cut + 1),))],
        compiler_params=limit(6),
        cost_estimate=pl.CostEstimate(flops=10**9, bytes_accessed=8 * 10**6, transcendentals=0),
        name="long",
    )(*ins)
    return *outs[:3], outs[3:]


def add_kernel(following, count, *refs):
    total = refs[0][...]
    for got in refs[1 : 1 + count]:
        total = total + got[...].astype(F32)
    if following is None:
        refs[1 + count][...] = total.astype(BF16)
    else:
        outs, table = refs[1 + count : -1], refs[-1]
        table[...] = total
        hand_out(table, following, outs[0], outs[1:])


def add_up(own, got, following):
    if following is None:
        shapes, scratch = [jax.ShapeDtypeStruct(own.shape, BF16)], []
    else:
        shapes, scratch = handed_out(*own.shape, following), [pltpu.VMEM(own.shape, F32)]
    return pl.pallas_call(
        functools.partial(add_kernel, following, len(got)),
        out_shape=shapes,
        in_specs=[VMEM] * (1 + len(got)),
        out_specs=[VMEM] * len(shapes),
        scratch_shapes=scratch,
        compiler_params=limit(3),
        name="add_up",
    )(own, *got)


def join_kernel(stage, own, *refs):
    put_together(own, refs[:-1], stage, refs[-1])


def join(own, got, stage):
    return pl.pallas_call(
        functools.partial(join_kernel, stage),
        out_shape=jax.ShapeDtypeStruct((own.shape[0] * stage[1], own.shape[1]), BF16),
        in_specs=[VMEM] * (1 + len(got)),
        out_specs=VMEM,
        compiler_params=limit(3),
        name="join",
    )(own, *got)


def swap(sends, stage):
    return [
        exchange(sends[step - 1], "coord", step << stage[0]) for step in range(stage[1] - 1, 0, -1)
    ]


def after(first, second):
    return lax.optimization_barrier((first, second))[1]


def all_sums(halves, stages, ahead):
    beside = []
    owns = [half[0] for half in halves]
    sends = [half[1:] for half in halves]
    for stage, following in zip(stages, stages[1:] + [None], strict=True):
        got = [swap(send, stage) for send in sends]
        for i in range(len(owns)):
            own = after(owns[0], owns[i]) if i else owns[i]
            order = got[i][1:] + got[i][:1] if i else got[i]
            owns[i], *sends[i] = add_up(own, order, following)
    for stage in stages[:0:-1]:
        got = [swap([own] * (stage[1] - 1), stage) for own in owns]
        for i in range(len(owns)):
            own = after(owns[0], owns[i]) if i else owns[i]
            if stage is stages[1]:
                beside.append(ahead[i](owns[0]))
                own = after(beside[i], own)
            owns[i] = join(own, got[i], stage)
    return beside, [[own] + swap([own] * (stages[0][1] - 1), stages[0]) for own in owns]


def total_over(contrib, stages):
    assert lax.axis_size("ckpt") == 2
    count = lax.axis_size("coord")
    core = lax.axis_index("ckpt")
    total = contrib + exchange(contrib, "ckpt", 1)

    def from_other_core(nearer, further):
        pairs = [(2 * c + 1, 2 * (c ^ nearer)) for c in range(count)]
        pairs += [(2 * c, 2 * (c ^ further) + 1) for c in range(count)]
        return lax.ppermute(total, ("coord", "ckpt"), pairs)

    for shift, radix in stages:
        half = radix // 2
        if half == 1:
            total = total + from_other_core(1 << shift, 1 << shift)
            continue
        terms = []
        for step in range(half):
            got = from_other_core((step or half) << shift, (half + step) << shift)
            terms.append(got if step else jnp.where(core == 0, total, got))
        while len(terms) > 1:
            terms = [a + b for a, b in zip(terms[::2], terms[1::2], strict=True)]
        total = terms[0] + exchange(terms[0], "ckpt", 1)
    return total


def turn_kernel(x, go, x_t, go_t):
    x_t[...] = x[...].T
    go_t[...] = go[...].T


def turn(x, go):
    shape = jax.ShapeDtypeStruct(x.shape[::-1], BF16)
    return pl.pallas_call(
        turn_kernel,
        out_shape=[shape, shape],
        in_specs=[VMEM, VMEM],
        out_specs=[VMEM, VMEM],
        compiler_params=limit(4),
        name="turn",
    )(x, go)


def butterflies(blocks):
    half = 1
    while half < len(blocks):
        done = list(blocks)
        for low in range(len(blocks)):
            if not low & half:
                a, b = blocks[low], blocks[low | half]
                if b is None:
                    done[low], done[low | half] = a, a
                else:
                    done[low], done[low | half] = a + b, a - b
        blocks, half = done, half * 2
    return blocks


def along_block(value, out, row):
    size = value.shape[0]
    tiles = butterflies([value[i : i + 8, :] for i in range(0, size, 8)])
    for i, tile in enumerate(tiles):
        out[row + 8 * i : row + 8 * i + 8, :] = tile
    for begin in range(row, row + size, 64):
        tiles = butterflies([out[pl.ds(begin + j, 8, stride=8), :] for j in range(8)])
        for j, tile in enumerate(tiles):
            out[begin + 8 * j : begin + 8 * j + 8, :] = tile


def signed(value, flags, row):
    return jnp.where(flags[row : row + value.shape[0], :] == 0, value, -value)


def keep(aligned, value, flags, row, out):
    value = signed(value, flags, row)
    if aligned:
        along_block(value, out, row)
    else:
        out[row : row + value.shape[0], :] = value


def wide_kernel(aligned, block, first, stage, *refs):
    parts, refs = refs[: stage[1]], refs[stage[1] :]
    gg, gu, h, flags, out, table = refs
    put_together(parts[0], parts[1:], stage, table)
    tokens = gg.shape[1]
    flags = flags.at[first : first + out.shape[0]]
    row = 0
    for slot, piece in enumerate((gg, gu, h)):
        product = table[slot * tokens : (slot + 1) * tokens, :]
        size = block if aligned else piece.shape[0]
        for begin in range(0, piece.shape[0], size):
            value = dot(piece[begin : begin + size, :], product, ((1,), (0,)))
            keep(aligned, value, flags, row, out)
            row += size


def wide(aligned, block, first, stage, parts, gg, gu, h, flags):
    rank = flags.shape[1]
    return pl.pallas_call(
        functools.partial(wide_kernel, aligned, block, first, stage),
        out_shape=jax.ShapeDtypeStruct((3 * gg.shape[0], rank), F32),
        in_specs=[VMEM] * (len(parts) + 4),
        out_specs=VMEM,
        scratch_shapes=[pltpu.VMEM((parts[0].shape[0] * stage[1], rank), BF16)],
        compiler_params=limit(6),
        cost_estimate=pl.CostEstimate(flops=10**9, bytes_accessed=10**7, transcendentals=0),
        name="wide",
    )(*parts, gg, gu, h, flags)


def rows_kernel(aligned, block, stage, *refs):
    parts, refs = refs[: stage[1]], refs[stage[1] :]
    x_t, go_t, wide_mix, flags, mix, table = refs
    width, tokens = x_t.shape
    first = 3 * width
    length, rank = mix.shape
    put_together(parts[0], parts[1:], stage, table)
    product = [
        jnp.concatenate(
            [table[slot * tokens + part : slot * tokens + part + rank, :] for part in range(0, tokens, rank)],
            axis=1,
        )
        for slot in range(3)
    ]
    size = block if aligned else width
    both = jnp.concatenate(product[:2], axis=0)
    for begin in range(0, width, size):
        value = dot(x_t[begin : begin + size, :], both, ((1,), (1,)))
        keep(aligned, value[:, :rank], flags, begin, mix)
        keep(aligned, value[:, rank:], flags, width + begin, mix)
        value = dot(go_t[begin : begin + size, :], product[2], ((1,), (1,)))
        keep(aligned, value, flags, 2 * width + begin, mix)
    filled = first + wide_mix.shape[0]
    if not aligned:
        mix[first:filled, :] = wide_mix[...]
        mix[filled:, :] = jnp.zeros((length - filled, rank), F32)
        for begin in range(0, length, block):
            along_block(mix[begin : begin + block, :], mix, begin)
    number = length // block
    full = -(-filled // block)

    def load(i, begin):
        if not aligned or i * block < first:
            return mix[pl.ds(i * block + begin, 8), :]
        if i >= full:
            return None
        return wide_mix[pl.ds(i * block - first + begin, 8), :]

    for begin in range(0, block, 8):
        for i, value in enumerate(butterflies([load(i, begin) for i in range(number)])):
            mix[i * block + begin : i * block + begin + 8, :] = value


def along_rows(aligned, block, stage, length, parts, x_t, go_t, wide_mix, flags):
    rank = flags.shape[1]
    return pl.pallas_call(
        functools.partial(rows_kernel, aligned, block, stage),
        out_shape=jax.ShapeDtypeStruct((length, rank), F32),
        in_specs=[VMEM] * (len(parts) + 4),
        out_specs=VMEM,
        scratch_shapes=[pltpu.VMEM((parts[0].shape[0] * stage[1], rank), BF16)],
        compiler_params=limit(6),
        name="along_rows",
    )(*parts, x_t, go_t, wide_mix, flags)


def parity(value):
    for fold in (16, 8, 4, 2, 1):
        value = value ^ (value >> fold)
    return value & 1


def signs_kernel(bits, lanes, out):
    rank = out.shape[0]
    device = lax.axis_index("coord") * lax.axis_size("ckpt") + lax.axis_index("ckpt")
    index = lanes[...]

    def sign(bit):
        return (1 - 2 * (bit & 1)).astype(F32)

    low = lax.broadcasted_iota(jnp.int32, (8, index.shape[1]), 0)
    tile = sign(parity((index >> bits) & device))
    for bit in range(3):
        tile = tile * jnp.where((low >> bit & 1) == 0, 1.0, sign(index >> bit))
    tiles = [tile]
    for bit in range(3, rank.bit_length() - 1):
        tiles = tiles + [tile * sign(index >> bit) for tile in tiles]
    out[...] = jnp.concatenate(tiles, axis=0).astype(BF16)


def signs_of(rank, bits, index):
    samples = index.shape[0]
    return pl.pallas_call(
        functools.partial(signs_kernel, bits),
        out_shape=jax.ShapeDtypeStruct((rank, samples), BF16),
        in_specs=[VMEM],
        out_specs=VMEM,
        compiler_params=limit(10),
        name="signs",
    )(index.reshape(1, samples))


def pick_kernel(mix, where, rows):
    samples, rank = rows.shape
    group = min(128, samples)
    unroll = min(2, samples // group)
    place = lax.broadcasted_iota(jnp.int32, (8, rank), 0)
    masks = [place == i for i in range(8)]

    def picked_tile(sources, begin):
        tile = None
        for i in range(8):
            row = jnp.broadcast_to(mix[pl.ds(sources[begin + i], 1), :], (8, rank))
            tile = row if tile is None else jnp.where(masks[i], row, tile)
        return tile

    def pick(step, _):
        for part in range(unroll):
            span = pl.ds(pl.multiple_of((step * unroll + part) * group, group), group)
            sources, targets = where.at[span], rows.at[span]
            tiles = [picked_tile(sources, begin) for begin in range(0, group, 8)]
            for i, tile in enumerate(tiles):
                targets[8 * i : 8 * i + 8, :] = tile
        return _

    lax.fori_loop(0, samples // (group * unroll), pick, 0)


def picked(mix, where):
    return pl.pallas_call(
        pick_kernel,
        out_shape=jax.ShapeDtypeStruct((where.shape[0], mix.shape[1]), F32),
        in_specs=[VMEM, SMEM],
        out_specs=VMEM,
        compiler_params=limit(4),
        name="picked",
    )(mix, where)


def sample_kernel(final_scale, rows, signs, out):
    samples, rank = rows.shape
    shape = (rank, rank)
    diagonal = lax.broadcasted_iota(jnp.int32, shape, 0) == lax.broadcasted_iota(jnp.int32, shape, 1)
    for begin in range(0, samples, rank):
        value = rows[begin : begin + rank, :]
        high = value.astype(BF16)
        low = (value - high.astype(F32)).astype(BF16)
        sign = signs[:, begin : begin + rank]
        mixed = dot(
            jnp.concatenate([high, low], axis=1), jnp.concatenate([sign, sign], axis=0), ((1,), (0,))
        )
        chosen = jnp.sum(jnp.where(diagonal, mixed, 0.0), axis=0, keepdims=True)
        out[:, begin : begin + rank] = chosen * final_scale


def sampled(final_scale, rows, signs):
    return pl.pallas_call(
        functools.partial(sample_kernel, final_scale),
        out_shape=jax.ShapeDtypeStruct((1, rows.shape[0]), F32),
        in_specs=[VMEM, VMEM],
        out_specs=VMEM,
        compiler_params=limit(4),
        name="sampled",
    )(rows, signs)


def shards(x, gg, gu, h, go, a_gate, b_gate, a_up, b_up, a_down, b_down, flags, index):
    x, go, gg, gu, h = [a[0, 0] for a in (x, go, gg, gu, h)]
    a_gate, b_gate, a_up, b_up, a_down, b_down = [
        a[0] for a in (a_gate, b_gate, a_up, b_up, a_down, b_down)
    ]
    count = lax.axis_size("coord")
    tokens, rank = x.shape[0], a_gate.shape[1]
    total = flags.shape[0] * count * lax.axis_size("ckpt")
    flags = flags.reshape(-1, rank)
    length = flags.shape[0]
    first = 3 * x.shape[1]
    block = min(256, length)
    aligned = x.shape[1] % block == 0 and gg.shape[0] % block == 0
    where = (index >> (rank.bit_length() - 1)) & (length - 1)
    where = (where & ~63) | (where & 7) << 3 | where >> 3 & 7
    stages = stages_of(count)
    rows = 16 * count * -(-3 * tokens // (16 * count))
    x, go, short = short_products(
        rows, stages[0], *[in_hbm(a) for a in (x, go, a_gate, a_up, b_down)]
    )
    gg, gu, h, long = long_products(
        rows, stages[0], *[in_hbm(a) for a in (gg, gu, h, b_gate, b_up, a_down)]
    )
    flags = after(long[0], flags)
    bits = (length * rank).bit_length() - 1
    ahead = (
        lambda ready: turn(x, go),
        lambda ready: signs_of(rank, bits, after(ready, index)),
    )
    ((x_t, go_t), signs), (short, long) = all_sums([short, long], stages, ahead)
    wide_mix = wide(aligned, block, first, stages[0], short, gg, gu, h, flags)
    final_scale = adapter_scale * float(total) ** -0.5
    mix = along_rows(aligned, block, stages[0], length, long, x_t, go_t, wide_mix, flags)
    contrib = sampled(final_scale, picked(mix, where), signs)
    return total_over(contrib, stages)


def solution(mesh):
    in_specs = (
        P("ckpt", "groups", None, "coord"),
        P("ckpt", "groups", "coord", None),
        P("ckpt", "groups", "coord", None),
        P("ckpt", "groups", "coord", None),
        P("ckpt", "groups", None, "coord"),
        P("ckpt", "coord", None),
        P("ckpt", "coord", None),
        P("ckpt", "coord", None),
        P("ckpt", "coord", None),
        P("ckpt", "coord", None),
        P("ckpt", "coord", None),
        P(("coord", "ckpt")),
        P(),
    )
    out_specs = P("groups", None)
    return jax.shard_map(shards, mesh=mesh, in_specs=in_specs, out_specs=out_specs, check_vma=False)
```

```python
import functools

import jax
import jax.numpy as jnp
from jax import lax
from jax.experimental import pallas as pl
from jax.experimental.pallas import tpu as pltpu
from jax.sharding import PartitionSpec as P

F32 = jnp.float32
BF16 = jnp.bfloat16
MIB = 2**20
adapter_scale = 2.0

ANY = pl.BlockSpec(memory_space=pl.ANY)
VMEM = pl.BlockSpec(memory_space=pltpu.VMEM)
SMEM = pl.BlockSpec(memory_space=pltpu.SMEM)


def limit(size):
    return pltpu.CompilerParams(vmem_limit_bytes=int(size * MIB))


def in_hbm(value):
    return pltpu.with_memory_space_constraint(value, pltpu.HBM)


def exchange(value, axis, apart):
    pairs = [(source, source ^ apart) for source in range(lax.axis_size(axis))]
    return lax.ppermute(value, axis, pairs)


def dot(left, right, contract):
    return lax.dot_general(left, right, (contract, ((), ())), preferred_element_type=F32)


def fetch(sources, targets, sems, cuts):
    groups = []
    slot = 0
    for source, target, cut in zip(sources, targets, cuts, strict=True):
        rows = source.shape[0]
        size = -(-rows // (cut * 16)) * 16
        group = []
        for begin in range(0, rows, size):
            end = min(begin + size, rows)
            copy = pltpu.make_async_copy(
                source.at[begin:end], target.at[begin:end], sems.at[slot]
            )
            copy.start()
            group.append(copy)
            slot += 1
        groups.append(group)

    def wait(which):
        for copy in groups[which]:
            copy.wait()

    return wait


def stages_of(count):
    stages, shift = [], 0
    while count > 1:
        radix = 2 if shift == 0 else min(4, count)
        stages.append((shift, radix))
        shift += radix.bit_length() - 1
        count //= radix
    return stages


def my_digit(stage):
    return (lax.axis_index("coord") >> stage[0]) & (stage[1] - 1)


def hand_out(table, stage, own, sends):
    digit = my_digit(stage)
    size = own.shape[0]
    own[...] = table[pl.ds(pl.multiple_of(digit * size, 16), size), :]
    for step, send in enumerate(sends, 1):
        begin = pl.multiple_of((digit ^ step) * size, 16)
        send[...] = table[pl.ds(begin, size), :].astype(BF16)


def put_together(own, others, stage, table):
    digit = my_digit(stage)
    size = own.shape[0]
    table[pl.ds(pl.multiple_of(digit * size, 16), size), :] = own[...]
    for step, other in enumerate(others, 1):
        table[pl.ds(pl.multiple_of((digit ^ step) * size, 16), size), :] = other[...]


def handed_out(rows, rank, stage):
    size = rows // stage[1]
    sends = [jax.ShapeDtypeStruct((size, rank), BF16)] * (stage[1] - 1)
    return [jax.ShapeDtypeStruct((size, rank), F32)] + sends


def fill(table, row):
    if table.shape[0] > row:
        table[row:, :] = jnp.zeros((table.shape[0] - row, table.shape[1]), F32)


def short_kernel(stage, cuts, *refs):
    ins, (x, go), (own, *sends), (a_gate, a_up, b_down, table, sems) = (
        refs[:5], refs[5:7], refs[7:-5], refs[-5:]
    )
    wait = fetch(ins, (x, go, a_gate, a_up, b_down), sems, cuts)
    for which in range(5):
        wait(which)
    tokens = x.shape[0]
    table[:tokens, :] = dot(x[...], a_gate[...], ((1,), (0,)))
    table[tokens : 2 * tokens, :] = dot(x[...], a_up[...], ((1,), (0,)))
    table[2 * tokens : 3 * tokens, :] = dot(go[...], b_down[...], ((1,), (0,)))
    fill(table, 3 * tokens)
    hand_out(table, stage, own, sends)


def short_products(rows, stage, *ins):
    rank = ins[2].shape[1]
    cuts = (2, 2, 1, 1, 1)
    shapes = [jax.ShapeDtypeStruct(a.shape, a.dtype) for a in ins[:2]]
    shapes = shapes + handed_out(rows, rank, stage)
    x, go, *sends = pl.pallas_call(
        functools.partial(short_kernel, stage, cuts),
        out_shape=shapes,
        in_specs=[ANY] * len(ins),
        out_specs=[VMEM] * len(shapes),
        scratch_shapes=[pltpu.VMEM(a.shape, a.dtype) for a in ins[2:]]
        + [pltpu.VMEM((rows, rank), F32), pltpu.SemaphoreType.DMA((sum(cuts),))],
        compiler_params=limit(4),
        cost_estimate=pl.CostEstimate(flops=10**8, bytes_accessed=6 * 10**6, transcendentals=0),
        name="short",
    )(*ins)
    return x, go, sends


def long_kernel(stage, cut, *refs):
    ins, held, (own, *sends), (*adapters, table, sems) = refs[:6], refs[6:9], refs[9:-5], refs[-5:]
    rank = table.shape[1]
    per = cut + 1
    waits = []

    def begin(slot):
        wait = fetch(
            (ins[3 + slot], ins[slot]),
            (adapters[slot], held[slot]),
            sems.at[slot * per : (slot + 1) * per],
            (1, cut),
        )
        waits.append(wait)

    begin(0)
    begin(1)
    row = 0
    for slot in range(3):
        waits[slot](0)
        adapter = adapters[slot][...].T
        waits[slot](1)
        if slot == 0:
            begin(2)
        value = dot(adapter, held[slot][...], ((1,), (0,)))
        for part in range(value.shape[1] // rank):
            table[row : row + rank, :] = value[:, part * rank : (part + 1) * rank]
            row += rank
    fill(table, row)
    hand_out(table, stage, own, sends)


def long_products(rows, stage, *ins):
    rank = ins[3].shape[1]
    cut = 4
    held = [jax.ShapeDtypeStruct(a.shape, a.dtype) for a in ins[:3]]
    shapes = held + handed_out(rows, rank, stage)
    outs = pl.pallas_call(
        functools.partial(long_kernel, stage, cut),
        out_shape=shapes,
        in_specs=[ANY] * 6,
        out_specs=[VMEM] * len(shapes),
        scratch_shapes=[pltpu.VMEM(a.shape, a.dtype) for a in ins[3:]]
        + [pltpu.VMEM((rows, rank), F32), pltpu.SemaphoreType.DMA((3 * (cut + 1),))],
        compiler_params=limit(6),
        cost_estimate=pl.CostEstimate(flops=10**9, bytes_accessed=8 * 10**6, transcendentals=0),
        name="long",
    )(*ins)
    return *outs[:3], outs[3:]


def add_kernel(following, count, *refs):
    total = refs[0][...]
    for got in refs[1 : 1 + count]:
        total = total + got[...].astype(F32)
    if following is None:
        refs[1 + count][...] = total.astype(BF16)
    else:
        outs, table = refs[1 + count : -1], refs[-1]
        table[...] = total
        hand_out(table, following, outs[0], outs[1:])


def add_up(own, got, following):
    if following is None:
        shapes, scratch = [jax.ShapeDtypeStruct(own.shape, BF16)], []
    else:
        shapes, scratch = handed_out(*own.shape, following), [pltpu.VMEM(own.shape, F32)]
    return pl.pallas_call(
        functools.partial(add_kernel, following, len(got)),
        out_shape=shapes,
        in_specs=[VMEM] * (1 + len(got)),
        out_specs=[VMEM] * len(shapes),
        scratch_shapes=scratch,
        compiler_params=limit(3),
        name="add_up",
    )(own, *got)


def join_kernel(stage, own, *refs):
    put_together(own, refs[:-1], stage, refs[-1])


def join(own, got, stage):
    return pl.pallas_call(
        functools.partial(join_kernel, stage),
        out_shape=jax.ShapeDtypeStruct((own.shape[0] * stage[1], own.shape[1]), BF16),
        in_specs=[VMEM] * (1 + len(got)),
        out_specs=VMEM,
        compiler_params=limit(3),
        name="join",
    )(own, *got)


def swap(sends, stage):
    return [
        exchange(sends[step - 1], "coord", step << stage[0]) for step in range(1, stage[1])
    ]


def after(first, second):
    return lax.optimization_barrier((first, second))[1]


def all_sums(halves, stages):
    owns = [half[0] for half in halves]
    sends = [half[1:] for half in halves]
    for stage, following in zip(stages, stages[1:] + [None], strict=True):
        got = [swap(send, stage) for send in sends]
        for i in range(len(owns)):
            own = after(owns[0], owns[i]) if i else owns[i]
            owns[i], *sends[i] = add_up(own, got[i][::-1], following)
    for stage in stages[:0:-1]:
        got = [swap([own] * (stage[1] - 1), stage) for own in owns]
        for i in range(len(owns)):
            own = after(owns[0], owns[i]) if i else owns[i]
            owns[i] = join(own, got[i], stage)
    return [[own] + swap([own] * (stages[0][1] - 1), stages[0]) for own in owns]


def total_over(contrib, count):
    assert lax.axis_size("ckpt") == 2
    core = lax.axis_index("ckpt")
    total = contrib + exchange(contrib, "ckpt", 1)
    shift = 0
    while 1 << shift < count:
        radix = min(8, count >> shift)
        half = radix // 2
        terms = []
        for step in range(half - 1, -1, -1):
            nearer, further = (step or half) << shift, (half + step) << shift
            pairs = [(2 * c + 1, 2 * (c ^ nearer)) for c in range(count)]
            pairs += [(2 * c, 2 * (c ^ further) + 1) for c in range(count)]
            got = lax.ppermute(total, ("coord", "ckpt"), pairs)
            terms.append(got if step else jnp.where(core == 0, total, got))
        while len(terms) > 1:
            terms = [a + b for a, b in zip(terms[::2], terms[1::2], strict=True)]
        total = terms[0] + exchange(terms[0], "ckpt", 1)
        shift += radix.bit_length() - 1
    return total


def turn_kernel(x, go, x_t, go_t):
    x_t[...] = x[...].T
    go_t[...] = go[...].T


def turn(x, go):
    shape = jax.ShapeDtypeStruct(x.shape[::-1], BF16)
    return pl.pallas_call(
        turn_kernel,
        out_shape=[shape, shape],
        in_specs=[VMEM, VMEM],
        out_specs=[VMEM, VMEM],
        compiler_params=limit(4),
        name="turn",
    )(x, go)


def butterflies(blocks):
    half = 1
    while half < len(blocks):
        done = list(blocks)
        for low in range(len(blocks)):
            if not low & half:
                a, b = blocks[low], blocks[low | half]
                if b is None:
                    done[low], done[low | half] = a, a
                else:
                    done[low], done[low | half] = a + b, a - b
        blocks, half = done, half * 2
    return blocks


def along_block(value, out, row):
    size = value.shape[0]
    tiles = butterflies([value[i : i + 8, :] for i in range(0, size, 8)])
    for i, tile in enumerate(tiles):
        out[row + 8 * i : row + 8 * i + 8, :] = tile
    for begin in range(row, row + size, 64):
        tiles = butterflies([out[pl.ds(begin + j, 8, stride=8), :] for j in range(8)])
        for j, tile in enumerate(tiles):
            out[begin + 8 * j : begin + 8 * j + 8, :] = tile


def signed(value, flags, row):
    return jnp.where(flags[row : row + value.shape[0], :] == 0, value, -value)


def keep(aligned, value, flags, row, out):
    value = signed(value, flags, row)
    if aligned:
        along_block(value, out, row)
    else:
        out[row : row + value.shape[0], :] = value


def wide_kernel(aligned, block, first, stage, *refs):
    parts, refs = refs[: stage[1]], refs[stage[1] :]
    gg, gu, h, flags, out, table = refs
    put_together(parts[0], parts[1:], stage, table)
    tokens = gg.shape[1]
    flags = flags.at[first : first + out.shape[0]]
    row = 0
    for slot, piece in enumerate((gg, gu, h)):
        product = table[slot * tokens : (slot + 1) * tokens, :]
        size = block if aligned else piece.shape[0]
        for begin in range(0, piece.shape[0], size):
            value = dot(piece[begin : begin + size, :], product, ((1,), (0,)))
            keep(aligned, value, flags, row, out)
            row += size


def wide(aligned, block, first, stage, parts, gg, gu, h, flags):
    rank = flags.shape[1]
    return pl.pallas_call(
        functools.partial(wide_kernel, aligned, block, first, stage),
        out_shape=jax.ShapeDtypeStruct((3 * gg.shape[0], rank), F32),
        in_specs=[VMEM] * (len(parts) + 4),
        out_specs=VMEM,
        scratch_shapes=[pltpu.VMEM((parts[0].shape[0] * stage[1], rank), BF16)],
        compiler_params=limit(6),
        cost_estimate=pl.CostEstimate(flops=10**9, bytes_accessed=10**7, transcendentals=0),
        name="wide",
    )(*parts, gg, gu, h, flags)


def rows_kernel(aligned, block, stage, *refs):
    parts, refs = refs[: stage[1]], refs[stage[1] :]
    x_t, go_t, wide_mix, flags, mix, table = refs
    width, tokens = x_t.shape
    first = 3 * width
    length, rank = mix.shape
    put_together(parts[0], parts[1:], stage, table)
    product = [
        jnp.concatenate(
            [table[slot * tokens + part : slot * tokens + part + rank, :] for part in range(0, tokens, rank)],
            axis=1,
        )
        for slot in range(3)
    ]
    size = block if aligned else width
    both = jnp.concatenate(product[:2], axis=0)
    for begin in range(0, width, size):
        value = dot(x_t[begin : begin + size, :], both, ((1,), (1,)))
        keep(aligned, value[:, :rank], flags, begin, mix)
        keep(aligned, value[:, rank:], flags, width + begin, mix)
        value = dot(go_t[begin : begin + size, :], product[2], ((1,), (1,)))
        keep(aligned, value, flags, 2 * width + begin, mix)
    filled = first + wide_mix.shape[0]
    if not aligned:
        mix[first:filled, :] = wide_mix[...]
        mix[filled:, :] = jnp.zeros((length - filled, rank), F32)
        for begin in range(0, length, block):
            along_block(mix[begin : begin + block, :], mix, begin)
    number = length // block
    full = -(-filled // block)

    def load(i, begin):
        if not aligned or i * block < first:
            return mix[pl.ds(i * block + begin, 8), :]
        if i >= full:
            return None
        return wide_mix[pl.ds(i * block - first + begin, 8), :]

    for begin in range(0, block, 8):
        for i, value in enumerate(butterflies([load(i, begin) for i in range(number)])):
            mix[i * block + begin : i * block + begin + 8, :] = value


def along_rows(aligned, block, stage, length, parts, x_t, go_t, wide_mix, flags):
    rank = flags.shape[1]
    return pl.pallas_call(
        functools.partial(rows_kernel, aligned, block, stage),
        out_shape=jax.ShapeDtypeStruct((length, rank), F32),
        in_specs=[VMEM] * (len(parts) + 4),
        out_specs=VMEM,
        scratch_shapes=[pltpu.VMEM((parts[0].shape[0] * stage[1], rank), BF16)],
        compiler_params=limit(6),
        name="along_rows",
    )(*parts, x_t, go_t, wide_mix, flags)


def parity(value):
    for fold in (16, 8, 4, 2, 1):
        value = value ^ (value >> fold)
    return value & 1


def signs_kernel(bits, lanes, out):
    rank = out.shape[0]
    device = lax.axis_index("coord") * lax.axis_size("ckpt") + lax.axis_index("ckpt")
    index = lanes[...]

    def sign(bit):
        return (1 - 2 * (bit & 1)).astype(F32)

    low = lax.broadcasted_iota(jnp.int32, (8, index.shape[1]), 0)
    tile = sign(parity((index >> bits) & device))
    for bit in range(3):
        tile = tile * jnp.where((low >> bit & 1) == 0, 1.0, sign(index >> bit))
    tiles = [tile]
    for bit in range(3, rank.bit_length() - 1):
        tiles = tiles + [tile * sign(index >> bit) for tile in tiles]
    out[...] = jnp.concatenate(tiles, axis=0).astype(BF16)


def signs_of(rank, bits, index):
    samples = index.shape[0]
    return pl.pallas_call(
        functools.partial(signs_kernel, bits),
        out_shape=jax.ShapeDtypeStruct((rank, samples), BF16),
        in_specs=[VMEM],
        out_specs=VMEM,
        compiler_params=limit(10),
        name="signs",
    )(index.reshape(1, samples))


def pick_kernel(mix, where, rows):
    samples, rank = rows.shape
    group = min(128, samples)
    unroll = min(2, samples // group)
    place = lax.broadcasted_iota(jnp.int32, (8, rank), 0)
    masks = [place == i for i in range(8)]

    def picked_tile(sources, begin):
        tile = None
        for i in range(8):
            row = jnp.broadcast_to(mix[pl.ds(sources[begin + i], 1), :], (8, rank))
            tile = row if tile is None else jnp.where(masks[i], row, tile)
        return tile

    def pick(step, _):
        for part in range(unroll):
            span = pl.ds(pl.multiple_of((step * unroll + part) * group, group), group)
            sources, targets = where.at[span], rows.at[span]
            tiles = [picked_tile(sources, begin) for begin in range(0, group, 8)]
            for i, tile in enumerate(tiles):
                targets[8 * i : 8 * i + 8, :] = tile
        return _

    lax.fori_loop(0, samples // (group * unroll), pick, 0)


def picked(mix, where):
    return pl.pallas_call(
        pick_kernel,
        out_shape=jax.ShapeDtypeStruct((where.shape[0], mix.shape[1]), F32),
        in_specs=[VMEM, SMEM],
        out_specs=VMEM,
        compiler_params=limit(4),
        name="picked",
    )(mix, where)


def sample_kernel(final_scale, rows, signs, out):
    samples, rank = rows.shape
    shape = (rank, rank)
    diagonal = lax.broadcasted_iota(jnp.int32, shape, 0) == lax.broadcasted_iota(jnp.int32, shape, 1)
    for begin in range(0, samples, rank):
        value = rows[begin : begin + rank, :]
        high = value.astype(BF16)
        low = (value - high.astype(F32)).astype(BF16)
        sign = signs[:, begin : begin + rank]
        mixed = dot(
            jnp.concatenate([high, low], axis=1), jnp.concatenate([sign, sign], axis=0), ((1,), (0,))
        )
        chosen = jnp.sum(jnp.where(diagonal, mixed, 0.0), axis=0, keepdims=True)
        out[:, begin : begin + rank] = chosen * final_scale


def sampled(final_scale, rows, signs):
    return pl.pallas_call(
        functools.partial(sample_kernel, final_scale),
        out_shape=jax.ShapeDtypeStruct((1, rows.shape[0]), F32),
        in_specs=[VMEM, VMEM],
        out_specs=VMEM,
        compiler_params=limit(4),
        name="sampled",
    )(rows, signs)


def shards(x, gg, gu, h, go, a_gate, b_gate, a_up, b_up, a_down, b_down, flags, index):
    x, go, gg, gu, h = [a[0, 0] for a in (x, go, gg, gu, h)]
    a_gate, b_gate, a_up, b_up, a_down, b_down = [
        a[0] for a in (a_gate, b_gate, a_up, b_up, a_down, b_down)
    ]
    count = lax.axis_size("coord")
    tokens, rank = x.shape[0], a_gate.shape[1]
    total = flags.shape[0] * count * lax.axis_size("ckpt")
    flags = flags.reshape(-1, rank)
    length = flags.shape[0]
    first = 3 * x.shape[1]
    block = min(256, length)
    aligned = x.shape[1] % block == 0 and gg.shape[0] % block == 0
    where = (index >> (rank.bit_length() - 1)) & (length - 1)
    where = (where & ~63) | (where & 7) << 3 | where >> 3 & 7
    stages = stages_of(count)
    rows = 16 * count * -(-3 * tokens // (16 * count))
    x, go, short = short_products(
        rows, stages[0], *[in_hbm(a) for a in (x, go, a_gate, a_up, b_down)]
    )
    gg, gu, h, long = long_products(
        rows, stages[0], *[in_hbm(a) for a in (gg, gu, h, b_gate, b_up, a_down)]
    )
    flags = after(long[0], flags)
    bits = (length * rank).bit_length() - 1
    short, long = all_sums([short, long], stages)
    x_t, go_t = turn(after(long[0], x), go)
    signs = signs_of(rank, bits, after(long[0], index))
    wide_mix = wide(aligned, block, first, stages[0], short, gg, gu, h, flags)
    final_scale = adapter_scale * float(total) ** -0.5
    mix = along_rows(aligned, block, stages[0], length, long, x_t, go_t, wide_mix, flags)
    contrib = sampled(final_scale, picked(mix, where), signs)
    return total_over(contrib, count)


def solution(mesh):
    in_specs = (
        P("ckpt", "groups", None, "coord"),
        P("ckpt", "groups", "coord", None),
        P("ckpt", "groups", "coord", None),
        P("ckpt", "groups", "coord", None),
        P("ckpt", "groups", None, "coord"),
        P("ckpt", "coord", None),
        P("ckpt", "coord", None),
        P("ckpt", "coord", None),
        P("ckpt", "coord", None),
        P("ckpt", "coord", None),
        P("ckpt", "coord", None),
        P(("coord", "ckpt")),
        P(),
    )
    out_specs = P("groups", None)
    return jax.shard_map(shards, mesh=mesh, in_specs=in_specs, out_specs=out_specs, check_vma=False)
```

```python
import functools

import jax
import jax.numpy as jnp
from jax import lax
from jax.experimental import pallas as pl
from jax.experimental.pallas import tpu as pltpu
from jax.sharding import PartitionSpec as P

F32 = jnp.float32
BF16 = jnp.bfloat16
MIB = 2**20
adapter_scale = 2.0

ANY = pl.BlockSpec(memory_space=pl.ANY)
VMEM = pl.BlockSpec(memory_space=pltpu.VMEM)
SMEM = pl.BlockSpec(memory_space=pltpu.SMEM)


def limit(size):
    return pltpu.CompilerParams(vmem_limit_bytes=int(size * MIB))


def in_hbm(value):
    return pltpu.with_memory_space_constraint(value, pltpu.HBM)


def exchange(value, axis, apart):
    pairs = [(source, source ^ apart) for source in range(lax.axis_size(axis))]
    return lax.ppermute(value, axis, pairs)


def dot(left, right, contract):
    return lax.dot_general(left, right, (contract, ((), ())), preferred_element_type=F32)


def fetch(sources, targets, sems, cuts):
    groups = []
    slot = 0
    for source, target, cut in zip(sources, targets, cuts, strict=True):
        rows = source.shape[0]
        size = -(-rows // (cut * 16)) * 16
        group = []
        for begin in range(0, rows, size):
            end = min(begin + size, rows)
            copy = pltpu.make_async_copy(
                source.at[begin:end], target.at[begin:end], sems.at[slot]
            )
            copy.start()
            group.append(copy)
            slot += 1
        groups.append(group)

    def wait(which):
        for copy in groups[which]:
            copy.wait()

    return wait


def stages_of(count):
    stages, shift = [], 0
    while count > 1:
        radix = 2 if shift == 0 else min(4, count)
        stages.append((shift, radix))
        shift += radix.bit_length() - 1
        count //= radix
    return stages


def my_digit(stage):
    return (lax.axis_index("coord") >> stage[0]) & (stage[1] - 1)


def hand_out(table, stage, own, sends):
    digit = my_digit(stage)
    size = own.shape[0]
    own[...] = table[pl.ds(pl.multiple_of(digit * size, 16), size), :]
    for step, send in enumerate(sends, 1):
        begin = pl.multiple_of((digit ^ step) * size, 16)
        send[...] = table[pl.ds(begin, size), :].astype(BF16)


def put_together(own, others, stage, table):
    digit = my_digit(stage)
    size = own.shape[0]
    table[pl.ds(pl.multiple_of(digit * size, 16), size), :] = own[...]
    for step, other in enumerate(others[::-1], 1):
        table[pl.ds(pl.multiple_of((digit ^ step) * size, 16), size), :] = other[...]


def handed_out(rows, rank, stage):
    size = rows // stage[1]
    sends = [jax.ShapeDtypeStruct((size, rank), BF16)] * (stage[1] - 1)
    return [jax.ShapeDtypeStruct((size, rank), F32)] + sends


def fill(table, row):
    if table.shape[0] > row:
        table[row:, :] = jnp.zeros((table.shape[0] - row, table.shape[1]), F32)


def short_kernel(stage, cuts, *refs):
    ins, (x, go), (own, *sends), (a_gate, a_up, b_down, table, sems) = (
        refs[:5], refs[5:7], refs[7:-5], refs[-5:]
    )
    wait = fetch(ins, (x, go, a_gate, a_up, b_down), sems, cuts)
    for which in range(5):
        wait(which)
    tokens = x.shape[0]
    table[:tokens, :] = dot(x[...], a_gate[...], ((1,), (0,)))
    table[tokens : 2 * tokens, :] = dot(x[...], a_up[...], ((1,), (0,)))
    table[2 * tokens : 3 * tokens, :] = dot(go[...], b_down[...], ((1,), (0,)))
    fill(table, 3 * tokens)
    hand_out(table, stage, own, sends)


def short_products(rows, stage, *ins):
    rank = ins[2].shape[1]
    cuts = (2, 2, 1, 1, 1)
    shapes = [jax.ShapeDtypeStruct(a.shape, a.dtype) for a in ins[:2]]
    shapes = shapes + handed_out(rows, rank, stage)
    x, go, *sends = pl.pallas_call(
        functools.partial(short_kernel, stage, cuts),
        out_shape=shapes,
        in_specs=[ANY] * len(ins),
        out_specs=[VMEM] * len(shapes),
        scratch_shapes=[pltpu.VMEM(a.shape, a.dtype) for a in ins[2:]]
        + [pltpu.VMEM((rows, rank), F32), pltpu.SemaphoreType.DMA((sum(cuts),))],
        compiler_params=limit(4),
        cost_estimate=pl.CostEstimate(flops=10**8, bytes_accessed=6 * 10**6, transcendentals=0),
        name="short",
    )(*ins)
    return x, go, sends


def long_kernel(stage, cut, *refs):
    ins, held, (own, *sends), (*adapters, table, sems) = refs[:6], refs[6:9], refs[9:-5], refs[-5:]
    rank = table.shape[1]
    per = cut + 1
    waits = []

    def begin(slot):
        wait = fetch(
            (ins[3 + slot], ins[slot]),
            (adapters[slot], held[slot]),
            sems.at[slot * per : (slot + 1) * per],
            (1, cut),
        )
        waits.append(wait)

    for slot in range(3):
        begin(slot)
    row = 0
    for slot in range(3):
        waits[slot](0)
        adapter = adapters[slot][...].T
        waits[slot](1)
        value = dot(adapter, held[slot][...], ((1,), (0,)))
        for part in range(value.shape[1] // rank):
            table[row : row + rank, :] = value[:, part * rank : (part + 1) * rank]
            row += rank
    fill(table, row)
    hand_out(table, stage, own, sends)


def long_products(rows, stage, *ins):
    rank = ins[3].shape[1]
    cut = 4
    held = [jax.ShapeDtypeStruct(a.shape, a.dtype) for a in ins[:3]]
    shapes = held + handed_out(rows, rank, stage)
    outs = pl.pallas_call(
        functools.partial(long_kernel, stage, cut),
        out_shape=shapes,
        in_specs=[ANY] * 6,
        out_specs=[VMEM] * len(shapes),
        scratch_shapes=[pltpu.VMEM(a.shape, a.dtype) for a in ins[3:]]
        + [pltpu.VMEM((rows, rank), F32), pltpu.SemaphoreType.DMA((3 * (cut + 1),))],
        compiler_params=limit(6),
        cost_estimate=pl.CostEstimate(flops=10**9, bytes_accessed=8 * 10**6, transcendentals=0),
        name="long",
    )(*ins)
    return *outs[:3], outs[3:]


def add_kernel(following, count, *refs):
    total = refs[0][...]
    for got in refs[1 : 1 + count]:
        total = total + got[...].astype(F32)
    if following is None:
        refs[1 + count][...] = total.astype(BF16)
    else:
        outs, table = refs[1 + count : -1], refs[-1]
        table[...] = total
        hand_out(table, following, outs[0], outs[1:])


def add_up(own, got, following):
    if following is None:
        shapes, scratch = [jax.ShapeDtypeStruct(own.shape, BF16)], []
    else:
        shapes, scratch = handed_out(*own.shape, following), [pltpu.VMEM(own.shape, F32)]
    return pl.pallas_call(
        functools.partial(add_kernel, following, len(got)),
        out_shape=shapes,
        in_specs=[VMEM] * (1 + len(got)),
        out_specs=[VMEM] * len(shapes),
        scratch_shapes=scratch,
        compiler_params=limit(3),
        name="add_up",
    )(own, *got)


def join_kernel(stage, own, *refs):
    put_together(own, refs[:-1], stage, refs[-1])


def join(own, got, stage):
    return pl.pallas_call(
        functools.partial(join_kernel, stage),
        out_shape=jax.ShapeDtypeStruct((own.shape[0] * stage[1], own.shape[1]), BF16),
        in_specs=[VMEM] * (1 + len(got)),
        out_specs=VMEM,
        compiler_params=limit(3),
        name="join",
    )(own, *got)


def swap(sends, stage):
    return [
        exchange(sends[step - 1], "coord", step << stage[0]) for step in range(stage[1] - 1, 0, -1)
    ]


def after(first, second):
    return lax.optimization_barrier((first, second))[1]


def all_sums(halves, stages, ahead):
    beside = []
    owns = [half[0] for half in halves]
    sends = [half[1:] for half in halves]
    for stage, following in zip(stages, stages[1:] + [None], strict=True):
        got = [swap(send, stage) for send in sends]
        for i in range(len(owns)):
            own = after(owns[0], owns[i]) if i else owns[i]
            order = got[i][1:] + got[i][:1] if i else got[i]
            owns[i], *sends[i] = add_up(own, order, following)
    for stage in stages[:0:-1]:
        got = [swap([own] * (stage[1] - 1), stage) for own in owns]
        for i in range(len(owns)):
            own = after(owns[0], owns[i]) if i else owns[i]
            if stage is stages[1]:
                beside.append(ahead[i](owns[0]))
                own = after(beside[i], own)
            owns[i] = join(own, got[i], stage)
    return beside, [[own] + swap([own] * (stages[0][1] - 1), stages[0]) for own in owns]


def total_over(contrib, count):
    assert lax.axis_size("ckpt") == 2
    core = lax.axis_index("ckpt")
    total = contrib + exchange(contrib, "ckpt", 1)
    shift = 0
    while 1 << shift < count:
        radix = min(8, count >> shift)
        half = radix // 2
        terms = []
        for step in range(half):
            nearer, further = (step or half) << shift, (half + step) << shift
            pairs = [(2 * c + 1, 2 * (c ^ nearer)) for c in range(count)]
            pairs += [(2 * c, 2 * (c ^ further) + 1) for c in range(count)]
            got = lax.ppermute(total, ("coord", "ckpt"), pairs)
            terms.append(got if step else jnp.where(core == 0, total, got))
        while len(terms) > 1:
            terms = [a + b for a, b in zip(terms[::2], terms[1::2], strict=True)]
        total = terms[0] + exchange(terms[0], "ckpt", 1)
        shift += radix.bit_length() - 1
    return total


def turn_kernel(x, go, x_t, go_t):
    x_t[...] = x[...].T
    go_t[...] = go[...].T


def turn(x, go):
    shape = jax.ShapeDtypeStruct(x.shape[::-1], BF16)
    return pl.pallas_call(
        turn_kernel,
        out_shape=[shape, shape],
        in_specs=[VMEM, VMEM],
        out_specs=[VMEM, VMEM],
        compiler_params=limit(4),
        name="turn",
    )(x, go)


def butterflies(blocks):
    half = 1
    while half < len(blocks):
        done = list(blocks)
        for low in range(len(blocks)):
            if not low & half:
                a, b = blocks[low], blocks[low | half]
                if b is None:
                    done[low], done[low | half] = a, a
                else:
                    done[low], done[low | half] = a + b, a - b
        blocks, half = done, half * 2
    return blocks


def along_block(value, out, row):
    size = value.shape[0]
    tiles = butterflies([value[i : i + 8, :] for i in range(0, size, 8)])
    for i, tile in enumerate(tiles):
        out[row + 8 * i : row + 8 * i + 8, :] = tile
    for begin in range(row, row + size, 64):
        tiles = butterflies([out[pl.ds(begin + j, 8, stride=8), :] for j in range(8)])
        for j, tile in enumerate(tiles):
            out[begin + 8 * j : begin + 8 * j + 8, :] = tile


def signed(value, flags, row):
    return jnp.where(flags[row : row + value.shape[0], :] == 0, value, -value)


def keep(aligned, value, flags, row, out):
    value = signed(value, flags, row)
    if aligned:
        along_block(value, out, row)
    else:
        out[row : row + value.shape[0], :] = value


def wide_kernel(aligned, block, first, stage, *refs):
    parts, refs = refs[: stage[1]], refs[stage[1] :]
    gg, gu, h, flags, out, table = refs
    put_together(parts[0], parts[1:], stage, table)
    tokens = gg.shape[1]
    flags = flags.at[first : first + out.shape[0]]
    row = 0
    for slot, piece in enumerate((gg, gu, h)):
        product = table[slot * tokens : (slot + 1) * tokens, :]
        size = block if aligned else piece.shape[0]
        for begin in range(0, piece.shape[0], size):
            value = dot(piece[begin : begin + size, :], product, ((1,), (0,)))
            keep(aligned, value, flags, row, out)
            row += size


def wide(aligned, block, first, stage, parts, gg, gu, h, flags):
    rank = flags.shape[1]
    return pl.pallas_call(
        functools.partial(wide_kernel, aligned, block, first, stage),
        out_shape=jax.ShapeDtypeStruct((3 * gg.shape[0], rank), F32),
        in_specs=[VMEM] * (len(parts) + 4),
        out_specs=VMEM,
        scratch_shapes=[pltpu.VMEM((parts[0].shape[0] * stage[1], rank), BF16)],
        compiler_params=limit(6),
        cost_estimate=pl.CostEstimate(flops=10**9, bytes_accessed=10**7, transcendentals=0),
        name="wide",
    )(*parts, gg, gu, h, flags)


def rows_kernel(aligned, block, stage, *refs):
    parts, refs = refs[: stage[1]], refs[stage[1] :]
    x_t, go_t, wide_mix, flags, mix, table = refs
    width, tokens = x_t.shape
    first = 3 * width
    length, rank = mix.shape
    put_together(parts[0], parts[1:], stage, table)
    product = [
        jnp.concatenate(
            [table[slot * tokens + part : slot * tokens + part + rank, :] for part in range(0, tokens, rank)],
            axis=1,
        )
        for slot in range(3)
    ]
    size = block if aligned else width
    both = jnp.concatenate(product[:2], axis=0)
    for begin in range(0, width, size):
        value = dot(x_t[begin : begin + size, :], both, ((1,), (1,)))
        keep(aligned, value[:, :rank], flags, begin, mix)
        keep(aligned, value[:, rank:], flags, width + begin, mix)
        value = dot(go_t[begin : begin + size, :], product[2], ((1,), (1,)))
        keep(aligned, value, flags, 2 * width + begin, mix)
    filled = first + wide_mix.shape[0]
    if not aligned:
        mix[first:filled, :] = wide_mix[...]
        mix[filled:, :] = jnp.zeros((length - filled, rank), F32)
        for begin in range(0, length, block):
            along_block(mix[begin : begin + block, :], mix, begin)
    number = length // block
    full = -(-filled // block)

    def load(i, begin):
        if not aligned or i * block < first:
            return mix[pl.ds(i * block + begin, 8), :]
        if i >= full:
            return None
        return wide_mix[pl.ds(i * block - first + begin, 8), :]

    for begin in range(0, block, 8):
        for i, value in enumerate(butterflies([load(i, begin) for i in range(number)])):
            mix[i * block + begin : i * block + begin + 8, :] = value


def along_rows(aligned, block, stage, length, parts, x_t, go_t, wide_mix, flags):
    rank = flags.shape[1]
    return pl.pallas_call(
        functools.partial(rows_kernel, aligned, block, stage),
        out_shape=jax.ShapeDtypeStruct((length, rank), F32),
        in_specs=[VMEM] * (len(parts) + 4),
        out_specs=VMEM,
        scratch_shapes=[pltpu.VMEM((parts[0].shape[0] * stage[1], rank), BF16)],
        compiler_params=limit(6),
        name="along_rows",
    )(*parts, x_t, go_t, wide_mix, flags)


def parity(value):
    for fold in (16, 8, 4, 2, 1):
        value = value ^ (value >> fold)
    return value & 1


def signs_kernel(bits, lanes, out):
    rank = out.shape[0]
    device = lax.axis_index("coord") * lax.axis_size("ckpt") + lax.axis_index("ckpt")
    index = lanes[...]

    def sign(bit):
        return (1 - 2 * (bit & 1)).astype(F32)

    low = lax.broadcasted_iota(jnp.int32, (8, index.shape[1]), 0)
    tile = sign(parity((index >> bits) & device))
    for bit in range(3):
        tile = tile * jnp.where((low >> bit & 1) == 0, 1.0, sign(index >> bit))
    tiles = [tile]
    for bit in range(3, rank.bit_length() - 1):
        tiles = tiles + [tile * sign(index >> bit) for tile in tiles]
    out[...] = jnp.concatenate(tiles, axis=0).astype(BF16)


def signs_of(rank, bits, index):
    samples = index.shape[0]
    return pl.pallas_call(
        functools.partial(signs_kernel, bits),
        out_shape=jax.ShapeDtypeStruct((rank, samples), BF16),
        in_specs=[VMEM],
        out_specs=VMEM,
        compiler_params=limit(10),
        name="signs",
    )(index.reshape(1, samples))


def pick_kernel(mix, where, rows):
    samples, rank = rows.shape
    group = min(128, samples)
    unroll = min(2, samples // group)
    place = lax.broadcasted_iota(jnp.int32, (8, rank), 0)
    masks = [place == i for i in range(8)]

    def picked_tile(sources, begin):
        tile = None
        for i in range(8):
            row = jnp.broadcast_to(mix[pl.ds(sources[begin + i], 1), :], (8, rank))
            tile = row if tile is None else jnp.where(masks[i], row, tile)
        return tile

    def pick(step, _):
        for part in range(unroll):
            span = pl.ds(pl.multiple_of((step * unroll + part) * group, group), group)
            sources, targets = where.at[span], rows.at[span]
            tiles = [picked_tile(sources, begin) for begin in range(0, group, 8)]
            for i, tile in enumerate(tiles):
                targets[8 * i : 8 * i + 8, :] = tile
        return _

    lax.fori_loop(0, samples // (group * unroll), pick, 0)


def picked(mix, where):
    return pl.pallas_call(
        pick_kernel,
        out_shape=jax.ShapeDtypeStruct((where.shape[0], mix.shape[1]), F32),
        in_specs=[VMEM, SMEM],
        out_specs=VMEM,
        compiler_params=limit(4),
        name="picked",
    )(mix, where)


def sample_kernel(final_scale, rows, signs, out):
    samples, rank = rows.shape
    shape = (rank, rank)
    diagonal = lax.broadcasted_iota(jnp.int32, shape, 0) == lax.broadcasted_iota(jnp.int32, shape, 1)
    for begin in range(0, samples, rank):
        value = rows[begin : begin + rank, :]
        high = value.astype(BF16)
        low = (value - high.astype(F32)).astype(BF16)
        sign = signs[:, begin : begin + rank]
        mixed = dot(
            jnp.concatenate([high, low], axis=1), jnp.concatenate([sign, sign], axis=0), ((1,), (0,))
        )
        chosen = jnp.sum(jnp.where(diagonal, mixed, 0.0), axis=0, keepdims=True)
        out[:, begin : begin + rank] = chosen * final_scale


def sampled(final_scale, rows, signs):
    return pl.pallas_call(
        functools.partial(sample_kernel, final_scale),
        out_shape=jax.ShapeDtypeStruct((1, rows.shape[0]), F32),
        in_specs=[VMEM, VMEM],
        out_specs=VMEM,
        compiler_params=limit(4),
        name="sampled",
    )(rows, signs)


def shards(x, gg, gu, h, go, a_gate, b_gate, a_up, b_up, a_down, b_down, flags, index):
    x, go, gg, gu, h = [a[0, 0] for a in (x, go, gg, gu, h)]
    a_gate, b_gate, a_up, b_up, a_down, b_down = [
        a[0] for a in (a_gate, b_gate, a_up, b_up, a_down, b_down)
    ]
    count = lax.axis_size("coord")
    tokens, rank = x.shape[0], a_gate.shape[1]
    total = flags.shape[0] * count * lax.axis_size("ckpt")
    flags = flags.reshape(-1, rank)
    length = flags.shape[0]
    first = 3 * x.shape[1]
    block = min(256, length)
    aligned = x.shape[1] % block == 0 and gg.shape[0] % block == 0
    where = (index >> (rank.bit_length() - 1)) & (length - 1)
    where = (where & ~63) | (where & 7) << 3 | where >> 3 & 7
    stages = stages_of(count)
    rows = 16 * count * -(-3 * tokens // (16 * count))
    x, go, short = short_products(
        rows, stages[0], *[in_hbm(a) for a in (x, go, a_gate, a_up, b_down)]
    )
    gg, gu, h, long = long_products(
        rows, stages[0], *[in_hbm(a) for a in (gg, gu, h, b_gate, b_up, a_down)]
    )
    flags = after(long[0], flags)
    bits = (length * rank).bit_length() - 1
    ahead = (
        lambda ready: turn(x, go),
        lambda ready: signs_of(rank, bits, after(ready, index)),
    )
    ((x_t, go_t), signs), (short, long) = all_sums([short, long], stages, ahead)
    wide_mix = wide(aligned, block, first, stages[0], short, gg, gu, h, flags)
    final_scale = adapter_scale * float(total) ** -0.5
    mix = along_rows(aligned, block, stages[0], length, long, x_t, go_t, wide_mix, flags)
    contrib = sampled(final_scale, picked(mix, where), signs)
    return total_over(contrib, count)


def solution(mesh):
    in_specs = (
        P("ckpt", "groups", None, "coord"),
        P("ckpt", "groups", "coord", None),
        P("ckpt", "groups", "coord", None),
        P("ckpt", "groups", "coord", None),
        P("ckpt", "groups", None, "coord"),
        P("ckpt", "coord", None),
        P("ckpt", "coord", None),
        P("ckpt", "coord", None),
        P("ckpt", "coord", None),
        P("ckpt", "coord", None),
        P("ckpt", "coord", None),
        P(("coord", "ckpt")),
        P(),
    )
    out_specs = P("groups", None)
    return jax.shard_map(shards, mesh=mesh, in_specs=in_specs, out_specs=out_specs, check_vma=False)
```
